32 devices in a mesh: section: 4 (over z), dp: 2 (over x), fsdp: 4 (over y, core).
Axes of the slice: x: 2, y: 2, z: 4, core: 2. Of those that a mesh axis runs over, the one named last changes fastest.
Arguments:
- x_down: bfloat16 [4, 2, 512, 6144], P('section', 'dp', 'fsdp'), may hold values from -6 to 6
- x_up: bfloat16 [4, 2, 512, 6144], P('section', 'dp', 'fsdp'), may hold values from -6 to 6
- w_tiles: bfloat16 [4, 2, 20, 2, 128, 128], P('section', None, 'fsdp'), as said below
- tile_rows: int32 [4, 2, 20], P('section'), may hold values from 0 to 47, as said below
- tile_cols: int32 [4, 2, 20], P('section'), may hold values from 0 to 191, as said below
- counts: int32 [4, 2, 4], P('section'), may hold values from 2 to 5, as said below
Outputs:
- tile_grads: bfloat16 [4, 20, 2, 128, 128], P('section', 'fsdp')
The draws below stay inside these ranges and needn't reach their ends.
Inputs may be any that keep to these rules, and one draw needn't show every extreme that they name: w_tiles[l, 1] equals w_tiles[(l + 2) mod 4, 0]. tile_rows[l, 1] equals tile_rows[(l + 2) mod 4, 0]; the 20 row blocks of one layer are distinct. tile_cols[l, 1] equals tile_cols[(l + 2) mod 4, 0]; every column block that a layer uses is used by exactly two of its slots. counts[l, 1] equals counts[(l + 2) mod 4, 0]; the counts of one layer are the numbers 5 - i * 5 // 4 for i < 4 in some order.
All inputs are finite; a program needn't handle non-finite values.
Results may differ from the reference program's by a relative error of at most 0.0065.
Values may be sent and summed in bfloat16 or wider, within the bound.
No kernel may reach another device: no remote copies, remote signals or barrier semaphores. Data moves between devices by JAX's collectives and lax.ppermute only.
A program may use at most 64 MiB of HBM per device.

```python
import math
import jax
import jax.numpy as jnp
from jax import lax

D = 6144
FF = 24576
TILE = 128
CAP = 5
ROWS = 128
SECTIONS = 4
REPLICAS = 2
OWNERS = 4
SLOTS = 20
TOKROWS = 512
TOTAL = 2048


def tile_pattern(key):

    def one_layer(layer_key):
        key_rows, key_cols, key_counts, key_pairs = jax.random.split(layer_key, 4)
        row_ids = jax.random.permutation(key_rows, D // TILE)[:SLOTS].astype(jnp.int32)
        half_cols = jax.random.permutation(key_cols, FF // TILE)[:SLOTS // 2].astype(jnp.int32)
        doubled = jnp.concatenate([half_cols, half_cols])
        placing = jax.random.permutation(key_pairs, SLOTS).astype(jnp.int32)
        col_ids = jnp.zeros((SLOTS,), jnp.int32).at[placing].set(doubled)
        order = jax.random.permutation(key_counts, OWNERS).astype(jnp.int32)
        owner_counts = CAP - order * CAP // OWNERS
        return (row_ids, col_ids, owner_counts)
    layer_keys = jax.random.split(jax.random.fold_in(key, 11), SECTIONS)
    row_ids, col_ids, owner_counts = jax.vmap(one_layer)(layer_keys)

    def paired(values):
        return jnp.stack([values, jnp.roll(values, SECTIONS // 2, axis=0)], axis=1).astype(jnp.int32)
    return (paired(row_ids), paired(col_ids), paired(owner_counts))


def draw_tile_rows(key, part):
    return tile_pattern(key)[0]


def draw_tile_cols(key, part):
    return tile_pattern(key)[1]


def draw_counts(key, part):
    return tile_pattern(key)[2]


def draw_w_tiles(key, part):
    shape = (SECTIONS, SLOTS, 2, TILE, TILE)
    base = jax.random.normal(jax.random.fold_in(key, 5), shape, jnp.float32)
    base = base * TILE ** (-0.5)
    return jnp.stack([base, jnp.roll(base, SECTIONS // 2, axis=0)], axis=1).astype(jnp.bfloat16)


def level_of(own_key, shape, cuts, least, high):
    gain = 1.0
    for axis_at, blocks in cuts:
        heights = jax.random.uniform(jax.random.fold_in(jax.random.fold_in(own_key, 6), axis_at), (blocks,), jnp.float32, least / len(cuts), high / len(cuts))
        gain = gain * jnp.repeat(jnp.exp(heights), shape[axis_at] // blocks).reshape((-1,) + (1,) * (len(shape) - 1 - axis_at))
    return gain


def centred(stream_key, shape, scale, bound, cuts=(), held_as=jnp.bfloat16):
    result = jax.random.normal(stream_key, shape, jnp.float32) * scale
    if len(cuts) > 0:
        result = level_of(stream_key, shape, cuts, -0.22, 0.18) * result
    return jnp.clip(result, min=-bound, max=bound).astype(held_as)


def setup_inputs(seed: int = 0) -> dict:
    arg_keys = jax.random.split(jax.random.key(seed), 7)
    x_down = centred(arg_keys[0], (SECTIONS, REPLICAS, TOKROWS, D), 1.0, 6.0, ((0, 4), (1, 2), (2, 4)))
    x_up = centred(arg_keys[1], (SECTIONS, REPLICAS, TOKROWS, D), 1.0, 6.0, ((0, 4), (1, 2), (2, 4)))
    w_tiles = draw_w_tiles(jax.random.fold_in(arg_keys[6], 71), 0)
    tile_rows = draw_tile_rows(jax.random.fold_in(arg_keys[6], 71), 0)
    tile_cols = draw_tile_cols(jax.random.fold_in(arg_keys[6], 71), 0)
    counts = draw_counts(jax.random.fold_in(arg_keys[6], 71), 0)
    return {"x_down": x_down, "x_up": x_up, "w_tiles": w_tiles, "tile_rows": tile_rows, "tile_cols": tile_cols, "counts": counts}


tanh_scale = math.sqrt(2.0 / math.pi)
cubic_coef = 0.044715

def gelu_pair(hidden):
    inner = tanh_scale * (hidden + cubic_coef * hidden * hidden * hidden)
    tangent = jnp.tanh(inner)
    value = 0.5 * hidden * (1.0 + tangent)
    slope = 0.5 * (1.0 + tangent) + 0.5 * hidden * (1.0 - tangent * tangent) * tanh_scale * (1.0 + 3.0 * cubic_coef * hidden * hidden)
    return (value, slope)

def slot_masks(col_ids, counts_in):
    slots = col_ids.shape[0]
    owners = counts_in.shape[0]
    per_owner = slots // owners
    slot_ids = jnp.arange(slots, dtype=jnp.int32)
    owner_ids = slot_ids // per_owner
    per_slot = lax.optimization_barrier(jnp.sum(jnp.where(owner_ids[:, None] == jnp.arange(owners, dtype=jnp.int32)[None, :], counts_in[None, :], 0), axis=1))
    living = slot_ids % per_owner < per_slot
    shared = (col_ids[:, None] == col_ids[None, :]) & living[:, None] & living[None, :]
    return shared.astype(jnp.float32)

def device_term(inputs, weights, row_ids, shared, loss_scale):
    high = lax.Precision.HIGHEST
    blocks = inputs.reshape(inputs.shape[0], -1, TILE)[:, row_ids]
    wide = blocks.astype(jnp.float32)
    first_w = weights[:, 0].astype(jnp.float32)
    second_w = weights[:, 1].astype(jnp.float32)
    contrib = jnp.einsum('nsu,suv->nsv', wide, first_w, precision=high)
    hidden = jnp.einsum('st,ntv->nsv', shared, contrib, precision=high)
    value, slope = gelu_pair(hidden)
    active = lax.optimization_barrier(value.astype(jnp.bfloat16)).astype(jnp.float32)
    delta = jnp.einsum('nsu,suv->nsv', active, second_w, precision=high)
    cotangent = lax.optimization_barrier((loss_scale * (wide + delta)).astype(jnp.bfloat16)).astype(jnp.float32)
    spread = jnp.einsum('nsv,suv->nsu', cotangent, second_w, precision=high)
    grad_act = jnp.einsum('st,ntu->nsu', shared, spread, precision=high)
    grad_pre = lax.optimization_barrier((grad_act * slope).astype(jnp.bfloat16)).astype(jnp.float32)
    grad_first = jnp.einsum('nsu,nsv->suv', wide, grad_pre, precision=high)
    grad_second = jnp.einsum('nsu,nsv->suv', active, cotangent, precision=high)
    return jnp.stack([grad_first, grad_second], axis=1).astype(jnp.bfloat16)

def reference(x_down, x_up, w_tiles, tile_rows, tile_cols, counts):
    loss_scale = TOTAL ** (-0.5)

    def one_layer(layer):
        partner = (layer + SECTIONS // 2) % SECTIONS
        weights = w_tiles[layer, 0]
        row_ids = tile_rows[layer, 0]
        shared = slot_masks(tile_cols[layer, 0], counts[layer, 0])
        batches = jnp.concatenate([x_down[layer].reshape(-1, ROWS, D), x_up[partner].reshape(-1, ROWS, D)], axis=0)

        def accumulate(summed, inputs):
            piece = lax.optimization_barrier(device_term(inputs, weights, row_ids, shared, loss_scale))
            return (summed + piece.astype(jnp.float32), None)
        summed, _ = lax.scan(accumulate, jnp.zeros((SLOTS, 2, TILE, TILE), jnp.float32), batches)
        return summed.astype(jnp.bfloat16)
    return lax.map(one_layer, jnp.arange(SECTIONS, dtype=jnp.int32))
```

```python
import functools
import math

import jax
import jax.numpy as jnp
from jax import lax
from jax.experimental import pallas as pl
from jax.experimental.pallas import tpu as pltpu
from jax.sharding import PartitionSpec as P

TILE = 128
BF16_ROWS = 16

tanh_scale = math.sqrt(2.0 / math.pi)
cubic_coef = 0.044715


def gelu_pair(hidden):
    square = hidden * hidden
    tangent = jnp.tanh(tanh_scale * (hidden + cubic_coef * hidden * square))
    half = 0.5 * (1.0 + tangent)
    value = hidden * half
    slope = half + 0.5 * hidden * (1.0 - tangent * tangent) * tanh_scale * (
        1.0 + 3.0 * cubic_coef * square
    )
    return (value, slope)


def live_total(slots, owners):
    cap = slots // owners
    return sum(cap - i * cap // owners for i in range(owners))


def slot_order(col_ids, counts_in, live):
    slots = col_ids.shape[0]
    per_owner = slots // counts_in.shape[0]
    slot_ids = jnp.arange(slots, dtype=jnp.int32)
    living = slot_ids % per_owner < jnp.repeat(counts_in, per_owner)
    same = (col_ids[:, None] == col_ids[None, :]) & living[:, None] & living[None, :]
    coupled = jnp.sum(same.astype(jnp.int32), axis=1) > 1
    first = jnp.min(jnp.where(same, slot_ids[None, :], slots), axis=1)
    key = jnp.where(living, jnp.where(coupled, first, slots + slot_ids), 2 * slots) * slots + slot_ids
    rank = jnp.sum((key[None, :] < key[:, None]).astype(jnp.int32), axis=1)
    hit = (rank[None, :] == jnp.arange(live, dtype=jnp.int32)[:, None]).astype(jnp.int32)
    order = jnp.sum(hit * slot_ids[None, :], axis=1)
    flags = jnp.sum(hit * coupled.astype(jnp.int32)[None, :], axis=1)
    return order, flags


def pick_kernel(live, order_ref, rows_ref, x_ref, out_ref, sems):
    copies = []
    for i in range(live):
        at = pl.multiple_of(rows_ref[order_ref[i]] * TILE, TILE)
        copy = pltpu.make_async_copy(x_ref.at[:, pl.ds(at, TILE)], out_ref.at[i], sems.at[i])
        copy.start()
        copies.append(copy)
    for copy in copies:
        copy.wait()


def pick_blocks(inputs, order, row_ids, live):
    rows = inputs.shape[0]
    return pl.pallas_call(
        functools.partial(pick_kernel, live),
        out_shape=jax.ShapeDtypeStruct((live, rows, TILE), inputs.dtype),
        in_specs=[
            pl.BlockSpec(memory_space=pltpu.SMEM),
            pl.BlockSpec(memory_space=pltpu.SMEM),
            pl.BlockSpec(memory_space=pl.ANY),
        ],
        out_specs=pl.BlockSpec(memory_space=pl.ANY),
        scratch_shapes=[pltpu.SemaphoreType.DMA((live,))],
        cost_estimate=pl.CostEstimate(
            flops=0, bytes_accessed=2 * live * rows * TILE * 2, transcendentals=0
        ),
    )(order, row_ids, inputs)


def dot(a, b, over_a, over_b):
    return lax.dot_general(
        a, b, (((over_a,), (over_b,)), ((), ())), preferred_element_type=jnp.float32
    )


def grads_kernel(units, sure, loss_scale, order_ref, flags_ref, down_ref, up_ref, w_ref, out_ref):
    parts, cut = out_ref.shape[0], out_ref.shape[2]

    def put(at, grad):
        grad = grad.astype(out_ref.dtype)
        for part in range(parts):
            out_ref[part, at] = grad[part * cut : (part + 1) * cut]

    for unit in range(units):
        a, b = 2 * unit, 2 * unit + 1
        xs = jnp.concatenate(
            [
                jnp.concatenate([down_ref[a], up_ref[a]], axis=0),
                jnp.concatenate([down_ref[b], up_ref[b]], axis=0),
            ],
            axis=1,
        )
        slot_a, slot_b = order_ref[a], order_ref[b]
        first_a, first_b = w_ref[slot_a, 0], w_ref[slot_b, 0]
        seconds = jnp.concatenate([w_ref[slot_a, 1], w_ref[slot_b, 1]], axis=1)
        if unit < sure:
            hidden = dot(xs, jnp.concatenate([first_a, first_b], axis=0), 1, 0)
            value, slope = gelu_pair(hidden)
            active = value.astype(jnp.bfloat16)
            delta = dot(active, seconds, 1, 0)
            cotangent = (loss_scale * (xs.astype(jnp.float32) + delta)).astype(jnp.bfloat16)
            grad_act = dot(cotangent, seconds, 1, 1)
            grad_pre = (grad_act * slope).astype(jnp.bfloat16)
            grad_first = dot(xs, grad_pre, 0, 0)
            grad_second = dot(active, cotangent, 0, 0)
            put(2 * a, grad_first[:TILE])
            put(2 * b, grad_first[TILE:])
            put(2 * a + 1, grad_second[:, :TILE])
            put(2 * b + 1, grad_second[:, TILE:])
        else:
            mix = flags_ref[a].astype(jnp.float32)
            contrib_a = dot(xs[:, :TILE], first_a, 1, 0)
            contrib_b = dot(xs[:, TILE:], first_b, 1, 0)
            hiddens = (contrib_a + mix * contrib_b, contrib_b + mix * contrib_a)
            spreads, slopes, actives, cotangents = [], [], [], []
            for i in range(2):
                value, slope = gelu_pair(hiddens[i])
                active = value.astype(jnp.bfloat16)
                second = seconds[:, i * TILE : (i + 1) * TILE]
                delta = dot(active, second, 1, 0)
                x = xs[:, i * TILE : (i + 1) * TILE].astype(jnp.float32)
                cotangent = (loss_scale * (x + delta)).astype(jnp.bfloat16)
                spreads.append(dot(cotangent, second, 1, 1))
                slopes.append(slope)
                actives.append(active)
                cotangents.append(cotangent)
            for i, at in enumerate((a, b)):
                grad_act = spreads[i] + mix * spreads[1 - i]
                grad_pre = (grad_act * slopes[i]).astype(jnp.bfloat16)
                put(2 * at, dot(xs[:, i * TILE : (i + 1) * TILE], grad_pre, 0, 0))
                put(2 * at + 1, dot(actives[i], cotangents[i], 0, 0))


def tile_terms(down, up, weights, order, flags, sure, loss_scale, parts):
    live, rows = down.shape[:2]
    cut = TILE // parts
    pieces = parts if cut % BF16_ROWS == 0 else 1
    vmem = pl.BlockSpec(memory_space=pltpu.VMEM)
    smem = pl.BlockSpec(memory_space=pltpu.SMEM)
    terms = pl.pallas_call(
        functools.partial(grads_kernel, live // 2, sure, loss_scale),
        out_shape=jax.ShapeDtypeStruct((pieces, 2 * live, TILE // pieces, TILE), jnp.bfloat16),
        in_specs=[smem, smem, vmem, vmem, vmem],
        out_specs=vmem,
        compiler_params=pltpu.CompilerParams(vmem_limit_bytes=32 * 1024 * 1024),
        cost_estimate=pl.CostEstimate(
            flops=10 * 2 * live * rows * TILE * TILE,
            bytes_accessed=5_000_000,
            transcendentals=2 * live * rows * TILE,
        ),
    )(order, flags, down, up, weights)
    return jnp.swapaxes(
        terms.reshape(pieces, 2 * live, parts // pieces, cut, TILE), 1, 2
    ).reshape(parts, 2 * live, cut, TILE)


def sum_kernel(live, order_ref, terms_ref, out_ref):
    out_ref[...] = jnp.zeros_like(out_ref)
    for i in range(live):
        for k in range(2):
            total = terms_ref[0, 2 * i + k].astype(jnp.float32)
            for source in range(1, terms_ref.shape[0]):
                total += terms_ref[source, 2 * i + k].astype(jnp.float32)
            out_ref[order_ref[i], k] = total.astype(out_ref.dtype)


def sum_terms(terms, order, slots):
    parts, doubled, cut, width = terms.shape
    return pl.pallas_call(
        functools.partial(sum_kernel, doubled // 2),
        out_shape=jax.ShapeDtypeStruct((slots, 2, cut, width), jnp.bfloat16),
        in_specs=[
            pl.BlockSpec(memory_space=pltpu.SMEM),
            pl.BlockSpec(memory_space=pltpu.VMEM),
        ],
        out_specs=pl.BlockSpec(memory_space=pltpu.VMEM),
        compiler_params=pltpu.CompilerParams(vmem_limit_bytes=32 * 1024 * 1024),
        cost_estimate=pl.CostEstimate(
            flops=parts * doubled * cut * width, bytes_accessed=2_000_000, transcendentals=0
        ),
    )(order, terms)


def body(x_down, x_up, w_tiles, tile_rows, tile_cols, counts):
    rows_here = x_down.shape[2]
    slots, owners = tile_cols.shape[2], counts.shape[2]
    live = live_total(slots, owners)
    sure = slots // 2 - (slots - live)
    replicas = lax.axis_size("dp")
    parts = replicas * owners
    loss_scale = float(2 * rows_here * parts) ** (-0.5)
    sections = lax.axis_size("section")
    mirror_by = sections // 2

    partner_order, _ = slot_order(tile_cols[0, 1], counts[0, 1], live)
    leaving = pick_blocks(x_up[0, 0], partner_order, tile_rows[0, 1], live)
    arrived = lax.ppermute(
        leaving, "section", [(i, (i + mirror_by) % sections) for i in range(sections)]
    )
    gathered = lax.all_gather(w_tiles[0, 0], "fsdp", axis=0, tiled=True)
    order, flags = slot_order(tile_cols[0, 0], counts[0, 0], live)
    staying = pick_blocks(x_down[0, 0], order, tile_rows[0, 0], live)
    terms = tile_terms(staying, arrived, gathered, order, flags, sure, loss_scale, parts)
    plane = ("dp", "fsdp")
    traded = lax.all_to_all(terms, plane, split_axis=0, concat_axis=0, tiled=True)
    summed = sum_terms(traded, order, slots)
    cut = summed.shape[2]
    by_owner = summed.reshape(owners, slots // owners * 2, cut, TILE)
    for_all = jnp.broadcast_to(by_owner[None], (replicas,) + by_owner.shape).reshape(
        (parts,) + by_owner.shape[1:]
    )
    mine = lax.all_to_all(for_all, plane, split_axis=0, concat_axis=0, tiled=True)
    return jnp.swapaxes(mine, 0, 1).reshape(1, slots // owners, 2, TILE, TILE)


def solution(mesh):
    in_specs = (
        P("section", "dp", "fsdp", None),
        P("section", "dp", "fsdp", None),
        P("section", None, "fsdp", None, None, None),
        P("section", None, None),
        P("section", None, None),
        P("section", None, None),
    )
    out_specs = P("section", "fsdp", None, None, None)
    return jax.shard_map(body, mesh=mesh, in_specs=in_specs, out_specs=out_specs, check_vma=False)
```

```python
import functools
import math

import jax
import jax.numpy as jnp
from jax import lax
from jax.experimental import pallas as pl
from jax.experimental.pallas import tpu as pltpu
from jax.sharding import PartitionSpec as P

TILE = 128
BF16_ROWS = 16

tanh_scale = math.sqrt(2.0 / math.pi)
cubic_coef = 0.044715


def gelu_pair(hidden):
    square = hidden * hidden
    tangent = jnp.tanh(tanh_scale * (hidden + cubic_coef * hidden * square))
    half = 0.5 * (1.0 + tangent)
    value = hidden * half
    slope = half + 0.5 * hidden * (1.0 - tangent * tangent) * tanh_scale * (
        1.0 + 3.0 * cubic_coef * square
    )
    return (value, slope)


def live_total(slots, owners):
    cap = slots // owners
    return sum(cap - i * cap // owners for i in range(owners))


def order_slots(cols_ref, counts_ref, which, slots, live, order_ref, flags_ref):
    per_owner = slots // counts_ref.shape[2]
    cols = [cols_ref[0, which, s] for s in range(slots)]
    living = [counts_ref[0, which, s // per_owner] > s % per_owner for s in range(slots)]
    partner = [jnp.int32(-1)] * slots
    for s in range(slots):
        for t in range(s + 1, slots):
            same = (cols[s] == cols[t]) & living[s] & living[t]
            partner[s] = jnp.where(same, t, partner[s])
            partner[t] = jnp.where(same, s, partner[t])
    ahead = jnp.int32(0)
    for s in range(slots):
        leads = partner[s] > s
        at = jnp.where(leads, ahead, live)
        order_ref[at] = s
        order_ref[at + 1] = partner[s]
        flags_ref[at] = 1
        flags_ref[at + 1] = 1
        ahead = ahead + jnp.where(leads, 2, 0)
    for s in range(slots):
        alone = living[s] & (partner[s] < 0)
        at = jnp.where(alone, ahead, live)
        order_ref[at] = s
        flags_ref[at] = 0
        ahead = ahead + jnp.where(alone, 1, 0)


def pick_kernel(which, slots, live, rows_ref, cols_ref, counts_ref, x_ref, *refs):
    out_refs, (order_ref, flags_ref, sems) = refs[:-3], refs[-3:]
    order_slots(cols_ref, counts_ref, which, slots, live, order_ref, flags_ref)
    copies = []
    for out_ref in out_refs:
        for i in range(out_ref.shape[0]):
            slot = order_ref[len(copies)]
            at = pl.multiple_of(rows_ref[0, which, slot] * TILE, TILE)
            copy = pltpu.make_async_copy(
                x_ref.at[0, 0, :, pl.ds(at, TILE)], out_ref.at[i], sems.at[len(copies)]
            )
            copy.start()
            copies.append(copy)
    for copy in copies:
        copy.wait()


def pick_blocks(inputs, which, tile_rows, tile_cols, counts, chunks, share_order):
    rows, slots, live = inputs.shape[2], tile_cols.shape[2], sum(chunks)
    smem = pl.BlockSpec(memory_space=pltpu.SMEM)
    vmem = pl.BlockSpec(memory_space=pltpu.VMEM)
    out_shape = [jax.ShapeDtypeStruct((n, rows, TILE), inputs.dtype) for n in chunks]
    out_specs = [vmem] * len(chunks)
    scratch = [pltpu.SMEM((live + 2,), jnp.int32)] * 2
    if share_order:
        out_shape += [jax.ShapeDtypeStruct((live + 2,), jnp.int32)] * 2
        out_specs += [smem] * 2
        scratch = []
    return pl.pallas_call(
        functools.partial(pick_kernel, which, slots, live),
        out_shape=out_shape,
        in_specs=[smem, smem, smem, pl.BlockSpec(memory_space=pl.ANY)],
        out_specs=out_specs,
        scratch_shapes=scratch + [pltpu.SemaphoreType.DMA((live,))],
        cost_estimate=pl.CostEstimate(
            flops=0, bytes_accessed=2 * live * rows * TILE * 2, transcendentals=0
        ),
    )(tile_rows, tile_cols, counts, inputs)


def dot(a, b, over_a, over_b):
    return lax.dot_general(
        a, b, (((over_a,), (over_b,)), ((), ())), preferred_element_type=jnp.float32
    )


def grads_kernel(units, base, sure, loss_scale, order_ref, flags_ref, down_ref, up_ref, w_ref, out_ref):
    parts, cut = out_ref.shape[0], out_ref.shape[2]

    def put(at, grad):
        grad = grad.astype(out_ref.dtype)
        for part in range(parts):
            out_ref[part, at] = grad[part * cut : (part + 1) * cut]

    for unit in range(units):
        a, b = 2 * unit, 2 * unit + 1
        xs = jnp.concatenate(
            [
                jnp.concatenate([down_ref[a], up_ref[a]], axis=0),
                jnp.concatenate([down_ref[b], up_ref[b]], axis=0),
            ],
            axis=1,
        )
        slot_a, slot_b = order_ref[base + a], order_ref[base + b]
        first_a, first_b = w_ref[slot_a, 0], w_ref[slot_b, 0]
        seconds = jnp.concatenate([w_ref[slot_a, 1], w_ref[slot_b, 1]], axis=1)
        if unit < sure:
            hidden = dot(xs, jnp.concatenate([first_a, first_b], axis=0), 1, 0)
            value, slope = gelu_pair(hidden)
            active = value.astype(jnp.bfloat16)
            delta = dot(active, seconds, 1, 0)
            cotangent = (loss_scale * (xs.astype(jnp.float32) + delta)).astype(jnp.bfloat16)
            grad_act = dot(cotangent, seconds, 1, 1)
            grad_pre = (grad_act * slope).astype(jnp.bfloat16)
            grad_first = dot(xs, grad_pre, 0, 0)
            grad_second = dot(active, cotangent, 0, 0)
            put(2 * a, grad_first[:TILE])
            put(2 * b, grad_first[TILE:])
            put(2 * a + 1, grad_second[:, :TILE])
            put(2 * b + 1, grad_second[:, TILE:])
        else:
            mix = flags_ref[base + a].astype(jnp.float32)
            contrib_a = dot(xs[:, :TILE], first_a, 1, 0)
            contrib_b = dot(xs[:, TILE:], first_b, 1, 0)
            hiddens = (contrib_a + mix * contrib_b, contrib_b + mix * contrib_a)
            spreads, slopes, actives, cotangents = [], [], [], []
            for i in range(2):
                value, slope = gelu_pair(hiddens[i])
                active = value.astype(jnp.bfloat16)
                second = seconds[:, i * TILE : (i + 1) * TILE]
                delta = dot(active, second, 1, 0)
                x = xs[:, i * TILE : (i + 1) * TILE].astype(jnp.float32)
                cotangent = (loss_scale * (x + delta)).astype(jnp.bfloat16)
                spreads.append(dot(cotangent, second, 1, 1))
                slopes.append(slope)
                actives.append(active)
                cotangents.append(cotangent)
            for i, at in enumerate((a, b)):
                grad_act = spreads[i] + mix * spreads[1 - i]
                grad_pre = (grad_act * slopes[i]).astype(jnp.bfloat16)
                put(2 * at, dot(xs[:, i * TILE : (i + 1) * TILE], grad_pre, 0, 0))
                put(2 * at + 1, dot(actives[i], cotangents[i], 0, 0))


def tile_terms(down, up, weights, order, flags, base, sure, loss_scale, parts):
    live, rows = down.shape[:2]
    cut = TILE // parts
    pieces = parts if cut % BF16_ROWS == 0 else 1
    vmem = pl.BlockSpec(memory_space=pltpu.VMEM)
    smem = pl.BlockSpec(memory_space=pltpu.SMEM)
    terms = pl.pallas_call(
        functools.partial(grads_kernel, live // 2, base, sure, loss_scale),
        out_shape=jax.ShapeDtypeStruct((pieces, 2 * live, TILE // pieces, TILE), jnp.bfloat16),
        in_specs=[smem, smem, vmem, vmem, vmem],
        out_specs=vmem,
        compiler_params=pltpu.CompilerParams(vmem_limit_bytes=32 * 1024 * 1024),
        cost_estimate=pl.CostEstimate(
            flops=10 * 2 * live * rows * TILE * TILE,
            bytes_accessed=5_000_000,
            transcendentals=2 * live * rows * TILE,
        ),
    )(order, flags, down, up, weights)
    return jnp.swapaxes(
        terms.reshape(pieces, 2 * live, parts // pieces, cut, TILE), 1, 2
    ).reshape(parts, 2 * live, cut, TILE)


def sum_kernel(chunks, order_ref, *refs):
    terms_refs, out_ref = refs[:-1], refs[-1]
    out_ref[...] = jnp.zeros_like(out_ref)
    base = 0
    for terms_ref, live in zip(terms_refs, chunks):
        for i in range(live):
            for k in range(2):
                total = terms_ref[0, 2 * i + k].astype(jnp.float32)
                for source in range(1, terms_ref.shape[0]):
                    total += terms_ref[source, 2 * i + k].astype(jnp.float32)
                out_ref[order_ref[base + i], k] = total.astype(out_ref.dtype)
        base += live


def sum_terms(chunk_terms, order, slots):
    parts, _, cut, width = chunk_terms[0].shape
    chunks = [terms.shape[1] // 2 for terms in chunk_terms]
    vmem = pl.BlockSpec(memory_space=pltpu.VMEM)
    return pl.pallas_call(
        functools.partial(sum_kernel, chunks),
        out_shape=jax.ShapeDtypeStruct((slots, 2, cut, width), jnp.bfloat16),
        in_specs=[pl.BlockSpec(memory_space=pltpu.SMEM)] + [vmem] * len(chunks),
        out_specs=vmem,
        compiler_params=pltpu.CompilerParams(vmem_limit_bytes=32 * 1024 * 1024),
        cost_estimate=pl.CostEstimate(
            flops=parts * 2 * sum(chunks) * cut * width, bytes_accessed=2_000_000, transcendentals=0
        ),
    )(order, *chunk_terms)


def body(x_down, x_up, w_tiles, tile_rows, tile_cols, counts):
    rows_here = x_down.shape[2]
    slots, owners = tile_cols.shape[2], counts.shape[2]
    live = live_total(slots, owners)
    sure = slots // 2 - (slots - live)
    chunks = [2 * sure, live - 2 * sure]
    replicas = lax.axis_size("dp")
    parts = replicas * owners
    loss_scale = float(2 * rows_here * parts) ** (-0.5)
    sections = lax.axis_size("section")
    across = [(i, (i + sections // 2) % sections) for i in range(sections)]

    leaving = pick_blocks(x_up, 1, tile_rows, tile_cols, counts, chunks, False)
    arrived = [lax.ppermute(blocks, "section", across) for blocks in leaving]
    gathered = lax.all_gather(w_tiles[0, 0], "fsdp", axis=0, tiled=True)
    *staying, order, flags = pick_blocks(x_down, 0, tile_rows, tile_cols, counts, chunks, True)
    plane = ("dp", "fsdp")
    traded, base = [], 0
    for down, up in zip(staying, arrived):
        terms = tile_terms(
            down, up, gathered, order, flags, base, sure - base // 2, loss_scale, parts
        )
        traded.append(lax.all_to_all(terms, plane, split_axis=0, concat_axis=0, tiled=True))
        base += down.shape[0]
    summed = sum_terms(traded, order, slots)
    cut = summed.shape[2]
    by_owner = summed.reshape(owners, slots // owners * 2, cut, TILE)
    for_all = jnp.broadcast_to(by_owner[None], (replicas,) + by_owner.shape).reshape(
        (parts,) + by_owner.shape[1:]
    )
    mine = lax.all_to_all(for_all, plane, split_axis=0, concat_axis=0, tiled=True)
    return jnp.swapaxes(mine, 0, 1).reshape(1, slots // owners, 2, TILE, TILE)


def solution(mesh):
    in_specs = (
        P("section", "dp", "fsdp", None),
        P("section", "dp", "fsdp", None),
        P("section", None, "fsdp", None, None, None),
        P("section", None, None),
        P("section", None, None),
        P("section", None, None),
    )
    out_specs = P("section", "fsdp", None, None, None)
    return jax.shard_map(body, mesh=mesh, in_specs=in_specs, out_specs=out_specs, check_vma=False)
```

```python
import functools
import math

import jax
import jax.numpy as jnp
from jax import lax
from jax.experimental import pallas as pl
from jax.experimental.pallas import tpu as pltpu
from jax.sharding import PartitionSpec as P

TILE = 128
PLANE = ("dp", "fsdp")
SOURCES_AT_ONCE = 4

tanh_scale = math.sqrt(2.0 / math.pi)
cubic_coef = 0.044715


def gelu_pair(hidden):
    square = hidden * hidden
    tangent = jnp.tanh(tanh_scale * (hidden + cubic_coef * hidden * square))
    half = 0.5 * (1.0 + tangent)
    value = hidden * half
    slope = half + 0.5 * hidden * (1.0 - tangent * tangent) * tanh_scale * (
        1.0 + 3.0 * cubic_coef * square
    )
    return (value, slope)


def live_total(slots, owners):
    cap = slots // owners
    return sum(cap - i * cap // owners for i in range(owners))


def order_slots(cols_ref, counts_ref, which, slots, live, order_ref, flags_ref):
    per_owner = slots // counts_ref.shape[2]
    cols = [cols_ref[0, which, s] for s in range(slots)]
    living = [counts_ref[0, which, s // per_owner] > s % per_owner for s in range(slots)]
    partner = [jnp.int32(-1)] * slots
    for s in range(slots):
        for t in range(s + 1, slots):
            same = (cols[s] == cols[t]) & living[s] & living[t]
            partner[s] = jnp.where(same, t, partner[s])
            partner[t] = jnp.where(same, s, partner[t])
    ahead = jnp.int32(0)
    for s in range(slots):
        leads = partner[s] > s
        at = jnp.where(leads, ahead, live)
        order_ref[at] = s
        order_ref[at + 1] = partner[s]
        flags_ref[at] = 1
        flags_ref[at + 1] = 1
        ahead = ahead + jnp.where(leads, 2, 0)
    for s in range(slots):
        alone = living[s] & (partner[s] < 0)
        at = jnp.where(alone, ahead, live)
        order_ref[at] = s
        flags_ref[at] = 0
        ahead = ahead + jnp.where(alone, 1, 0)
    order_ref[live] = 0
    order_ref[live + 1] = 0


def pack_kernel(
    live, halfway, rows_ref, cols_ref, counts_ref, down_ref, up_ref, w_ref,
    out_ref, own_w_ref, order_ref, flags_ref, up_order_ref, up_flags_ref, sems, w_sem,
):
    slots = cols_ref.shape[2]
    places = out_ref.shape[0] // 2
    weights = pltpu.make_async_copy(w_ref.at[0, 0], own_w_ref, w_sem)
    weights.start()
    behind = jnp.where(lax.axis_index("section") < halfway, 0, places)
    copies = []
    for which, x_ref, order, flags, base in (
        (1, up_ref, up_order_ref, up_flags_ref, places - behind),
        (0, down_ref, order_ref, flags_ref, behind),
    ):
        order_slots(cols_ref, counts_ref, which, slots, live, order, flags)
        for i in range(live):
            at = pl.multiple_of(rows_ref[0, which, order[i]] * TILE, TILE)
            copy = pltpu.make_async_copy(
                x_ref.at[0, 0, :, pl.ds(at, TILE)],
                out_ref.at[base + i // 2, i % 2],
                sems.at[len(copies)],
            )
            copy.start()
            copies.append(copy)
    for place in range(live // 2, places):
        out_ref[place] = jnp.zeros(out_ref.shape[1:], out_ref.dtype)
        out_ref[places + place] = jnp.zeros(out_ref.shape[1:], out_ref.dtype)
    for copy in copies:
        copy.wait()
    weights.wait()


def pack(x_down, x_up, w_tiles, tile_rows, tile_cols, counts, live, places, halfway):
    rows = x_down.shape[2]
    smem = pl.BlockSpec(memory_space=pltpu.SMEM)
    vmem = pl.BlockSpec(memory_space=pltpu.VMEM)
    hbm = pl.BlockSpec(memory_space=pl.ANY)
    return pl.pallas_call(
        functools.partial(pack_kernel, live, halfway),
        out_shape=[
            jax.ShapeDtypeStruct((2 * places, 2, rows, TILE), x_down.dtype),
            jax.ShapeDtypeStruct(w_tiles.shape[2:], w_tiles.dtype),
            jax.ShapeDtypeStruct((live + 2,), jnp.int32),
            jax.ShapeDtypeStruct((live + 2,), jnp.int32),
        ],
        in_specs=[smem, smem, smem, hbm, hbm, hbm],
        out_specs=[vmem, vmem, smem, smem],
        scratch_shapes=[
            pltpu.SMEM((live + 2,), jnp.int32),
            pltpu.SMEM((live + 2,), jnp.int32),
            pltpu.SemaphoreType.DMA((2 * live,)),
            pltpu.SemaphoreType.DMA,
        ],
        compiler_params=pltpu.CompilerParams(vmem_limit_bytes=32 * 1024 * 1024),
        cost_estimate=pl.CostEstimate(
            flops=0, bytes_accessed=8 * live * rows * TILE, transcendentals=0
        ),
    )(tile_rows, tile_cols, counts, x_down, x_up, w_tiles)


def dot(a, b, over_a, over_b):
    return lax.dot_general(
        a, b, (((over_a,), (over_b,)), ((), ())), preferred_element_type=jnp.float32
    )


def grads_kernel(
    units, loss_scale, order_ref, flags_ref, x_ref, w_ref, out_ref,
    w_own, first_sum, second_sum, sems,
):
    sources, _, rows, _ = x_ref.shape
    unit = jnp.minimum(lax.axis_index(PLANE), units - 1)
    copies = [
        pltpu.make_async_copy(w_ref.at[order_ref[2 * unit + i]], w_own.at[i], sems.at[i])
        for i in range(2)
    ]
    for copy in copies:
        copy.start()
    first_sum[...] = jnp.zeros_like(first_sum)
    second_sum[...] = jnp.zeros_like(second_sum)
    for copy in copies:
        copy.wait()
    together = min(SOURCES_AT_ONCE, sources)
    steps = sources // together
    coupled = flags_ref[2 * unit] == 1

    def read(step):
        at = step * together
        return [
            x_ref[pl.ds(at, together), i].reshape(together * rows, TILE) for i in range(2)
        ]

    @pl.when(coupled)
    def _():
        def go(step, carry):
            xs = jnp.concatenate(read(step), axis=1)
            firsts = jnp.concatenate([w_own[0, 0], w_own[1, 0]], axis=0)
            seconds = jnp.concatenate([w_own[0, 1], w_own[1, 1]], axis=1)
            value, slope = gelu_pair(dot(xs, firsts, 1, 0))
            active = value.astype(jnp.bfloat16)
            delta = dot(active, seconds, 1, 0)
            cotangent = (loss_scale * (xs.astype(jnp.float32) + delta)).astype(jnp.bfloat16)
            grad_act = dot(cotangent, seconds, 1, 1)
            grad_pre = (grad_act * slope).astype(jnp.bfloat16)
            first_sum[...] += dot(xs, grad_pre, 0, 0)
            second_sum[...] += dot(active, cotangent, 0, 0)
            return carry

        lax.fori_loop(0, steps, go, 0, unroll=min(steps, 4))

    @pl.when(jnp.logical_not(coupled))
    def _():
        def go(step, carry):
            for i, x in enumerate(read(step)):
                across = slice(i * TILE, (i + 1) * TILE)
                value, slope = gelu_pair(dot(x, w_own[i, 0], 1, 0))
                active = value.astype(jnp.bfloat16)
                delta = dot(active, w_own[i, 1], 1, 0)
                cotangent = (loss_scale * (x.astype(jnp.float32) + delta)).astype(jnp.bfloat16)
                grad_act = dot(cotangent, w_own[i, 1], 1, 1)
                grad_pre = (grad_act * slope).astype(jnp.bfloat16)
                first_sum[across, :] += dot(x, grad_pre, 0, 0)
                second_sum[:, across] += dot(active, cotangent, 0, 0)
            return carry

        lax.fori_loop(0, steps, go, 0, unroll=min(steps, 4))

    for i in range(2):
        across = slice(i * TILE, (i + 1) * TILE)
        out_ref[i, 0] = first_sum[across, :].astype(out_ref.dtype)
        out_ref[i, 1] = second_sum[:, across].astype(out_ref.dtype)


def unit_grads(blocks, weights, order, flags, units, loss_scale):
    sources, _, rows, _ = blocks.shape
    smem = pl.BlockSpec(memory_space=pltpu.SMEM)
    vmem = pl.BlockSpec(memory_space=pltpu.VMEM)
    return pl.pallas_call(
        functools.partial(grads_kernel, units, loss_scale),
        out_shape=jax.ShapeDtypeStruct((2, 2, TILE, TILE), jnp.bfloat16),
        in_specs=[smem, smem, vmem, pl.BlockSpec(memory_space=pl.ANY)],
        out_specs=vmem,
        scratch_shapes=[
            pltpu.VMEM((2, 2, TILE, TILE), jnp.bfloat16),
            pltpu.VMEM((2 * TILE, TILE), jnp.float32),
            pltpu.VMEM((TILE, 2 * TILE), jnp.float32),
            pltpu.SemaphoreType.DMA((2,)),
        ],
        compiler_params=pltpu.CompilerParams(vmem_limit_bytes=32 * 1024 * 1024),
        cost_estimate=pl.CostEstimate(
            flops=20 * sources * rows * TILE * TILE,
            bytes_accessed=4 * sources * rows * TILE,
            transcendentals=2 * sources * rows * TILE,
        ),
    )(order, flags, blocks, weights)


def place_kernel(live, order_ref, counts_ref, grads_ref, out_ref, sems):
    owner = lax.axis_index("fsdp")
    per_owner = out_ref.shape[0]
    for slot in range(per_owner):

        @pl.when(counts_ref[0, 0, owner] <= slot)
        def _():
            out_ref[slot] = jnp.zeros(out_ref.shape[1:], out_ref.dtype)

    def each(act):
        for i in range(live):
            at = order_ref[i] - owner * per_owner

            @pl.when((at >= 0) & (at < per_owner))
            def _():
                act(
                    pltpu.make_async_copy(
                        grads_ref.at[i // 2, i % 2], out_ref.at[at], sems.at[i]
                    )
                )

    each(lambda copy: copy.start())
    each(lambda copy: copy.wait())


def place(grads, order, counts, live, per_owner):
    smem = pl.BlockSpec(memory_space=pltpu.SMEM)
    return pl.pallas_call(
        functools.partial(place_kernel, live),
        out_shape=jax.ShapeDtypeStruct((per_owner,) + grads.shape[2:], grads.dtype),
        in_specs=[smem, smem, pl.BlockSpec(memory_space=pl.ANY)],
        out_specs=pl.BlockSpec(memory_space=pltpu.VMEM),
        scratch_shapes=[pltpu.SemaphoreType.DMA((live,))],
        cost_estimate=pl.CostEstimate(flops=0, bytes_accessed=1_000_000, transcendentals=0),
    )(order, counts, grads)


def body(x_down, x_up, w_tiles, tile_rows, tile_cols, counts):
    rows_here = x_down.shape[2]
    slots, owners = tile_cols.shape[2], counts.shape[2]
    live = live_total(slots, owners)
    places = lax.axis_size("dp") * lax.axis_size("fsdp")
    sections = lax.axis_size("section")
    halfway = sections // 2
    loss_scale = float(2 * rows_here * places) ** (-0.5)

    packed, own_w, order, flags = pack(
        x_down, x_up, w_tiles, tile_rows, tile_cols, counts, live, places, halfway
    )
    weights = lax.all_gather(own_w, "fsdp", axis=0, tiled=True)
    groups = [
        [(s + side * halfway) * places + place for side in range(2) for place in range(places)]
        for s in range(halfway)
    ]
    blocks = lax.all_to_all(
        packed, ("section",) + PLANE, split_axis=0, concat_axis=0,
        axis_index_groups=groups, tiled=True,
    )
    mine = unit_grads(blocks, weights, order, flags, live // 2, loss_scale)
    everyone = lax.all_gather(mine, PLANE, axis=0, tiled=False)
    return place(everyone, order, counts, live, slots // owners)[None]


def solution(mesh):
    in_specs = (
        P("section", "dp", "fsdp", None),
        P("section", "dp", "fsdp", None),
        P("section", None, "fsdp", None, None, None),
        P("section", None, None),
        P("section", None, None),
        P("section", None, None),
    )
    out_specs = P("section", "fsdp", None, None, None)
    return jax.shard_map(body, mesh=mesh, in_specs=in_specs, out_specs=out_specs, check_vma=False)
```

```python
import functools
import math

import jax
import jax.numpy as jnp
from jax import lax
from jax.experimental import pallas as pl
from jax.experimental.pallas import tpu as pltpu
from jax.sharding import PartitionSpec as P

TILE = 128
PLANE = ("dp", "fsdp")
SOURCES_AT_ONCE = 4

tanh_scale = math.sqrt(2.0 / math.pi)
cubic_coef = 0.044715


def gelu_pair(hidden):
    square = hidden * hidden
    tangent = jnp.tanh(tanh_scale * (hidden + cubic_coef * hidden * square))
    half = 0.5 * (1.0 + tangent)
    value = hidden * half
    slope = half + 0.5 * hidden * (1.0 - tangent * tangent) * tanh_scale * (
        1.0 + 3.0 * cubic_coef * square
    )
    return (value, slope)


def live_total(slots, owners):
    cap = slots // owners
    return sum(cap - i * cap // owners for i in range(owners))


def order_slots(cols_ref, counts_ref, which, slots, live, order_ref, flags_ref):
    per_owner = slots // counts_ref.shape[2]
    cols = [cols_ref[0, which, s] for s in range(slots)]
    living = [counts_ref[0, which, s // per_owner] > s % per_owner for s in range(slots)]
    partner = [jnp.int32(-1)] * slots
    for s in range(slots):
        for t in range(s + 1, slots):
            same = (cols[s] == cols[t]) & living[s] & living[t]
            partner[s] = jnp.where(same, t, partner[s])
            partner[t] = jnp.where(same, s, partner[t])
    ahead = jnp.int32(0)
    for s in range(slots):
        leads = partner[s] > s
        at = jnp.where(leads, ahead, live)
        order_ref[at] = s
        order_ref[at + 1] = partner[s]
        flags_ref[at] = 1
        flags_ref[at + 1] = 1
        ahead = ahead + jnp.where(leads, 2, 0)
    for s in range(slots):
        alone = living[s] & (partner[s] < 0)
        at = jnp.where(alone, ahead, live)
        order_ref[at] = s
        flags_ref[at] = 0
        ahead = ahead + jnp.where(alone, 1, 0)
    order_ref[live] = 0
    order_ref[live + 1] = 0


def pack_kernel(
    live, halfway, rows_ref, cols_ref, counts_ref, down_ref, up_ref, w_ref,
    out_ref, own_w_ref, order_ref, flags_ref, up_order_ref, up_flags_ref, sems, w_sem,
):
    slots = cols_ref.shape[2]
    places = out_ref.shape[0] // 2
    weights = pltpu.make_async_copy(w_ref.at[0, 0], own_w_ref, w_sem)
    weights.start()
    behind = jnp.where(lax.axis_index("section") < halfway, 0, places)
    copies = []
    for which, x_ref, order, flags, base in (
        (1, up_ref, up_order_ref, up_flags_ref, places - behind),
        (0, down_ref, order_ref, flags_ref, behind),
    ):
        order_slots(cols_ref, counts_ref, which, slots, live, order, flags)
        for i in range(live):
            at = pl.multiple_of(rows_ref[0, which, order[i]] * TILE, TILE)
            copy = pltpu.make_async_copy(
                x_ref.at[0, 0, :, pl.ds(at, TILE)],
                out_ref.at[base + i // 2, i % 2],
                sems.at[len(copies)],
            )
            copy.start()
            copies.append(copy)
    for place in range(live // 2, places):
        out_ref[place] = jnp.zeros(out_ref.shape[1:], out_ref.dtype)
        out_ref[places + place] = jnp.zeros(out_ref.shape[1:], out_ref.dtype)
    for copy in copies:
        copy.wait()
    weights.wait()


def pack(x_down, x_up, w_tiles, tile_rows, tile_cols, counts, live, places, halfway):
    rows = x_down.shape[2]
    smem = pl.BlockSpec(memory_space=pltpu.SMEM)
    vmem = pl.BlockSpec(memory_space=pltpu.VMEM)
    hbm = pl.BlockSpec(memory_space=pl.ANY)
    return pl.pallas_call(
        functools.partial(pack_kernel, live, halfway),
        out_shape=[
            jax.ShapeDtypeStruct((2 * places, 2, rows, TILE), x_down.dtype),
            jax.ShapeDtypeStruct(w_tiles.shape[2:], w_tiles.dtype),
            jax.ShapeDtypeStruct((live + 2,), jnp.int32),
            jax.ShapeDtypeStruct((live + 2,), jnp.int32),
        ],
        in_specs=[smem, smem, smem, hbm, hbm, hbm],
        out_specs=[vmem, vmem, smem, smem],
        scratch_shapes=[
            pltpu.SMEM((live + 2,), jnp.int32),
            pltpu.SMEM((live + 2,), jnp.int32),
            pltpu.SemaphoreType.DMA((2 * live,)),
            pltpu.SemaphoreType.DMA,
        ],
        cost_estimate=pl.CostEstimate(
            flops=0, bytes_accessed=8 * live * rows * TILE, transcendentals=0
        ),
    )(tile_rows, tile_cols, counts, x_down, x_up, w_tiles)


def gather_all(array, axis):
    size = lax.axis_size(axis)
    far = size // 2
    while far:
        partner = lax.ppermute(array, axis, [(i, i ^ far) for i in range(size)])
        array = jnp.concatenate([array, partner], axis=0)
        far //= 2
    return array


def gather_place(size, owner, me):
    apart, far, weight, at = owner ^ me, size // 2, 1, 0
    while far:
        at = at + jnp.where((apart & far) != 0, weight, 0)
        far, weight = far // 2, weight * 2
    return at


def dot(a, b, over_a, over_b):
    return lax.dot_general(
        a, b, (((over_a,), (over_b,)), ((), ())), preferred_element_type=jnp.float32
    )


def grads_kernel(
    units, owners, loss_scale, order_ref, flags_ref, x_ref, w_ref, out_ref,
    w_own, first_sum, second_sum, sems,
):
    sources, _, rows, _ = x_ref.shape
    per_owner = w_ref.shape[0] // owners
    unit = jnp.minimum(lax.axis_index(PLANE), units - 1)
    me = lax.axis_index("fsdp")
    copies = []
    for i in range(2):
        slot = order_ref[2 * unit + i]
        owner = slot // per_owner
        at = gather_place(owners, owner, me) * per_owner + slot - owner * per_owner
        copies.append(pltpu.make_async_copy(w_ref.at[at], w_own.at[i], sems.at[i]))
    for copy in copies:
        copy.start()
    first_sum[...] = jnp.zeros_like(first_sum)
    second_sum[...] = jnp.zeros_like(second_sum)
    for copy in copies:
        copy.wait()
    together = min(SOURCES_AT_ONCE, sources)
    steps = sources // together
    coupled = flags_ref[2 * unit] == 1

    def read(step):
        at = step * together
        return [
            x_ref[pl.ds(at, together), i].reshape(together * rows, TILE) for i in range(2)
        ]

    @pl.when(coupled)
    def _():
        def go(step, carry):
            xs = jnp.concatenate(read(step), axis=1)
            firsts = jnp.concatenate([w_own[0, 0], w_own[1, 0]], axis=0)
            seconds = jnp.concatenate([w_own[0, 1], w_own[1, 1]], axis=1)
            value, slope = gelu_pair(dot(xs, firsts, 1, 0))
            active = value.astype(jnp.bfloat16)
            delta = dot(active, seconds, 1, 0)
            cotangent = (loss_scale * (xs.astype(jnp.float32) + delta)).astype(jnp.bfloat16)
            grad_act = dot(cotangent, seconds, 1, 1)
            grad_pre = (grad_act * slope).astype(jnp.bfloat16)
            first_sum[...] += dot(xs, grad_pre, 0, 0)
            second_sum[...] += dot(active, cotangent, 0, 0)
            return carry

        lax.fori_loop(0, steps, go, 0, unroll=min(steps, 4))

    @pl.when(jnp.logical_not(coupled))
    def _():
        def go(step, carry):
            for i, x in enumerate(read(step)):
                across = slice(i * TILE, (i + 1) * TILE)
                value, slope = gelu_pair(dot(x, w_own[i, 0], 1, 0))
                active = value.astype(jnp.bfloat16)
                delta = dot(active, w_own[i, 1], 1, 0)
                cotangent = (loss_scale * (x.astype(jnp.float32) + delta)).astype(jnp.bfloat16)
                grad_act = dot(cotangent, w_own[i, 1], 1, 1)
                grad_pre = (grad_act * slope).astype(jnp.bfloat16)
                first_sum[across, :] += dot(x, grad_pre, 0, 0)
                second_sum[:, across] += dot(active, cotangent, 0, 0)
            return carry

        lax.fori_loop(0, steps, go, 0, unroll=min(steps, 4))

    for i in range(2):
        across = slice(i * TILE, (i + 1) * TILE)
        for copy in range(out_ref.shape[0]):
            out_ref[copy, i, 0] = first_sum[across, :].astype(out_ref.dtype)
            out_ref[copy, i, 1] = second_sum[:, across].astype(out_ref.dtype)


def unit_grads(blocks, weights, order, flags, units, owners, copies, loss_scale):
    sources, _, rows, _ = blocks.shape
    smem = pl.BlockSpec(memory_space=pltpu.SMEM)
    vmem = pl.BlockSpec(memory_space=pltpu.VMEM)
    return pl.pallas_call(
        functools.partial(grads_kernel, units, owners, loss_scale),
        out_shape=jax.ShapeDtypeStruct((copies, 2, 2, TILE, TILE), jnp.bfloat16),
        in_specs=[smem, smem, vmem, pl.BlockSpec(memory_space=pl.ANY)],
        out_specs=vmem,
        scratch_shapes=[
            pltpu.VMEM((2, 2, TILE, TILE), jnp.bfloat16),
            pltpu.VMEM((2 * TILE, TILE), jnp.float32),
            pltpu.VMEM((TILE, 2 * TILE), jnp.float32),
            pltpu.SemaphoreType.DMA((2,)),
        ],
        cost_estimate=pl.CostEstimate(
            flops=20 * sources * rows * TILE * TILE,
            bytes_accessed=4 * sources * rows * TILE,
            transcendentals=2 * sources * rows * TILE,
        ),
    )(order, flags, blocks, weights)


def place_kernel(live, order_ref, counts_ref, same_ref, other_ref, out_ref, sems):
    owner = lax.axis_index("fsdp")
    per_owner = out_ref.shape[0]
    for slot in range(per_owner):

        @pl.when(counts_ref[0, 0, owner] <= slot)
        def _():
            out_ref[slot] = jnp.zeros(out_ref.shape[1:], out_ref.dtype)

    def each(act):
        for i in range(live):
            at = order_ref[i] - owner * per_owner
            mine = (at >= 0) & (at < per_owner)
            near = owner % 2 == i // 2 % 2
            for grads_ref, where in ((same_ref, near), (other_ref, jnp.logical_not(near))):

                @pl.when(mine & where)
                def _():
                    act(
                        pltpu.make_async_copy(
                            grads_ref.at[i // 4, i % 2], out_ref.at[at], sems.at[i]
                        )
                    )

    each(lambda copy: copy.start())
    each(lambda copy: copy.wait())


def place(same, other, order, counts, live, per_owner):
    smem = pl.BlockSpec(memory_space=pltpu.SMEM)
    hbm = pl.BlockSpec(memory_space=pl.ANY)
    return pl.pallas_call(
        functools.partial(place_kernel, live),
        out_shape=jax.ShapeDtypeStruct((per_owner,) + same.shape[2:], same.dtype),
        in_specs=[smem, smem, hbm, hbm],
        out_specs=pl.BlockSpec(memory_space=pltpu.VMEM),
        scratch_shapes=[pltpu.SemaphoreType.DMA((live,))],
        cost_estimate=pl.CostEstimate(flops=0, bytes_accessed=1_000_000, transcendentals=0),
    )(order, counts, same, other)


def body(x_down, x_up, w_tiles, tile_rows, tile_cols, counts):
    rows_here = x_down.shape[2]
    slots, owners = tile_cols.shape[2], counts.shape[2]
    live = live_total(slots, owners)
    places = lax.axis_size("dp") * lax.axis_size("fsdp")
    sections = lax.axis_size("section")
    halfway = sections // 2
    loss_scale = float(2 * rows_here * places) ** (-0.5)

    packed, own_w, order, flags = pack(
        x_down, x_up, w_tiles, tile_rows, tile_cols, counts, live, places, halfway
    )
    weights = gather_all(own_w, "fsdp")
    groups = [
        [(s + side * halfway) * places + place for side in range(2) for place in range(places)]
        for s in range(halfway)
    ]
    blocks = lax.all_to_all(
        packed, ("section",) + PLANE, split_axis=0, concat_axis=0,
        axis_index_groups=groups, tiled=True,
    )
    copies = places // 2
    mine = unit_grads(blocks, weights, order, flags, live // 2, owners, copies, loss_scale)
    same_core = [[place for place in range(places) if place % 2 == core] for core in range(2)]
    same = lax.all_to_all(
        mine, PLANE, split_axis=0, concat_axis=0, axis_index_groups=same_core, tiled=True
    )
    other = lax.ppermute(same, "fsdp", [(i, i ^ 1) for i in range(owners)])
    return place(same, other, order, counts, live, slots // owners)[None]


def solution(mesh):
    in_specs = (
        P("section", "dp", "fsdp", None),
        P("section", "dp", "fsdp", None),
        P("section", None, "fsdp", None, None, None),
        P("section", None, None),
        P("section", None, None),
        P("section", None, None),
    )
    out_specs = P("section", "fsdp", None, None, None)
    return jax.shard_map(body, mesh=mesh, in_specs=in_specs, out_specs=out_specs, check_vma=False)
```

```python
import functools
import math

import jax
import jax.numpy as jnp
from jax import lax
from jax.experimental import pallas as pl
from jax.experimental.pallas import tpu as pltpu
from jax.sharding import PartitionSpec as P

TILE = 128
PLANE = ("dp", "fsdp")
SOURCES_AT_ONCE = 4
COLUMNS = 192
IN_VMEM = pltpu.CompilerParams(vmem_limit_bytes=16 * 1024 * 1024)

tanh_scale = math.sqrt(2.0 / math.pi)
cubic_coef = 0.044715


def gelu_pair(hidden):
    square = hidden * hidden
    tangent = jnp.tanh(tanh_scale * (hidden + cubic_coef * hidden * square))
    half = 0.5 * (1.0 + tangent)
    value = hidden * half
    slope = half + 0.5 * hidden * (1.0 - tangent * tangent) * tanh_scale * (
        1.0 + 3.0 * cubic_coef * square
    )
    return (value, slope)


def live_total(slots, owners):
    cap = slots // owners
    return sum(cap - i * cap // owners for i in range(owners))


def order_slots(cols_ref, counts_ref, which, slots, live, order_ref, flags_ref, first_ref, last_ref):
    per_owner = slots // counts_ref.shape[2]
    cols = []
    for s in range(slots):
        living = counts_ref[0, which, s // per_owner] > s % per_owner
        cols.append(jnp.where(living, cols_ref[0, which, s], COLUMNS))
    for s in range(slots):
        last_ref[cols[s]] = s
        first_ref[cols[slots - 1 - s]] = slots - 1 - s
    ahead, alone = jnp.int32(0), []
    for s in range(slots):
        living = cols[s] < COLUMNS
        first, last = first_ref[cols[s]], last_ref[cols[s]]
        leads = living & (first == s) & (last > s)
        alone.append(living & (first == last))
        at = jnp.where(leads, ahead, live)
        order_ref[at] = s
        order_ref[at + 1] = last
        flags_ref[at] = 1
        ahead = ahead + jnp.where(leads, 2, 0)
    for s in range(slots):
        at = jnp.where(alone[s], ahead, live)
        order_ref[at] = s
        flags_ref[at] = 0
        ahead = ahead + jnp.where(alone[s], 1, 0)
    order_ref[live] = 0
    order_ref[live + 1] = 0


def pack_kernel(
    live, halfway, rows_ref, cols_ref, counts_ref, down_ref, up_ref, w_ref,
    out_ref, own_w_ref, order_ref, flags_ref,
    up_order_ref, up_flags_ref, first_ref, last_ref, sems, w_sem,
):
    slots = cols_ref.shape[2]
    places = out_ref.shape[0] // 2
    weights = pltpu.make_async_copy(w_ref.at[0, 0], own_w_ref, w_sem)
    weights.start()
    behind = jnp.where(lax.axis_index("section") < halfway, 0, places)
    copies = []
    for which, x_ref, order, flags, base in (
        (1, up_ref, up_order_ref, up_flags_ref, places - behind),
        (0, down_ref, order_ref, flags_ref, behind),
    ):
        order_slots(
            cols_ref, counts_ref, which, slots, live, order, flags, first_ref, last_ref
        )
        for i in range(live):
            at = pl.multiple_of(rows_ref[0, which, order[i]] * TILE, TILE)
            copy = pltpu.make_async_copy(
                x_ref.at[0, 0, :, pl.ds(at, TILE)],
                out_ref.at[base + i // 2, i % 2],
                sems.at[len(copies)],
            )
            copy.start()
            copies.append(copy)
    for place in range(live // 2, places):
        out_ref[place] = jnp.zeros(out_ref.shape[1:], out_ref.dtype)
        out_ref[places + place] = jnp.zeros(out_ref.shape[1:], out_ref.dtype)
    for copy in copies:
        copy.wait()
    weights.wait()


def pack(x_down, x_up, w_tiles, tile_rows, tile_cols, counts, live, places, halfway):
    rows = x_down.shape[2]
    smem = pl.BlockSpec(memory_space=pltpu.SMEM)
    vmem = pl.BlockSpec(memory_space=pltpu.VMEM)
    hbm = pl.BlockSpec(memory_space=pl.ANY)
    return pl.pallas_call(
        functools.partial(pack_kernel, live, halfway),
        out_shape=[
            jax.ShapeDtypeStruct((2 * places, 2, rows, TILE), x_down.dtype),
            jax.ShapeDtypeStruct(w_tiles.shape[2:], w_tiles.dtype),
            jax.ShapeDtypeStruct((live + 2,), jnp.int32),
            jax.ShapeDtypeStruct((live + 2,), jnp.int32),
        ],
        in_specs=[smem, smem, smem, hbm, hbm, hbm],
        out_specs=[vmem, vmem, smem, smem],
        scratch_shapes=[
            pltpu.SMEM((live + 2,), jnp.int32),
            pltpu.SMEM((live + 2,), jnp.int32),
            pltpu.SMEM((COLUMNS + 1,), jnp.int32),
            pltpu.SMEM((COLUMNS + 1,), jnp.int32),
            pltpu.SemaphoreType.DMA((2 * live,)),
            pltpu.SemaphoreType.DMA,
        ],
        cost_estimate=pl.CostEstimate(
            flops=0, bytes_accessed=8 * live * rows * TILE, transcendentals=0
        ),
    )(tile_rows, tile_cols, counts, x_down, x_up, w_tiles)


def gather_all(array, axis):
    size = lax.axis_size(axis)
    far = size // 2
    while far:
        partner = lax.ppermute(array, axis, [(i, i ^ far) for i in range(size)])
        array = jnp.concatenate([array, partner], axis=0)
        far //= 2
    return array


def gather_place(size, owner, me):
    apart, far, weight, at = owner ^ me, size // 2, 1, 0
    while far:
        at = at + jnp.where((apart & far) != 0, weight, 0)
        far, weight = far // 2, weight * 2
    return at


def dot(a, b, over_a, over_b):
    return lax.dot_general(
        a, b, (((over_a,), (over_b,)), ((), ())), preferred_element_type=jnp.float32
    )


def grads_kernel(
    units, owners, loss_scale, order_ref, flags_ref, x_ref, w_ref, out_ref,
    w_own, first_sum, second_sum, sems,
):
    sources, _, rows, _ = x_ref.shape
    per_owner = w_ref.shape[0] // owners
    unit = jnp.minimum(lax.axis_index(PLANE), units - 1)
    me = lax.axis_index("fsdp")
    copies = []
    for i in range(2):
        slot = order_ref[2 * unit + i]
        owner = slot // per_owner
        at = gather_place(owners, owner, me) * per_owner + slot - owner * per_owner
        copies.append(pltpu.make_async_copy(w_ref.at[at], w_own.at[i], sems.at[i]))
    for copy in copies:
        copy.start()
    first_sum[...] = jnp.zeros_like(first_sum)
    second_sum[...] = jnp.zeros_like(second_sum)
    for copy in copies:
        copy.wait()
    together = min(SOURCES_AT_ONCE, sources)
    steps = sources // together
    coupled = flags_ref[2 * unit] == 1

    def read(step):
        at = step * together
        return [
            x_ref[pl.ds(at, together), i].reshape(together * rows, TILE) for i in range(2)
        ]

    @pl.when(coupled)
    def _():
        def go(step, carry):
            xs = jnp.concatenate(read(step), axis=1)
            firsts = jnp.concatenate([w_own[0, 0], w_own[1, 0]], axis=0)
            seconds = jnp.concatenate([w_own[0, 1], w_own[1, 1]], axis=1)
            value, slope = gelu_pair(dot(xs, firsts, 1, 0))
            active = value.astype(jnp.bfloat16)
            delta = dot(active, seconds, 1, 0)
            cotangent = (loss_scale * (xs.astype(jnp.float32) + delta)).astype(jnp.bfloat16)
            grad_act = dot(cotangent, seconds, 1, 1)
            grad_pre = (grad_act * slope).astype(jnp.bfloat16)
            first_sum[...] += dot(xs, grad_pre, 0, 0)
            second_sum[...] += dot(active, cotangent, 0, 0)
            return carry

        lax.fori_loop(0, steps, go, 0, unroll=min(steps, 4))

    @pl.when(jnp.logical_not(coupled))
    def _():
        def go(step, carry):
            for i, x in enumerate(read(step)):
                across = slice(i * TILE, (i + 1) * TILE)
                value, slope = gelu_pair(dot(x, w_own[i, 0], 1, 0))
                active = value.astype(jnp.bfloat16)
                delta = dot(active, w_own[i, 1], 1, 0)
                cotangent = (loss_scale * (x.astype(jnp.float32) + delta)).astype(jnp.bfloat16)
                grad_act = dot(cotangent, w_own[i, 1], 1, 1)
                grad_pre = (grad_act * slope).astype(jnp.bfloat16)
                first_sum[across, :] += dot(x, grad_pre, 0, 0)
                second_sum[:, across] += dot(active, cotangent, 0, 0)
            return carry

        lax.fori_loop(0, steps, go, 0, unroll=min(steps, 4))

    for i in range(2):
        across = slice(i * TILE, (i + 1) * TILE)
        for copy in range(out_ref.shape[0]):
            out_ref[copy, i, 0] = first_sum[across, :].astype(out_ref.dtype)
            out_ref[copy, i, 1] = second_sum[:, across].astype(out_ref.dtype)


def unit_grads(blocks, weights, order, flags, units, owners, copies, loss_scale):
    sources, _, rows, _ = blocks.shape
    smem = pl.BlockSpec(memory_space=pltpu.SMEM)
    vmem = pl.BlockSpec(memory_space=pltpu.VMEM)
    return pl.pallas_call(
        functools.partial(grads_kernel, units, owners, loss_scale),
        out_shape=jax.ShapeDtypeStruct((copies, 2, 2, TILE, TILE), jnp.bfloat16),
        in_specs=[smem, smem, vmem, pl.BlockSpec(memory_space=pl.ANY)],
        out_specs=vmem,
        scratch_shapes=[
            pltpu.VMEM((2, 2, TILE, TILE), jnp.bfloat16),
            pltpu.VMEM((2 * TILE, TILE), jnp.float32),
            pltpu.VMEM((TILE, 2 * TILE), jnp.float32),
            pltpu.SemaphoreType.DMA((2,)),
        ],
        compiler_params=IN_VMEM,
        cost_estimate=pl.CostEstimate(
            flops=20 * sources * rows * TILE * TILE,
            bytes_accessed=4 * sources * rows * TILE,
            transcendentals=2 * sources * rows * TILE,
        ),
    )(order, flags, blocks, weights)


def place_kernel(live, order_ref, counts_ref, same_ref, other_ref, out_ref, sems):
    owner = lax.axis_index("fsdp")
    per_owner = out_ref.shape[0]
    for slot in range(per_owner):

        @pl.when(counts_ref[0, 0, owner] <= slot)
        def _():
            out_ref[slot] = jnp.zeros(out_ref.shape[1:], out_ref.dtype)

    def each(act):
        for i in range(live):
            at = order_ref[i] - owner * per_owner
            mine = (at >= 0) & (at < per_owner)
            near = owner % 2 == i // 2 % 2
            for grads_ref, where in ((same_ref, near), (other_ref, jnp.logical_not(near))):

                @pl.when(mine & where)
                def _():
                    act(
                        pltpu.make_async_copy(
                            grads_ref.at[i // 4, i % 2], out_ref.at[at], sems.at[i]
                        )
                    )

    each(lambda copy: copy.start())
    each(lambda copy: copy.wait())


def place(same, other, order, counts, live, per_owner):
    smem = pl.BlockSpec(memory_space=pltpu.SMEM)
    hbm = pl.BlockSpec(memory_space=pl.ANY)
    return pl.pallas_call(
        functools.partial(place_kernel, live),
        out_shape=jax.ShapeDtypeStruct((per_owner,) + same.shape[2:], same.dtype),
        in_specs=[smem, smem, hbm, hbm],
        out_specs=pl.BlockSpec(memory_space=pltpu.VMEM),
        scratch_shapes=[pltpu.SemaphoreType.DMA((live,))],
        compiler_params=IN_VMEM,
        cost_estimate=pl.CostEstimate(flops=0, bytes_accessed=1_000_000, transcendentals=0),
    )(order, counts, same, other)


def body(x_down, x_up, w_tiles, tile_rows, tile_cols, counts):
    rows_here = x_down.shape[2]
    slots, owners = tile_cols.shape[2], counts.shape[2]
    live = live_total(slots, owners)
    places = lax.axis_size("dp") * lax.axis_size("fsdp")
    sections = lax.axis_size("section")
    halfway = sections // 2
    loss_scale = float(2 * rows_here * places) ** (-0.5)

    packed, own_w, order, flags = pack(
        x_down, x_up, w_tiles, tile_rows, tile_cols, counts, live, places, halfway
    )
    weights = gather_all(own_w, "fsdp")
    groups = [
        [(s + side * halfway) * places + place for side in range(2) for place in range(places)]
        for s in range(halfway)
    ]
    blocks = lax.all_to_all(
        packed, ("section",) + PLANE, split_axis=0, concat_axis=0,
        axis_index_groups=groups, tiled=True,
    )
    copies = places // 2
    mine = unit_grads(blocks, weights, order, flags, live // 2, owners, copies, loss_scale)
    same_core = [[place for place in range(places) if place % 2 == core] for core in range(2)]
    same = lax.all_to_all(
        mine, PLANE, split_axis=0, concat_axis=0, axis_index_groups=same_core, tiled=True
    )
    other = lax.ppermute(same, "fsdp", [(i, i ^ 1) for i in range(owners)])
    return place(same, other, order, counts, live, slots // owners)[None]


def solution(mesh):
    in_specs = (
        P("section", "dp", "fsdp", None),
        P("section", "dp", "fsdp", None),
        P("section", None, "fsdp", None, None, None),
        P("section", None, None),
        P("section", None, None),
        P("section", None, None),
    )
    out_specs = P("section", "fsdp", None, None, None)
    return jax.shard_map(body, mesh=mesh, in_specs=in_specs, out_specs=out_specs, check_vma=False)
```

```python
import functools
import math

import jax
import jax.numpy as jnp
from jax import lax
from jax.experimental import pallas as pl
from jax.experimental.pallas import tpu as pltpu
from jax.sharding import PartitionSpec as P

TILE = 128
PLANE = ("dp", "fsdp")
SOURCES_AT_ONCE = 4
COLUMNS = 192
CORES = 2
IN_VMEM = pltpu.CompilerParams(vmem_limit_bytes=16 * 1024 * 1024)

tanh_scale = math.sqrt(2.0 / math.pi)
cubic_coef = 0.044715


def gelu_pair(hidden):
    square = hidden * hidden
    tangent = jnp.tanh(tanh_scale * (hidden + cubic_coef * hidden * square))
    half = 0.5 * (1.0 + tangent)
    value = hidden * half
    slope = half + 0.5 * hidden * (1.0 - tangent * tangent) * tanh_scale * (
        1.0 + 3.0 * cubic_coef * square
    )
    return (value, slope)


def live_total(slots, owners):
    cap = slots // owners
    return sum(cap - i * cap // owners for i in range(owners))


def unit_place(unit, per_half, owners):
    half, at = unit // per_half, unit % per_half
    return at // CORES * owners + half * CORES + at % CORES


def unit_here(per_half, owners):
    owner = lax.axis_index("fsdp")
    at = lax.axis_index("dp") * CORES + owner % CORES
    return owner // CORES * per_half + jnp.minimum(at, per_half - 1)


def order_units(
    cols_ref, counts_ref, which, slots, per_half, order_ref, flags_ref, first_ref, last_ref
):
    per_owner, middle, unused = slots // counts_ref.shape[2], slots // 2, 4 * per_half
    for i in range(order_ref.shape[0]):
        order_ref[i] = -1
        flags_ref[i] = 0
    cols = []
    for s in range(slots):
        living = counts_ref[0, which, s // per_owner] > s % per_owner
        cols.append(jnp.where(living, cols_ref[0, which, s], COLUMNS))
    for s in range(slots):
        last_ref[cols[s]] = s
        first_ref[cols[slots - 1 - s]] = slots - 1 - s
    filled = [jnp.int32(0), jnp.int32(0)]

    def put(unit, slot_a, slot_b, coupled, really):
        at = jnp.where(really, 2 * unit, unused)
        order_ref[at] = slot_a
        order_ref[at + 1] = slot_b
        flags_ref[at] = coupled

    count = lambda condition: jnp.where(condition, 1, 0)
    alone, mixed = [], []
    for s in range(slots):
        living = cols[s] < COLUMNS
        first, last = first_ref[cols[s]], last_ref[cols[s]]
        leads = living & (first == s) & (last > s)
        alone.append(living & (first == last))
        half = s // middle
        pure = leads & (last < (half + 1) * middle)
        put(half * per_half + filled[half], s, last, 1, pure)
        filled[half] = filled[half] + count(pure)
        if half == 0:
            mixed.append((s, last, 1, leads & (last >= middle)))
    waiting, odd = [jnp.int32(0), jnp.int32(0)], [jnp.int32(0), jnp.int32(0)]
    for s in range(slots):
        half = s // middle
        second = alone[s] & (odd[half] == 1)
        put(half * per_half + filled[half], waiting[half], s, 0, second)
        filled[half] = filled[half] + count(second)
        odd[half] = jnp.where(alone[s], 1 - odd[half], odd[half])
        waiting[half] = jnp.where(alone[s], s, waiting[half])
    mixed.append((waiting[0], waiting[1], 0, odd[0] == 1))
    for low, high, coupled, really in mixed:
        room = filled[0] < per_half
        unit = jnp.where(room, filled[0], per_half + filled[1])
        put(unit, jnp.where(room, low, high), jnp.where(room, high, low), coupled, really)
        filled[0] = filled[0] + count(really & room)
        filled[1] = filled[1] + count(really & jnp.logical_not(room))


def pack_kernel(
    per_half, halfway, rows_ref, cols_ref, counts_ref, down_ref, up_ref, w_ref,
    out_ref, own_w_ref, far_w_ref, order_ref, flags_ref,
    up_order_ref, up_flags_ref, first_ref, last_ref, sems, w_sems,
):
    slots, owners = cols_ref.shape[2], counts_ref.shape[2]
    per_owner, places, units = slots // owners, out_ref.shape[0] // 2, 2 * per_half
    behind = jnp.where(lax.axis_index("section") < halfway, 0, places)
    copies = [pltpu.make_async_copy(w_ref.at[0, 0], own_w_ref, w_sems.at[CORES])]
    copies[0].start()
    used = [unit_place(unit, per_half, owners) for unit in range(units)]
    for which, x_ref, order, flags, base in (
        (1, up_ref, up_order_ref, up_flags_ref, places - behind),
        (0, down_ref, order_ref, flags_ref, behind),
    ):
        order_units(
            cols_ref, counts_ref, which, slots, per_half, order, flags, first_ref, last_ref
        )
        for i in range(2 * units):
            row = rows_ref[0, which, jnp.maximum(order[i], 0)]
            at = pl.multiple_of(row * TILE, TILE)
            copy = pltpu.make_async_copy(
                x_ref.at[0, 0, :, pl.ds(at, TILE)],
                out_ref.at[base + used[i // 2], i % 2],
                sems.at[2 * units * which + i],
            )
            copy.start()
            copies.append(copy)
    owner = lax.axis_index("fsdp")
    for core in range(CORES):
        at = jnp.minimum(lax.axis_index("dp") * CORES + core, per_half - 1)
        asker = (1 - owner // CORES) * per_half + at
        held = order_ref[2 * asker + 1] - owner * per_owner
        held = jnp.where((held >= 0) & (held < per_owner), held, 0)
        copy = pltpu.make_async_copy(w_ref.at[0, 0, held], far_w_ref.at[core], w_sems.at[core])
        copy.start()
        copies.append(copy)
    for place in range(places):
        if place not in used:
            out_ref[place] = jnp.zeros(out_ref.shape[1:], out_ref.dtype)
            out_ref[places + place] = jnp.zeros(out_ref.shape[1:], out_ref.dtype)
    for copy in copies:
        copy.wait()


def pack(x_down, x_up, w_tiles, tile_rows, tile_cols, counts, per_half, places, halfway):
    rows, units = x_down.shape[2], 2 * per_half
    smem = pl.BlockSpec(memory_space=pltpu.SMEM)
    vmem = pl.BlockSpec(memory_space=pltpu.VMEM)
    hbm = pl.BlockSpec(memory_space=pl.ANY)
    return pl.pallas_call(
        functools.partial(pack_kernel, per_half, halfway),
        out_shape=[
            jax.ShapeDtypeStruct((2 * places, 2, rows, TILE), x_down.dtype),
            jax.ShapeDtypeStruct(w_tiles.shape[2:], w_tiles.dtype),
            jax.ShapeDtypeStruct((CORES,) + w_tiles.shape[3:], w_tiles.dtype),
            jax.ShapeDtypeStruct((2 * units + 2,), jnp.int32),
            jax.ShapeDtypeStruct((2 * units + 2,), jnp.int32),
        ],
        in_specs=[smem, smem, smem, hbm, hbm, hbm],
        out_specs=[vmem, vmem, vmem, smem, smem],
        scratch_shapes=[
            pltpu.SMEM((2 * units + 2,), jnp.int32),
            pltpu.SMEM((2 * units + 2,), jnp.int32),
            pltpu.SMEM((COLUMNS + 1,), jnp.int32),
            pltpu.SMEM((COLUMNS + 1,), jnp.int32),
            pltpu.SemaphoreType.DMA((4 * units,)),
            pltpu.SemaphoreType.DMA((CORES + 1,)),
        ],
        cost_estimate=pl.CostEstimate(
            flops=0, bytes_accessed=16 * units * rows * TILE, transcendentals=0
        ),
    )(tile_rows, tile_cols, counts, x_down, x_up, w_tiles)


def swapped(array, apart):
    size = lax.axis_size("fsdp")
    return lax.ppermute(array, "fsdp", [(i, i ^ apart) for i in range(size)])


def share_weights(own_w, far_w):
    both = jnp.concatenate([own_w, swapped(far_w, CORES)], axis=0)
    return jnp.concatenate([both, swapped(both, 1)], axis=0)


def weights_at(slot, per_owner):
    me, owner = lax.axis_index("fsdp"), slot // per_owner
    here = jnp.where(owner // CORES == me // CORES, slot - owner * per_owner, per_owner + me % CORES)
    return here + jnp.where(owner % CORES == me % CORES, 0, per_owner + CORES)


def dot(a, b, over_a, over_b):
    return lax.dot_general(
        a, b, (((over_a,), (over_b,)), ((), ())), preferred_element_type=jnp.float32
    )


def grads_kernel(
    per_half, owners, loss_scale, order_ref, flags_ref, x_ref, w_ref, out_ref,
    first_sum, second_sum,
):
    sources, _, rows, _ = x_ref.shape
    per_owner = w_ref.shape[0] // 2 - CORES
    unit = unit_here(per_half, owners)
    ats = [weights_at(jnp.maximum(order_ref[2 * unit + i], 0), per_owner) for i in range(2)]
    w_own = lambda i, k: w_ref[ats[i], k]
    first_sum[...] = jnp.zeros_like(first_sum)
    second_sum[...] = jnp.zeros_like(second_sum)
    together = min(SOURCES_AT_ONCE, sources)
    steps = sources // together
    coupled = flags_ref[2 * unit] == 1

    def read(step):
        at = step * together
        return [
            x_ref[pl.ds(at, together), i].reshape(together * rows, TILE) for i in range(2)
        ]

    @pl.when(coupled)
    def _():
        def go(step, carry):
            xs = jnp.concatenate(read(step), axis=1)
            firsts = jnp.concatenate([w_own(0, 0), w_own(1, 0)], axis=0)
            seconds = jnp.concatenate([w_own(0, 1), w_own(1, 1)], axis=1)
            value, slope = gelu_pair(dot(xs, firsts, 1, 0))
            active = value.astype(jnp.bfloat16)
            delta = dot(active, seconds, 1, 0)
            cotangent = (loss_scale * (xs.astype(jnp.float32) + delta)).astype(jnp.bfloat16)
            grad_act = dot(cotangent, seconds, 1, 1)
            grad_pre = (grad_act * slope).astype(jnp.bfloat16)
            first_sum[...] += dot(xs, grad_pre, 0, 0)
            second_sum[...] += dot(active, cotangent, 0, 0)
            return carry

        lax.fori_loop(0, steps, go, 0, unroll=min(steps, 4))

    @pl.when(jnp.logical_not(coupled))
    def _():
        def go(step, carry):
            for i, x in enumerate(read(step)):
                across = slice(i * TILE, (i + 1) * TILE)
                value, slope = gelu_pair(dot(x, w_own(i, 0), 1, 0))
                active = value.astype(jnp.bfloat16)
                delta = dot(active, w_own(i, 1), 1, 0)
                cotangent = (loss_scale * (x.astype(jnp.float32) + delta)).astype(jnp.bfloat16)
                grad_act = dot(cotangent, w_own(i, 1), 1, 1)
                grad_pre = (grad_act * slope).astype(jnp.bfloat16)
                first_sum[across, :] += dot(x, grad_pre, 0, 0)
                second_sum[:, across] += dot(active, cotangent, 0, 0)
            return carry

        lax.fori_loop(0, steps, go, 0, unroll=min(steps, 4))

    for i in range(2):
        across = slice(i * TILE, (i + 1) * TILE)
        for copy in range(out_ref.shape[0]):
            out_ref[copy, i, 0] = first_sum[across, :].astype(out_ref.dtype)
            out_ref[copy, i, 1] = second_sum[:, across].astype(out_ref.dtype)


def unit_grads(blocks, weights, order, flags, per_half, owners, copies, loss_scale):
    sources, _, rows, _ = blocks.shape
    smem = pl.BlockSpec(memory_space=pltpu.SMEM)
    vmem = pl.BlockSpec(memory_space=pltpu.VMEM)
    return pl.pallas_call(
        functools.partial(grads_kernel, per_half, owners, loss_scale),
        out_shape=jax.ShapeDtypeStruct((copies, 2, 2, TILE, TILE), jnp.bfloat16),
        in_specs=[smem, smem, vmem, vmem],
        out_specs=vmem,
        scratch_shapes=[
            pltpu.VMEM((2 * TILE, TILE), jnp.float32),
            pltpu.VMEM((TILE, 2 * TILE), jnp.float32),
        ],
        compiler_params=IN_VMEM,
        cost_estimate=pl.CostEstimate(
            flops=20 * sources * rows * TILE * TILE,
            bytes_accessed=4 * sources * rows * TILE,
            transcendentals=2 * sources * rows * TILE,
        ),
    )(order, flags, blocks, weights)


def place_kernel(per_half, order_ref, counts_ref, same_ref, other_ref, out_ref, zeros, sems, zero_sems):
    owner, owners = lax.axis_index("fsdp"), counts_ref.shape[2]
    per_owner = out_ref.shape[0]
    zeros[...] = jnp.zeros_like(zeros)

    def each(act):
        for i in range(4 * per_half):
            at = order_ref[i] - owner * per_owner
            mine = (at >= 0) & (at < per_owner)
            place = unit_place(i // 2, per_half, owners)
            near = owner % CORES == place % CORES
            for grads_ref, where in ((same_ref, near), (other_ref, jnp.logical_not(near))):

                @pl.when(mine & where)
                def _():
                    act(
                        pltpu.make_async_copy(
                            grads_ref.at[place // CORES, i % 2], out_ref.at[at], sems.at[i]
                        )
                    )

        for slot in range(per_owner):

            @pl.when(counts_ref[0, 0, owner] <= slot)
            def _():
                act(pltpu.make_async_copy(zeros, out_ref.at[slot], zero_sems.at[slot]))

    each(lambda copy: copy.start())
    each(lambda copy: copy.wait())


def place(same, other, order, counts, per_half, per_owner):
    smem = pl.BlockSpec(memory_space=pltpu.SMEM)
    hbm = pl.BlockSpec(memory_space=pl.ANY)
    return pl.pallas_call(
        functools.partial(place_kernel, per_half),
        out_shape=jax.ShapeDtypeStruct((per_owner,) + same.shape[2:], same.dtype),
        in_specs=[smem, smem, hbm, hbm],
        out_specs=hbm,
        scratch_shapes=[
            pltpu.VMEM(same.shape[2:], same.dtype),
            pltpu.SemaphoreType.DMA((4 * per_half,)),
            pltpu.SemaphoreType.DMA((per_owner,)),
        ],
        compiler_params=IN_VMEM,
        cost_estimate=pl.CostEstimate(flops=0, bytes_accessed=1_000_000, transcendentals=0),
    )(order, counts, same, other)


def body(x_down, x_up, w_tiles, tile_rows, tile_cols, counts):
    rows_here = x_down.shape[2]
    slots, owners = tile_cols.shape[2], counts.shape[2]
    per_half = (live_total(slots, owners) // 2 + 1) // 2
    places = lax.axis_size("dp") * lax.axis_size("fsdp")
    sections = lax.axis_size("section")
    halfway = sections // 2
    loss_scale = float(2 * rows_here * places) ** (-0.5)

    packed, own_w, far_w, order, flags = pack(
        x_down, x_up, w_tiles, tile_rows, tile_cols, counts, per_half, places, halfway
    )
    groups = [
        [(s + side * halfway) * places + place for side in range(2) for place in range(places)]
        for s in range(halfway)
    ]
    blocks = lax.all_to_all(
        packed, ("section",) + PLANE, split_axis=0, concat_axis=0,
        axis_index_groups=groups, tiled=True,
    )
    weights = share_weights(own_w, far_w)
    copies = places // CORES
    mine = unit_grads(blocks, weights, order, flags, per_half, owners, copies, loss_scale)
    same_core = [
        [place for place in range(places) if place % CORES == core] for core in range(CORES)
    ]
    same = lax.all_to_all(
        mine, PLANE, split_axis=0, concat_axis=0, axis_index_groups=same_core, tiled=True
    )
    other = swapped(same, 1)
    return place(same, other, order, counts, per_half, slots // owners)[None]


def solution(mesh):
    in_specs = (
        P("section", "dp", "fsdp", None),
        P("section", "dp", "fsdp", None),
        P("section", None, "fsdp", None, None, None),
        P("section", None, None),
        P("section", None, None),
        P("section", None, None),
    )
    out_specs = P("section", "fsdp", None, None, None)
    return jax.shard_map(body, mesh=mesh, in_specs=in_specs, out_specs=out_specs, check_vma=False)
```

```python
import functools
import math

import jax
import jax.numpy as jnp
from jax import lax
from jax.experimental import pallas as pl
from jax.experimental.pallas import tpu as pltpu
from jax.sharding import PartitionSpec as P

TILE = 128
PLANE = ("dp", "fsdp")
SOURCES_AT_ONCE = 4
COLUMNS = 192
CORES = 2
IN_VMEM = pltpu.CompilerParams(vmem_limit_bytes=16 * 1024 * 1024)

tanh_scale = math.sqrt(2.0 / math.pi)
cubic_coef = 0.044715


def gelu_pair(hidden):
    square = hidden * hidden
    tangent = jnp.tanh(tanh_scale * (hidden + cubic_coef * hidden * square))
    half = 0.5 * (1.0 + tangent)
    value = hidden * half
    slope = half + 0.5 * hidden * (1.0 - tangent * tangent) * tanh_scale * (
        1.0 + 3.0 * cubic_coef * square
    )
    return (value, slope)


def live_total(slots, owners):
    cap = slots // owners
    return sum(cap - i * cap // owners for i in range(owners))


def unit_place(unit, per_half, owners):
    half, at = unit // per_half, unit % per_half
    return at // CORES * owners + half * CORES + at % CORES


def unit_here(per_half, owners):
    owner = lax.axis_index("fsdp")
    at = lax.axis_index("dp") * CORES + owner % CORES
    return owner // CORES * per_half + jnp.minimum(at, per_half - 1)


def order_units(
    cols_ref, counts_ref, which, slots, per_half, order_ref, flags_ref, first_ref, last_ref
):
    per_owner, middle, unused = slots // counts_ref.shape[2], slots // 2, 4 * per_half
    for i in range(order_ref.shape[1]):
        order_ref[which, i] = -1
        flags_ref[which, i] = 0
    cols = []
    for s in range(slots):
        living = counts_ref[0, which, s // per_owner] > s % per_owner
        cols.append(jnp.where(living, cols_ref[0, which, s], COLUMNS))
    for s in range(slots):
        last_ref[cols[s]] = s
        first_ref[cols[slots - 1 - s]] = slots - 1 - s
    filled = [jnp.int32(0), jnp.int32(0)]

    def put(unit, slot_a, slot_b, coupled, really):
        at = jnp.where(really, 2 * unit, unused)
        order_ref[which, at] = slot_a
        order_ref[which, at + 1] = slot_b
        flags_ref[which, at] = coupled

    count = lambda condition: jnp.where(condition, 1, 0)
    alone, mixed = [], []
    for s in range(slots):
        living = cols[s] < COLUMNS
        first, last = first_ref[cols[s]], last_ref[cols[s]]
        leads = living & (first == s) & (last > s)
        alone.append(living & (first == last))
        half = s // middle
        pure = leads & (last < (half + 1) * middle)
        put(half * per_half + filled[half], s, last, 1, pure)
        filled[half] = filled[half] + count(pure)
        if half == 0:
            mixed.append((s, last, 1, leads & (last >= middle)))
    waiting, odd = [jnp.int32(0), jnp.int32(0)], [jnp.int32(0), jnp.int32(0)]
    for s in range(slots):
        half = s // middle
        second = alone[s] & (odd[half] == 1)
        put(half * per_half + filled[half], waiting[half], s, 0, second)
        filled[half] = filled[half] + count(second)
        odd[half] = jnp.where(alone[s], 1 - odd[half], odd[half])
        waiting[half] = jnp.where(alone[s], s, waiting[half])
    mixed.append((waiting[0], waiting[1], 0, odd[0] == 1))
    for low, high, coupled, really in mixed:
        room = filled[0] < per_half
        unit = jnp.where(room, filled[0], per_half + filled[1])
        put(unit, jnp.where(room, low, high), jnp.where(room, high, low), coupled, really)
        filled[0] = filled[0] + count(really & room)
        filled[1] = filled[1] + count(really & jnp.logical_not(room))


def pack_kernel(
    per_half, rows_ref, cols_ref, counts_ref, down_ref, up_ref, w_ref,
    out_ref, own_w_ref, order_ref, flags_ref, first_ref, last_ref, sems, w_sem,
):
    slots, owners = cols_ref.shape[2], counts_ref.shape[2]
    places, units = out_ref.shape[0], 2 * per_half
    copies = [pltpu.make_async_copy(w_ref.at[0], own_w_ref, w_sem)]
    copies[0].start()
    used = [unit_place(unit, per_half, owners) for unit in range(units)]
    for which, x_ref in ((1, up_ref), (0, down_ref)):
        order_units(
            cols_ref, counts_ref, which, slots, per_half, order_ref, flags_ref, first_ref, last_ref
        )
        for i in range(2 * units):
            row = rows_ref[0, which, jnp.maximum(order_ref[which, i], 0)]
            at = pl.multiple_of(row * TILE, TILE)
            copy = pltpu.make_async_copy(
                x_ref.at[0, 0, :, pl.ds(at, TILE)],
                out_ref.at[used[i // 2], which, i % 2],
                sems.at[which, i],
            )
            copy.start()
            copies.append(copy)
    for place in range(places):
        if place not in used:
            out_ref[place] = jnp.zeros(out_ref.shape[1:], out_ref.dtype)
    for copy in copies:
        copy.wait()


def pack(x_down, x_up, w_tiles, tile_rows, tile_cols, counts, per_half, places):
    rows, units = x_down.shape[2], 2 * per_half
    smem = pl.BlockSpec(memory_space=pltpu.SMEM)
    vmem = pl.BlockSpec(memory_space=pltpu.VMEM)
    hbm = pl.BlockSpec(memory_space=pl.ANY)
    return pl.pallas_call(
        functools.partial(pack_kernel, per_half),
        out_shape=[
            jax.ShapeDtypeStruct((places, 2, 2, rows, TILE), x_down.dtype),
            jax.ShapeDtypeStruct(w_tiles.shape[1:], w_tiles.dtype),
            jax.ShapeDtypeStruct((2, 2 * units + 2), jnp.int32),
            jax.ShapeDtypeStruct((2, 2 * units + 2), jnp.int32),
        ],
        in_specs=[smem, smem, smem, hbm, hbm, hbm],
        out_specs=[vmem, vmem, smem, smem],
        scratch_shapes=[
            pltpu.SMEM((COLUMNS + 1,), jnp.int32),
            pltpu.SMEM((COLUMNS + 1,), jnp.int32),
            pltpu.SemaphoreType.DMA((2, 2 * units)),
            pltpu.SemaphoreType.DMA,
        ],
        cost_estimate=pl.CostEstimate(
            flops=0, bytes_accessed=16 * units * rows * TILE, transcendentals=0
        ),
    )(tile_rows, tile_cols, counts, x_down, x_up, w_tiles)


def swapped(array, apart):
    size = lax.axis_size("fsdp")
    return lax.ppermute(array, "fsdp", [(i, i ^ apart) for i in range(size)])


def near_at(slot, per_owner):
    owner = slot // per_owner
    other = jnp.where(owner % CORES == lax.axis_index("fsdp") % CORES, 0, per_owner)
    return other + slot - owner * per_owner


def far_kernel(per_half, order_ref, near_ref, out_ref):
    per_owner, owners = near_ref.shape[1] // CORES, 2 * CORES
    unit = unit_here(per_half, owners)
    asker = jnp.where(unit < per_half, unit + per_half, unit - per_half)
    for which in range(2):
        slot = jnp.maximum(order_ref[which, 2 * asker + 1], 0)
        out_ref[which] = near_ref[which, near_at(slot, per_owner)]


def far_weights(near, order, per_half):
    vmem = pl.BlockSpec(memory_space=pltpu.VMEM)
    return pl.pallas_call(
        functools.partial(far_kernel, per_half),
        out_shape=jax.ShapeDtypeStruct(near.shape[:1] + near.shape[2:], near.dtype),
        in_specs=[pl.BlockSpec(memory_space=pltpu.SMEM), vmem],
        out_specs=vmem,
        compiler_params=IN_VMEM,
        cost_estimate=pl.CostEstimate(flops=0, bytes_accessed=300_000, transcendentals=0),
    )(order, near)


def dot(a, b, over_a, over_b):
    return lax.dot_general(
        a, b, (((over_a,), (over_b,)), ((), ())), preferred_element_type=jnp.float32
    )


def grads_kernel(
    which, per_half, owners, loss_scale, order_ref, flags_ref, x_ref, near_ref, far_ref, out_ref,
    w_unit, first_sum, second_sum,
):
    sources, _, _, rows, _ = x_ref.shape
    per_owner = near_ref.shape[1] // CORES
    unit = unit_here(per_half, owners)
    half = lax.axis_index("fsdp") // CORES
    for i in range(2):
        slot = jnp.maximum(order_ref[which, 2 * unit + i], 0)
        near = slot // per_owner // CORES == half

        @pl.when(near)
        def _():
            w_unit[i] = near_ref[which, near_at(slot, per_owner)]

        @pl.when(jnp.logical_not(near))
        def _():
            w_unit[i] = far_ref[which]

    first_sum[...] = jnp.zeros_like(first_sum)
    second_sum[...] = jnp.zeros_like(second_sum)
    together = min(SOURCES_AT_ONCE, sources)
    steps = sources // together
    coupled = flags_ref[which, 2 * unit] == 1

    def read(step):
        at = step * together
        return [
            x_ref[pl.ds(at, together), which, i].reshape(together * rows, TILE) for i in range(2)
        ]

    @pl.when(coupled)
    def _():
        def go(step, carry):
            xs = jnp.concatenate(read(step), axis=1)
            firsts = jnp.concatenate([w_unit[0, 0], w_unit[1, 0]], axis=0)
            seconds = jnp.concatenate([w_unit[0, 1], w_unit[1, 1]], axis=1)
            value, slope = gelu_pair(dot(xs, firsts, 1, 0))
            active = value.astype(jnp.bfloat16)
            delta = dot(active, seconds, 1, 0)
            cotangent = (loss_scale * (xs.astype(jnp.float32) + delta)).astype(jnp.bfloat16)
            grad_act = dot(cotangent, seconds, 1, 1)
            grad_pre = (grad_act * slope).astype(jnp.bfloat16)
            first_sum[...] += dot(xs, grad_pre, 0, 0)
            second_sum[...] += dot(active, cotangent, 0, 0)
            return carry

        lax.fori_loop(0, steps, go, 0, unroll=min(steps, 4))

    @pl.when(jnp.logical_not(coupled))
    def _():
        def go(step, carry):
            for i, x in enumerate(read(step)):
                across = slice(i * TILE, (i + 1) * TILE)
                value, slope = gelu_pair(dot(x, w_unit[i, 0], 1, 0))
                active = value.astype(jnp.bfloat16)
                delta = dot(active, w_unit[i, 1], 1, 0)
                cotangent = (loss_scale * (x.astype(jnp.float32) + delta)).astype(jnp.bfloat16)
                grad_act = dot(cotangent, w_unit[i, 1], 1, 1)
                grad_pre = (grad_act * slope).astype(jnp.bfloat16)
                first_sum[across, :] += dot(x, grad_pre, 0, 0)
                second_sum[:, across] += dot(active, cotangent, 0, 0)
            return carry

        lax.fori_loop(0, steps, go, 0, unroll=min(steps, 4))

    for i in range(2):
        across = slice(i * TILE, (i + 1) * TILE)
        out_ref[i, 0] = first_sum[across, :].astype(out_ref.dtype)
        out_ref[i, 1] = second_sum[:, across].astype(out_ref.dtype)


def unit_grads(which, blocks, near, far, order, flags, per_half, owners, loss_scale, dtype):
    sources, _, _, rows, _ = blocks.shape
    smem = pl.BlockSpec(memory_space=pltpu.SMEM)
    vmem = pl.BlockSpec(memory_space=pltpu.VMEM)
    return pl.pallas_call(
        functools.partial(grads_kernel, which, per_half, owners, loss_scale),
        out_shape=jax.ShapeDtypeStruct((2, 2, TILE, TILE), dtype),
        in_specs=[smem, smem, vmem, vmem, vmem],
        out_specs=vmem,
        scratch_shapes=[
            pltpu.VMEM((2, 2, TILE, TILE), jnp.bfloat16),
            pltpu.VMEM((2 * TILE, TILE), jnp.float32),
            pltpu.VMEM((TILE, 2 * TILE), jnp.float32),
        ],
        compiler_params=IN_VMEM,
        cost_estimate=pl.CostEstimate(
            flops=20 * sources * rows * TILE * TILE,
            bytes_accessed=4 * sources * rows * TILE,
            transcendentals=2 * sources * rows * TILE,
        ),
    )(order, flags, blocks, near, far)


def add_kernel(own_ref, arrived_ref, out_ref):
    total = (own_ref[...] + arrived_ref[...].astype(jnp.float32)).astype(out_ref.dtype)
    for copy in range(out_ref.shape[0]):
        out_ref[copy] = total


def add(own, arrived, copies):
    vmem = pl.BlockSpec(memory_space=pltpu.VMEM)
    return pl.pallas_call(
        add_kernel,
        out_shape=jax.ShapeDtypeStruct((copies,) + own.shape, jnp.bfloat16),
        in_specs=[vmem, vmem],
        out_specs=vmem,
        compiler_params=IN_VMEM,
        cost_estimate=pl.CostEstimate(flops=own.size, bytes_accessed=900_000, transcendentals=0),
    )(own, arrived)


def place_kernel(per_half, order_ref, counts_ref, same_ref, other_ref, out_ref, zeros, sems, zero_sems):
    owner, owners = lax.axis_index("fsdp"), counts_ref.shape[2]
    per_owner = out_ref.shape[0]
    zeros[...] = jnp.zeros_like(zeros)

    def each(act):
        for i in range(4 * per_half):
            at = order_ref[0, i] - owner * per_owner
            mine = (at >= 0) & (at < per_owner)
            place = unit_place(i // 2, per_half, owners)
            near = owner % CORES == place % CORES
            for grads_ref, where in ((same_ref, near), (other_ref, jnp.logical_not(near))):

                @pl.when(mine & where)
                def _():
                    act(
                        pltpu.make_async_copy(
                            grads_ref.at[place // CORES, i % 2], out_ref.at[at], sems.at[i]
                        )
                    )

        for slot in range(per_owner):

            @pl.when(counts_ref[0, 0, owner] <= slot)
            def _():
                act(pltpu.make_async_copy(zeros, out_ref.at[slot], zero_sems.at[slot]))

    each(lambda copy: copy.start())
    each(lambda copy: copy.wait())


def place(same, other, order, counts, per_half, per_owner):
    smem = pl.BlockSpec(memory_space=pltpu.SMEM)
    hbm = pl.BlockSpec(memory_space=pl.ANY)
    return pl.pallas_call(
        functools.partial(place_kernel, per_half),
        out_shape=jax.ShapeDtypeStruct((per_owner,) + same.shape[2:], same.dtype),
        in_specs=[smem, smem, hbm, hbm],
        out_specs=hbm,
        scratch_shapes=[
            pltpu.VMEM(same.shape[2:], same.dtype),
            pltpu.SemaphoreType.DMA((4 * per_half,)),
            pltpu.SemaphoreType.DMA((per_owner,)),
        ],
        compiler_params=IN_VMEM,
        cost_estimate=pl.CostEstimate(flops=0, bytes_accessed=1_000_000, transcendentals=0),
    )(order, counts, same, other)


def body(x_down, x_up, w_tiles, tile_rows, tile_cols, counts):
    rows_here = x_down.shape[2]
    slots, owners = tile_cols.shape[2], counts.shape[2]
    per_half = (live_total(slots, owners) // 2 + 1) // 2
    places = lax.axis_size("dp") * lax.axis_size("fsdp")
    sections = lax.axis_size("section")
    across = [(i, (i + sections // 2) % sections) for i in range(sections)]
    loss_scale = float(2 * rows_here * places) ** (-0.5)

    packed, own_w, order, flags = pack(
        x_down, x_up, w_tiles, tile_rows, tile_cols, counts, per_half, places
    )
    blocks = lax.all_to_all(packed, PLANE, split_axis=0, concat_axis=0, tiled=True)
    near = jnp.concatenate([own_w, swapped(own_w, 1)], axis=1)
    far = swapped(far_weights(near, order, per_half), CORES)
    grads = functools.partial(
        unit_grads, blocks=blocks, near=near, far=far, order=order, flags=flags,
        per_half=per_half, owners=owners, loss_scale=loss_scale,
    )
    arrived = lax.ppermute(grads(1, dtype=jnp.bfloat16), "section", across)
    mine = add(grads(0, dtype=jnp.float32), arrived, places // CORES)
    same_core = [
        [place for place in range(places) if place % CORES == core] for core in range(CORES)
    ]
    same = lax.all_to_all(
        mine, PLANE, split_axis=0, concat_axis=0, axis_index_groups=same_core, tiled=True
    )
    other = swapped(same, 1)
    return place(same, other, order, counts, per_half, slots // owners)[None]


def solution(mesh):
    in_specs = (
        P("section", "dp", "fsdp", None),
        P("section", "dp", "fsdp", None),
        P("section", None, "fsdp", None, None, None),
        P("section", None, None),
        P("section", None, None),
        P("section", None, None),
    )
    out_specs = P("section", "fsdp", None, None, None)
    return jax.shard_map(body, mesh=mesh, in_specs=in_specs, out_specs=out_specs, check_vma=False)
```

```python
import functools
import math

import jax
import jax.numpy as jnp
from jax import lax
from jax.experimental import pallas as pl
from jax.experimental.pallas import tpu as pltpu
from jax.sharding import PartitionSpec as P

TILE = 128
PLANE = ("dp", "fsdp")
SOURCES_AT_ONCE = 4
COLUMNS = 192
CORES = 2
IN_VMEM = pltpu.CompilerParams(vmem_limit_bytes=16 * 1024 * 1024)

tanh_scale = math.sqrt(2.0 / math.pi)
cubic_coef = 0.044715


def gelu_pair(hidden):
    square = hidden * hidden
    tangent = jnp.tanh(tanh_scale * (hidden + cubic_coef * hidden * square))
    half = 0.5 * (1.0 + tangent)
    value = hidden * half
    slope = half + 0.5 * hidden * (1.0 - tangent * tangent) * tanh_scale * (
        1.0 + 3.0 * cubic_coef * square
    )
    return (value, slope)


def live_total(slots, owners):
    cap = slots // owners
    return sum(cap - i * cap // owners for i in range(owners))


def unit_place(unit, per_half, owners):
    half, at = unit // per_half, unit % per_half
    return at // CORES * owners + half * CORES + at % CORES


def unit_here(per_half, owners):
    owner = lax.axis_index("fsdp")
    at = lax.axis_index("dp") * CORES + owner % CORES
    return owner // CORES * per_half + jnp.minimum(at, per_half - 1)


def order_units(
    cols_ref, counts_ref, which, slots, per_half, order_ref, flags_ref, first_ref, last_ref
):
    per_owner, middle, unused = slots // counts_ref.shape[2], slots // 2, 4 * per_half
    for i in range(order_ref.shape[1]):
        order_ref[which, i] = -1
        flags_ref[which, i] = 0
    cols = []
    for s in range(slots):
        living = counts_ref[0, which, s // per_owner] > s % per_owner
        cols.append(jnp.where(living, cols_ref[0, which, s], COLUMNS))
    for s in range(slots):
        last_ref[cols[s]] = s
        first_ref[cols[slots - 1 - s]] = slots - 1 - s
    filled = [jnp.int32(0), jnp.int32(0)]

    def put(unit, slot_a, slot_b, coupled, really):
        at = jnp.where(really, 2 * unit, unused)
        order_ref[which, at] = slot_a
        order_ref[which, at + 1] = slot_b
        flags_ref[which, at] = coupled

    count = lambda condition: jnp.where(condition, 1, 0)
    alone, mixed = [], []
    for s in range(slots):
        living = cols[s] < COLUMNS
        first, last = first_ref[cols[s]], last_ref[cols[s]]
        leads = living & (first == s) & (last > s)
        alone.append(living & (first == last))
        half = s // middle
        pure = leads & (last < (half + 1) * middle)
        put(half * per_half + filled[half], s, last, 1, pure)
        filled[half] = filled[half] + count(pure)
        if half == 0:
            mixed.append((s, last, 1, leads & (last >= middle)))
    waiting, odd = [jnp.int32(0), jnp.int32(0)], [jnp.int32(0), jnp.int32(0)]
    for s in range(slots):
        half = s // middle
        second = alone[s] & (odd[half] == 1)
        put(half * per_half + filled[half], waiting[half], s, 0, second)
        filled[half] = filled[half] + count(second)
        odd[half] = jnp.where(alone[s], 1 - odd[half], odd[half])
        waiting[half] = jnp.where(alone[s], s, waiting[half])
    mixed.append((waiting[0], waiting[1], 0, odd[0] == 1))
    for low, high, coupled, really in mixed:
        room = filled[0] < per_half
        unit = jnp.where(room, filled[0], per_half + filled[1])
        put(unit, jnp.where(room, low, high), jnp.where(room, high, low), coupled, really)
        filled[0] = filled[0] + count(really & room)
        filled[1] = filled[1] + count(really & jnp.logical_not(room))


def pick(which, per_half, owners, rows_ref, order_ref, x_ref, out_ref, sems):
    copies, used = [], [unit_place(unit, per_half, owners) for unit in range(2 * per_half)]
    for i in range(4 * per_half):
        row = rows_ref[0, which, jnp.maximum(order_ref[which, i], 0)]
        at = pl.multiple_of(row * TILE, TILE)
        copy = pltpu.make_async_copy(
            x_ref.at[0, 0, :, pl.ds(at, TILE)], out_ref.at[used[i // 2], i % 2], sems.at[i]
        )
        copy.start()
        copies.append(copy)
    for place in range(out_ref.shape[0]):
        if place not in used:
            out_ref[place] = jnp.zeros(out_ref.shape[1:], out_ref.dtype)
    return copies


def pack_up_kernel(
    per_half, rows_ref, cols_ref, counts_ref, x_ref, w_ref,
    out_ref, own_w_ref, order_ref, flags_ref, first_ref, last_ref, sems, w_sem,
):
    slots, owners = cols_ref.shape[2], counts_ref.shape[2]
    weights = pltpu.make_async_copy(w_ref.at[0], own_w_ref, w_sem)
    weights.start()
    tables = (order_ref, flags_ref, first_ref, last_ref)
    order_units(cols_ref, counts_ref, 1, slots, per_half, *tables)
    copies = pick(1, per_half, owners, rows_ref, order_ref, x_ref, out_ref, sems)
    order_units(cols_ref, counts_ref, 0, slots, per_half, *tables)
    for copy in copies + [weights]:
        copy.wait()


def pack_up(x_up, w_tiles, tile_rows, tile_cols, counts, per_half, places):
    rows, units = x_up.shape[2], 2 * per_half
    smem = pl.BlockSpec(memory_space=pltpu.SMEM)
    vmem = pl.BlockSpec(memory_space=pltpu.VMEM)
    hbm = pl.BlockSpec(memory_space=pl.ANY)
    return pl.pallas_call(
        functools.partial(pack_up_kernel, per_half),
        out_shape=[
            jax.ShapeDtypeStruct((places, 2, rows, TILE), x_up.dtype),
            jax.ShapeDtypeStruct(w_tiles.shape[1:], w_tiles.dtype),
            jax.ShapeDtypeStruct((2, 2 * units + 2), jnp.int32),
            jax.ShapeDtypeStruct((2, 2 * units + 2), jnp.int32),
        ],
        in_specs=[smem, smem, smem, hbm, hbm],
        out_specs=[vmem, vmem, smem, smem],
        scratch_shapes=[
            pltpu.SMEM((COLUMNS + 1,), jnp.int32),
            pltpu.SMEM((COLUMNS + 1,), jnp.int32),
            pltpu.SemaphoreType.DMA((2 * units,)),
            pltpu.SemaphoreType.DMA,
        ],
        cost_estimate=pl.CostEstimate(
            flops=0, bytes_accessed=8 * units * rows * TILE, transcendentals=0
        ),
    )(tile_rows, tile_cols, counts, x_up, w_tiles)


def pack_down_kernel(per_half, owners, rows_ref, order_ref, x_ref, out_ref, sems):
    for copy in pick(0, per_half, owners, rows_ref, order_ref, x_ref, out_ref, sems):
        copy.wait()


def pack_down(x_down, tile_rows, order, per_half, owners, places):
    rows, units = x_down.shape[2], 2 * per_half
    smem = pl.BlockSpec(memory_space=pltpu.SMEM)
    return pl.pallas_call(
        functools.partial(pack_down_kernel, per_half, owners),
        out_shape=jax.ShapeDtypeStruct((places, 2, rows, TILE), x_down.dtype),
        in_specs=[smem, smem, pl.BlockSpec(memory_space=pl.ANY)],
        out_specs=pl.BlockSpec(memory_space=pltpu.VMEM),
        scratch_shapes=[pltpu.SemaphoreType.DMA((2 * units,))],
        cost_estimate=pl.CostEstimate(
            flops=0, bytes_accessed=8 * units * rows * TILE, transcendentals=0
        ),
    )(tile_rows, order, x_down)


def swapped(array, apart):
    size = lax.axis_size("fsdp")
    return lax.ppermute(array, "fsdp", [(i, i ^ apart) for i in range(size)])


def near_at(slot, per_owner):
    owner = slot // per_owner
    other = jnp.where(owner % CORES == lax.axis_index("fsdp") % CORES, 0, per_owner)
    return other + slot - owner * per_owner


def far_kernel(per_half, order_ref, near_ref, out_ref):
    per_owner, owners = near_ref.shape[1] // CORES, 2 * CORES
    unit = unit_here(per_half, owners)
    asker = jnp.where(unit < per_half, unit + per_half, unit - per_half)
    for which in range(2):
        slot = jnp.maximum(order_ref[which, 2 * asker + 1], 0)
        out_ref[which] = near_ref[which, near_at(slot, per_owner)]


def far_weights(near, order, per_half):
    vmem = pl.BlockSpec(memory_space=pltpu.VMEM)
    return pl.pallas_call(
        functools.partial(far_kernel, per_half),
        out_shape=jax.ShapeDtypeStruct(near.shape[:1] + near.shape[2:], near.dtype),
        in_specs=[pl.BlockSpec(memory_space=pltpu.SMEM), vmem],
        out_specs=vmem,
        compiler_params=IN_VMEM,
        cost_estimate=pl.CostEstimate(flops=0, bytes_accessed=300_000, transcendentals=0),
    )(order, near)


def dot(a, b, over_a, over_b):
    return lax.dot_general(
        a, b, (((over_a,), (over_b,)), ((), ())), preferred_element_type=jnp.float32
    )


def grads_kernel(
    which, per_half, owners, loss_scale, order_ref, flags_ref, x_ref, near_ref, far_ref, out_ref,
    w_unit, first_sum, second_sum,
):
    sources, _, rows, _ = x_ref.shape
    per_owner = near_ref.shape[1] // CORES
    unit = unit_here(per_half, owners)
    half = lax.axis_index("fsdp") // CORES
    for i in range(2):
        slot = jnp.maximum(order_ref[which, 2 * unit + i], 0)
        near = slot // per_owner // CORES == half

        @pl.when(near)
        def _():
            w_unit[i] = near_ref[which, near_at(slot, per_owner)]

        @pl.when(jnp.logical_not(near))
        def _():
            w_unit[i] = far_ref[which]

    first_sum[...] = jnp.zeros_like(first_sum)
    second_sum[...] = jnp.zeros_like(second_sum)
    together = min(SOURCES_AT_ONCE, sources)
    steps = sources // together
    coupled = flags_ref[which, 2 * unit] == 1

    def read(step):
        at = step * together
        return [
            x_ref[pl.ds(at, together), i].reshape(together * rows, TILE) for i in range(2)
        ]

    @pl.when(coupled)
    def _():
        def go(step, carry):
            xs = jnp.concatenate(read(step), axis=1)
            firsts = jnp.concatenate([w_unit[0, 0], w_unit[1, 0]], axis=0)
            seconds = jnp.concatenate([w_unit[0, 1], w_unit[1, 1]], axis=1)
            value, slope = gelu_pair(dot(xs, firsts, 1, 0))
            active = value.astype(jnp.bfloat16)
            delta = dot(active, seconds, 1, 0)
            cotangent = (loss_scale * (xs.astype(jnp.float32) + delta)).astype(jnp.bfloat16)
            grad_act = dot(cotangent, seconds, 1, 1)
            grad_pre = (grad_act * slope).astype(jnp.bfloat16)
            first_sum[...] += dot(xs, grad_pre, 0, 0)
            second_sum[...] += dot(active, cotangent, 0, 0)
            return carry

        lax.fori_loop(0, steps, go, 0, unroll=min(steps, 4))

    @pl.when(jnp.logical_not(coupled))
    def _():
        def go(step, carry):
            for i, x in enumerate(read(step)):
                across = slice(i * TILE, (i + 1) * TILE)
                value, slope = gelu_pair(dot(x, w_unit[i, 0], 1, 0))
                active = value.astype(jnp.bfloat16)
                delta = dot(active, w_unit[i, 1], 1, 0)
                cotangent = (loss_scale * (x.astype(jnp.float32) + delta)).astype(jnp.bfloat16)
                grad_act = dot(cotangent, w_unit[i, 1], 1, 1)
                grad_pre = (grad_act * slope).astype(jnp.bfloat16)
                first_sum[across, :] += dot(x, grad_pre, 0, 0)
                second_sum[:, across] += dot(active, cotangent, 0, 0)
            return carry

        lax.fori_loop(0, steps, go, 0, unroll=min(steps, 4))

    for i in range(2):
        across = slice(i * TILE, (i + 1) * TILE)
        out_ref[i, 0] = first_sum[across, :].astype(out_ref.dtype)
        out_ref[i, 1] = second_sum[:, across].astype(out_ref.dtype)


def unit_grads(which, blocks, near, far, order, flags, per_half, owners, loss_scale, dtype):
    sources, _, rows, _ = blocks.shape
    smem = pl.BlockSpec(memory_space=pltpu.SMEM)
    vmem = pl.BlockSpec(memory_space=pltpu.VMEM)
    return pl.pallas_call(
        functools.partial(grads_kernel, which, per_half, owners, loss_scale),
        out_shape=jax.ShapeDtypeStruct((2, 2, TILE, TILE), dtype),
        in_specs=[smem, smem, vmem, vmem, vmem],
        out_specs=vmem,
        scratch_shapes=[
            pltpu.VMEM((2, 2, TILE, TILE), jnp.bfloat16),
            pltpu.VMEM((2 * TILE, TILE), jnp.float32),
            pltpu.VMEM((TILE, 2 * TILE), jnp.float32),
        ],
        compiler_params=IN_VMEM,
        cost_estimate=pl.CostEstimate(
            flops=20 * sources * rows * TILE * TILE,
            bytes_accessed=4 * sources * rows * TILE,
            transcendentals=2 * sources * rows * TILE,
        ),
    )(order, flags, blocks, near, far)


def add_kernel(own_ref, arrived_ref, out_ref):
    total = (own_ref[...] + arrived_ref[...].astype(jnp.float32)).astype(out_ref.dtype)
    for copy in range(out_ref.shape[0]):
        out_ref[copy] = total


def add(own, arrived, copies):
    vmem = pl.BlockSpec(memory_space=pltpu.VMEM)
    return pl.pallas_call(
        add_kernel,
        out_shape=jax.ShapeDtypeStruct((copies,) + own.shape, jnp.bfloat16),
        in_specs=[vmem, vmem],
        out_specs=vmem,
        compiler_params=IN_VMEM,
        cost_estimate=pl.CostEstimate(flops=own.size, bytes_accessed=900_000, transcendentals=0),
    )(own, arrived)


def place_kernel(per_half, order_ref, counts_ref, same_ref, other_ref, out_ref, zeros, sems, zero_sems):
    owner, owners = lax.axis_index("fsdp"), counts_ref.shape[2]
    per_owner = out_ref.shape[0]
    zeros[...] = jnp.zeros_like(zeros)

    def each(act):
        for i in range(4 * per_half):
            at = order_ref[0, i] - owner * per_owner
            mine = (at >= 0) & (at < per_owner)
            place = unit_place(i // 2, per_half, owners)
            near = owner % CORES == place % CORES
            for grads_ref, where in ((same_ref, near), (other_ref, jnp.logical_not(near))):

                @pl.when(mine & where)
                def _():
                    act(
                        pltpu.make_async_copy(
                            grads_ref.at[place // CORES, i % 2], out_ref.at[at], sems.at[i]
                        )
                    )

        for slot in range(per_owner):

            @pl.when(counts_ref[0, 0, owner] <= slot)
            def _():
                act(pltpu.make_async_copy(zeros, out_ref.at[slot], zero_sems.at[slot]))

    each(lambda copy: copy.start())
    each(lambda copy: copy.wait())


def place(same, other, order, counts, per_half, per_owner):
    smem = pl.BlockSpec(memory_space=pltpu.SMEM)
    hbm = pl.BlockSpec(memory_space=pl.ANY)
    return pl.pallas_call(
        functools.partial(place_kernel, per_half),
        out_shape=jax.ShapeDtypeStruct((per_owner,) + same.shape[2:], same.dtype),
        in_specs=[smem, smem, hbm, hbm],
        out_specs=hbm,
        scratch_shapes=[
            pltpu.VMEM(same.shape[2:], same.dtype),
            pltpu.SemaphoreType.DMA((4 * per_half,)),
            pltpu.SemaphoreType.DMA((per_owner,)),
        ],
        compiler_params=IN_VMEM,
        cost_estimate=pl.CostEstimate(flops=0, bytes_accessed=1_000_000, transcendentals=0),
    )(order, counts, same, other)


def body(x_down, x_up, w_tiles, tile_rows, tile_cols, counts):
    rows_here = x_down.shape[2]
    slots, owners = tile_cols.shape[2], counts.shape[2]
    per_half = (live_total(slots, owners) // 2 + 1) // 2
    places = lax.axis_size("dp") * lax.axis_size("fsdp")
    sections = lax.axis_size("section")
    across = [(i, (i + sections // 2) % sections) for i in range(sections)]
    loss_scale = float(2 * rows_here * places) ** (-0.5)

    trade = lambda packed: lax.all_to_all(packed, PLANE, split_axis=0, concat_axis=0, tiled=True)
    up, own_w, order, flags = pack_up(
        x_up, w_tiles, tile_rows, tile_cols, counts, per_half, places
    )
    up = trade(up)
    down = trade(pack_down(x_down, tile_rows, order, per_half, owners, places))
    near = jnp.concatenate([own_w, swapped(own_w, 1)], axis=1)
    far = swapped(far_weights(near, order, per_half), CORES)
    grads = functools.partial(
        unit_grads, near=near, far=far, order=order, flags=flags,
        per_half=per_half, owners=owners, loss_scale=loss_scale,
    )
    arrived = lax.ppermute(grads(1, up, dtype=jnp.bfloat16), "section", across)
    mine = add(grads(0, down, dtype=jnp.float32), arrived, places // CORES)
    same_core = [
        [place for place in range(places) if place % CORES == core] for core in range(CORES)
    ]
    same = lax.all_to_all(
        mine, PLANE, split_axis=0, concat_axis=0, axis_index_groups=same_core, tiled=True
    )
    other = swapped(same, 1)
    return place(same, other, order, counts, per_half, slots // owners)[None]


def solution(mesh):
    in_specs = (
        P("section", "dp", "fsdp", None),
        P("section", "dp", "fsdp", None),
        P("section", None, "fsdp", None, None, None),
        P("section", None, None),
        P("section", None, None),
        P("section", None, None),
    )
    out_specs = P("section", "fsdp", None, None, None)
    return jax.shard_map(body, mesh=mesh, in_specs=in_specs, out_specs=out_specs, check_vma=False)
```

```python
import functools
import math

import jax
import jax.numpy as jnp
from jax import lax
from jax.experimental import pallas as pl
from jax.experimental.pallas import tpu as pltpu
from jax.sharding import PartitionSpec as P

TILE = 128
PLANE = ("dp", "fsdp")
SOURCES_AT_ONCE = 8
COLUMNS = 192
CORES = 2
IN_VMEM = pltpu.CompilerParams(vmem_limit_bytes=16 * 1024 * 1024)

tanh_scale = math.sqrt(2.0 / math.pi)
cubic_coef = 0.044715


def gelu_pair(hidden):
    square = hidden * hidden
    tangent = jnp.tanh(tanh_scale * (hidden + cubic_coef * hidden * square))
    half = 0.5 * (1.0 + tangent)
    value = hidden * half
    slope = half + 0.5 * hidden * (1.0 - tangent * tangent) * tanh_scale * (
        1.0 + 3.0 * cubic_coef * square
    )
    return (value, slope)


def live_total(slots, owners):
    cap = slots // owners
    return sum(cap - i * cap // owners for i in range(owners))


def unit_place(unit, per_half, owners):
    half, at = unit // per_half, unit % per_half
    return at // CORES * owners + half * CORES + at % CORES


def unit_here(per_half, owners):
    owner = lax.axis_index("fsdp")
    at = lax.axis_index("dp") * CORES + owner % CORES
    return owner // CORES * per_half + jnp.minimum(at, per_half - 1)


def order_units(
    cols_ref, counts_ref, which, slots, per_half, order_ref, flags_ref, first_ref, last_ref
):
    per_owner, middle, unused = slots // counts_ref.shape[2], slots // 2, 4 * per_half
    for i in range(order_ref.shape[1]):
        order_ref[which, i] = -1
        flags_ref[which, i] = 0
    cols = []
    for s in range(slots):
        living = counts_ref[0, which, s // per_owner] > s % per_owner
        cols.append(jnp.where(living, cols_ref[0, which, s], COLUMNS))
    for s in range(slots):
        last_ref[cols[s]] = s
        first_ref[cols[slots - 1 - s]] = slots - 1 - s
    filled = [jnp.int32(0), jnp.int32(0)]

    def put(unit, slot_a, slot_b, coupled, really):
        at = jnp.where(really, 2 * unit, unused)
        order_ref[which, at] = slot_a
        order_ref[which, at + 1] = slot_b
        flags_ref[which, at] = coupled

    count = lambda condition: jnp.where(condition, 1, 0)
    alone, mixed = [], []
    for s in range(slots):
        living = cols[s] < COLUMNS
        first, last = first_ref[cols[s]], last_ref[cols[s]]
        leads = living & (first == s) & (last > s)
        alone.append(living & (first == last))
        half = s // middle
        pure = leads & (last < (half + 1) * middle)
        put(half * per_half + filled[half], s, last, 1, pure)
        filled[half] = filled[half] + count(pure)
        if half == 0:
            mixed.append((s, last, 1, leads & (last >= middle)))
    waiting, odd = [jnp.int32(0), jnp.int32(0)], [jnp.int32(0), jnp.int32(0)]
    for s in range(slots):
        half = s // middle
        second = alone[s] & (odd[half] == 1)
        put(half * per_half + filled[half], waiting[half], s, 0, second)
        filled[half] = filled[half] + count(second)
        odd[half] = jnp.where(alone[s], 1 - odd[half], odd[half])
        waiting[half] = jnp.where(alone[s], s, waiting[half])
    mixed.append((waiting[0], waiting[1], 0, odd[0] == 1))
    for low, high, coupled, really in mixed:
        room = filled[0] < per_half
        unit = jnp.where(room, filled[0], per_half + filled[1])
        put(unit, jnp.where(room, low, high), jnp.where(room, high, low), coupled, really)
        filled[0] = filled[0] + count(really & room)
        filled[1] = filled[1] + count(really & jnp.logical_not(room))


def pack_kernel(
    per_half, rows_ref, cols_ref, counts_ref, down_ref, up_ref,
    out_ref, order_ref, flags_ref, first_ref, last_ref, sems,
):
    slots, owners = cols_ref.shape[2], counts_ref.shape[2]
    places, units = out_ref.shape[0], 2 * per_half
    copies = []
    used = [unit_place(unit, per_half, owners) for unit in range(units)]
    for which, x_ref in ((1, up_ref), (0, down_ref)):
        order_units(
            cols_ref, counts_ref, which, slots, per_half, order_ref, flags_ref, first_ref, last_ref
        )
        for i in range(2 * units):
            row = rows_ref[0, which, jnp.maximum(order_ref[which, i], 0)]
            at = pl.multiple_of(row * TILE, TILE)
            copy = pltpu.make_async_copy(
                x_ref.at[0, 0, :, pl.ds(at, TILE)],
                out_ref.at[used[i // 2], which, i % 2],
                sems.at[which, i],
            )
            copy.start()
            copies.append(copy)
    for place in range(places):
        if place not in used:
            out_ref[place] = jnp.zeros(out_ref.shape[1:], out_ref.dtype)
    for copy in copies:
        copy.wait()


def pack(x_down, x_up, tile_rows, tile_cols, counts, per_half, places):
    rows, units = x_down.shape[2], 2 * per_half
    smem = pl.BlockSpec(memory_space=pltpu.SMEM)
    vmem = pl.BlockSpec(memory_space=pltpu.VMEM)
    hbm = pl.BlockSpec(memory_space=pl.ANY)
    return pl.pallas_call(
        functools.partial(pack_kernel, per_half),
        out_shape=[
            jax.ShapeDtypeStruct((places, 2, 2, rows, TILE), x_down.dtype),
            jax.ShapeDtypeStruct((2, 2 * units + 2), jnp.int32),
            jax.ShapeDtypeStruct((2, 2 * units + 2), jnp.int32),
        ],
        in_specs=[smem, smem, smem, hbm, hbm],
        out_specs=[vmem, smem, smem],
        scratch_shapes=[
            pltpu.SMEM((COLUMNS + 1,), jnp.int32),
            pltpu.SMEM((COLUMNS + 1,), jnp.int32),
            pltpu.SemaphoreType.DMA((2, 2 * units)),
        ],
        cost_estimate=pl.CostEstimate(
            flops=0, bytes_accessed=16 * units * rows * TILE, transcendentals=0
        ),
    )(tile_rows, tile_cols, counts, x_down, x_up)


def swapped(array, apart):
    size = lax.axis_size("fsdp")
    return lax.ppermute(array, "fsdp", [(i, i ^ apart) for i in range(size)])


def near_at(slot, per_owner):
    owner = slot // per_owner
    other = jnp.where(owner % CORES == lax.axis_index("fsdp") % CORES, 0, per_owner)
    return other + slot - owner * per_owner


def far_kernel(per_half, order_ref, near_ref, out_ref):
    per_owner, owners = near_ref.shape[1] // CORES, 2 * CORES
    unit = unit_here(per_half, owners)
    asker = jnp.where(unit < per_half, unit + per_half, unit - per_half)
    for which in range(2):
        slot = jnp.maximum(order_ref[which, 2 * asker + 1], 0)
        out_ref[which] = near_ref[which, near_at(slot, per_owner)]


def far_weights(near, order, per_half):
    vmem = pl.BlockSpec(memory_space=pltpu.VMEM)
    return pl.pallas_call(
        functools.partial(far_kernel, per_half),
        out_shape=jax.ShapeDtypeStruct(near.shape[:1] + near.shape[2:], near.dtype),
        in_specs=[pl.BlockSpec(memory_space=pltpu.SMEM), vmem],
        out_specs=vmem,
        compiler_params=IN_VMEM,
        cost_estimate=pl.CostEstimate(flops=0, bytes_accessed=300_000, transcendentals=0),
    )(order, near)


def dot(a, b, over_a, over_b):
    return lax.dot_general(
        a, b, (((over_a,), (over_b,)), ((), ())), preferred_element_type=jnp.float32
    )


def grads_kernel(
    which, per_half, owners, loss_scale, order_ref, flags_ref, x_ref, near_ref, far_ref, out_ref,
    w_unit, first_sum, second_sum,
):
    sources, _, _, rows, _ = x_ref.shape
    per_owner = near_ref.shape[1] // CORES
    unit = unit_here(per_half, owners)
    half = lax.axis_index("fsdp") // CORES
    for i in range(2):
        slot = jnp.maximum(order_ref[which, 2 * unit + i], 0)
        near = slot // per_owner // CORES == half

        @pl.when(near)
        def _():
            w_unit[i] = near_ref[which, near_at(slot, per_owner)]

        @pl.when(jnp.logical_not(near))
        def _():
            w_unit[i] = far_ref[which]

    together = min(SOURCES_AT_ONCE, sources)
    steps = sources // together
    if steps > 1:
        first_sum[...] = jnp.zeros_like(first_sum)
        second_sum[...] = jnp.zeros_like(second_sum)

    def sum_up(total_ref, where, term):
        total_ref[where] = total_ref[where] + term if steps > 1 else term

    coupled = flags_ref[which, 2 * unit] == 1

    def read(step):
        at = step * together
        return [
            x_ref[pl.ds(at, together), which, i].reshape(together * rows, TILE) for i in range(2)
        ]

    @pl.when(coupled)
    def _():
        def go(step, carry):
            xs = jnp.concatenate(read(step), axis=1)
            firsts = jnp.concatenate([w_unit[0, 0], w_unit[1, 0]], axis=0)
            seconds = jnp.concatenate([w_unit[0, 1], w_unit[1, 1]], axis=1)
            value, slope = gelu_pair(dot(xs, firsts, 1, 0))
            active = value.astype(jnp.bfloat16)
            delta = dot(active, seconds, 1, 0)
            cotangent = (loss_scale * (xs.astype(jnp.float32) + delta)).astype(jnp.bfloat16)
            grad_act = dot(cotangent, seconds, 1, 1)
            grad_pre = (grad_act * slope).astype(jnp.bfloat16)
            sum_up(first_sum, ..., dot(xs, grad_pre, 0, 0))
            sum_up(second_sum, ..., dot(active, cotangent, 0, 0))
            return carry

        lax.fori_loop(0, steps, go, 0, unroll=min(steps, 4))

    @pl.when(jnp.logical_not(coupled))
    def _():
        def go(step, carry):
            for i, x in enumerate(read(step)):
                across = slice(i * TILE, (i + 1) * TILE)
                value, slope = gelu_pair(dot(x, w_unit[i, 0], 1, 0))
                active = value.astype(jnp.bfloat16)
                delta = dot(active, w_unit[i, 1], 1, 0)
                cotangent = (loss_scale * (x.astype(jnp.float32) + delta)).astype(jnp.bfloat16)
                grad_act = dot(cotangent, w_unit[i, 1], 1, 1)
                grad_pre = (grad_act * slope).astype(jnp.bfloat16)
                sum_up(first_sum, (across, slice(None)), dot(x, grad_pre, 0, 0))
                sum_up(second_sum, (slice(None), across), dot(active, cotangent, 0, 0))
            return carry

        lax.fori_loop(0, steps, go, 0, unroll=min(steps, 4))

    for i in range(2):
        across = slice(i * TILE, (i + 1) * TILE)
        out_ref[i, 0] = first_sum[across, :].astype(out_ref.dtype)
        out_ref[i, 1] = second_sum[:, across].astype(out_ref.dtype)


def unit_grads(which, blocks, near, far, order, flags, per_half, owners, loss_scale, dtype):
    sources, _, _, rows, _ = blocks.shape
    smem = pl.BlockSpec(memory_space=pltpu.SMEM)
    vmem = pl.BlockSpec(memory_space=pltpu.VMEM)
    return pl.pallas_call(
        functools.partial(grads_kernel, which, per_half, owners, loss_scale),
        out_shape=jax.ShapeDtypeStruct((2, 2, TILE, TILE), dtype),
        in_specs=[smem, smem, vmem, vmem, vmem],
        out_specs=vmem,
        scratch_shapes=[
            pltpu.VMEM((2, 2, TILE, TILE), jnp.bfloat16),
            pltpu.VMEM((2 * TILE, TILE), jnp.float32),
            pltpu.VMEM((TILE, 2 * TILE), jnp.float32),
        ],
        compiler_params=IN_VMEM,
        cost_estimate=pl.CostEstimate(
            flops=20 * sources * rows * TILE * TILE,
            bytes_accessed=4 * sources * rows * TILE,
            transcendentals=2 * sources * rows * TILE,
        ),
    )(order, flags, blocks, near, far)


def add_kernel(own_ref, arrived_ref, out_ref):
    total = (own_ref[...] + arrived_ref[...].astype(jnp.float32)).astype(out_ref.dtype)
    for copy in range(out_ref.shape[0]):
        out_ref[copy] = total


def add(own, arrived, copies):
    vmem = pl.BlockSpec(memory_space=pltpu.VMEM)
    return pl.pallas_call(
        add_kernel,
        out_shape=jax.ShapeDtypeStruct((copies,) + own.shape, jnp.bfloat16),
        in_specs=[vmem, vmem],
        out_specs=vmem,
        compiler_params=IN_VMEM,
        cost_estimate=pl.CostEstimate(flops=own.size, bytes_accessed=900_000, transcendentals=0),
    )(own, arrived)


def place_kernel(per_half, order_ref, counts_ref, same_ref, other_ref, out_ref, zeros, sems, zero_sems):
    owner, owners = lax.axis_index("fsdp"), counts_ref.shape[2]
    per_owner = out_ref.shape[0]
    zeros[...] = jnp.zeros_like(zeros)

    def each(act):
        for i in range(4 * per_half):
            at = order_ref[0, i] - owner * per_owner
            mine = (at >= 0) & (at < per_owner)
            place = unit_place(i // 2, per_half, owners)
            near = owner % CORES == place % CORES
            for grads_ref, where in ((same_ref, near), (other_ref, jnp.logical_not(near))):

                @pl.when(mine & where)
                def _():
                    act(
                        pltpu.make_async_copy(
                            grads_ref.at[place // CORES, i % 2], out_ref.at[at], sems.at[i]
                        )
                    )

        for slot in range(per_owner):

            @pl.when(counts_ref[0, 0, owner] <= slot)
            def _():
                act(pltpu.make_async_copy(zeros, out_ref.at[slot], zero_sems.at[slot]))

    each(lambda copy: copy.start())
    each(lambda copy: copy.wait())


def place(same, other, order, counts, per_half, per_owner):
    smem = pl.BlockSpec(memory_space=pltpu.SMEM)
    hbm = pl.BlockSpec(memory_space=pl.ANY)
    return pl.pallas_call(
        functools.partial(place_kernel, per_half),
        out_shape=jax.ShapeDtypeStruct((per_owner,) + same.shape[2:], same.dtype),
        in_specs=[smem, smem, hbm, hbm],
        out_specs=hbm,
        scratch_shapes=[
            pltpu.VMEM(same.shape[2:], same.dtype),
            pltpu.SemaphoreType.DMA((4 * per_half,)),
            pltpu.SemaphoreType.DMA((per_owner,)),
        ],
        compiler_params=IN_VMEM,
        cost_estimate=pl.CostEstimate(flops=0, bytes_accessed=1_000_000, transcendentals=0),
    )(order, counts, same, other)


def body(x_down, x_up, w_tiles, tile_rows, tile_cols, counts):
    rows_here = x_down.shape[2]
    slots, owners = tile_cols.shape[2], counts.shape[2]
    per_half = (live_total(slots, owners) // 2 + 1) // 2
    places = lax.axis_size("dp") * lax.axis_size("fsdp")
    sections = lax.axis_size("section")
    across = [(i, (i + sections // 2) % sections) for i in range(sections)]
    loss_scale = float(2 * rows_here * places) ** (-0.5)

    packed, order, flags = pack(x_down, x_up, tile_rows, tile_cols, counts, per_half, places)
    blocks = lax.all_to_all(packed, PLANE, split_axis=0, concat_axis=0, tiled=True)
    near = jnp.concatenate([w_tiles[0], swapped(w_tiles[0], 1)], axis=1)
    far = swapped(far_weights(near, order, per_half), CORES)
    grads = functools.partial(
        unit_grads, blocks=blocks, near=near, far=far, order=order, flags=flags,
        per_half=per_half, owners=owners, loss_scale=loss_scale,
    )
    arrived = lax.ppermute(grads(1, dtype=jnp.bfloat16), "section", across)
    mine = add(grads(0, dtype=jnp.float32), arrived, places // CORES)
    same_core = [
        [place for place in range(places) if place % CORES == core] for core in range(CORES)
    ]
    same = lax.all_to_all(
        mine, PLANE, split_axis=0, concat_axis=0, axis_index_groups=same_core, tiled=True
    )
    other = swapped(same, 1)
    return place(same, other, order, counts, per_half, slots // owners)[None]


def solution(mesh):
    in_specs = (
        P("section", "dp", "fsdp", None),
        P("section", "dp", "fsdp", None),
        P("section", None, "fsdp", None, None, None),
        P("section", None, None),
        P("section", None, None),
        P("section", None, None),
    )
    out_specs = P("section", "fsdp", None, None, None)
    return jax.shard_map(body, mesh=mesh, in_specs=in_specs, out_specs=out_specs, check_vma=False)
```

```python
import functools
import math

import jax
import jax.numpy as jnp
from jax import lax
from jax.experimental import pallas as pl
from jax.experimental.pallas import tpu as pltpu
from jax.sharding import PartitionSpec as P

TILE = 128
PLANE = ("dp", "fsdp")
SOURCES_AT_ONCE = 8
COLUMNS = 192
CORES = 2
IN_VMEM = pltpu.CompilerParams(vmem_limit_bytes=16 * 1024 * 1024)

tanh_scale = math.sqrt(2.0 / math.pi)
cubic_coef = 0.044715


def gelu_pair(hidden):
    square = hidden * hidden
    tangent = jnp.tanh(tanh_scale * (hidden + cubic_coef * hidden * square))
    half = 0.5 * (1.0 + tangent)
    value = hidden * half
    slope = half + 0.5 * hidden * (1.0 - tangent * tangent) * tanh_scale * (
        1.0 + 3.0 * cubic_coef * square
    )
    return (value, slope)


def live_total(slots, owners):
    cap = slots // owners
    return sum(cap - i * cap // owners for i in range(owners))


def unit_place(unit, per_half, owners):
    half, at = unit // per_half, unit % per_half
    return at // CORES * owners + half * CORES + at % CORES


def unit_here(per_half, owners):
    owner = lax.axis_index("fsdp")
    at = lax.axis_index("dp") * CORES + owner % CORES
    return owner // CORES * per_half + jnp.minimum(at, per_half - 1)


def order_units(
    cols_ref, counts_ref, which, slots, per_half, order_ref, flags_ref, first_ref, last_ref
):
    per_owner, middle, unused = slots // counts_ref.shape[2], slots // 2, 4 * per_half
    for i in range(order_ref.shape[1]):
        order_ref[which, i] = -1
        flags_ref[which, i] = 0
    cols = []
    for s in range(slots):
        living = counts_ref[0, which, s // per_owner] > s % per_owner
        cols.append(jnp.where(living, cols_ref[0, which, s], COLUMNS))
    for s in range(slots):
        last_ref[cols[s]] = s
        first_ref[cols[slots - 1 - s]] = slots - 1 - s
    filled = [jnp.int32(0), jnp.int32(0)]

    def put(unit, slot_a, slot_b, coupled, really):
        at = jnp.where(really, 2 * unit, unused)
        order_ref[which, at] = slot_a
        order_ref[which, at + 1] = slot_b
        flags_ref[which, at] = coupled

    count = lambda condition: jnp.where(condition, 1, 0)
    alone, mixed = [], []
    for s in range(slots):
        living = cols[s] < COLUMNS
        first, last = first_ref[cols[s]], last_ref[cols[s]]
        leads = living & (first == s) & (last > s)
        alone.append(living & (first == last))
        half = s // middle
        pure = leads & (last < (half + 1) * middle)
        put(half * per_half + filled[half], s, last, 1, pure)
        filled[half] = filled[half] + count(pure)
        if half == 0:
            mixed.append((s, last, 1, leads & (last >= middle)))
    waiting, odd = [jnp.int32(0), jnp.int32(0)], [jnp.int32(0), jnp.int32(0)]
    for s in range(slots):
        half = s // middle
        second = alone[s] & (odd[half] == 1)
        put(half * per_half + filled[half], waiting[half], s, 0, second)
        filled[half] = filled[half] + count(second)
        odd[half] = jnp.where(alone[s], 1 - odd[half], odd[half])
        waiting[half] = jnp.where(alone[s], s, waiting[half])
    mixed.append((waiting[0], waiting[1], 0, odd[0] == 1))
    for low, high, coupled, really in mixed:
        room = filled[0] < per_half
        unit = jnp.where(room, filled[0], per_half + filled[1])
        put(unit, jnp.where(room, low, high), jnp.where(room, high, low), coupled, really)
        filled[0] = filled[0] + count(really & room)
        filled[1] = filled[1] + count(really & jnp.logical_not(room))


def pack_kernel(
    per_half, rows_ref, cols_ref, counts_ref, down_ref, up_ref,
    out_ref, order_ref, flags_ref, first_ref, last_ref, sems,
):
    slots, owners = cols_ref.shape[2], counts_ref.shape[2]
    places, units = out_ref.shape[0], 2 * per_half
    copies = []
    used = [unit_place(unit, per_half, owners) for unit in range(units)]
    for which, x_ref in ((1, up_ref), (0, down_ref)):
        order_units(
            cols_ref, counts_ref, which, slots, per_half, order_ref, flags_ref, first_ref, last_ref
        )
        for i in range(2 * units):
            row = rows_ref[0, which, jnp.maximum(order_ref[which, i], 0)]
            at = pl.multiple_of(row * TILE, TILE)
            copy = pltpu.make_async_copy(
                x_ref.at[0, 0, :, pl.ds(at, TILE)],
                out_ref.at[used[i // 2], which, i % 2],
                sems.at[which, i],
            )
            copy.start()
            copies.append(copy)
    for place in range(places):
        if place not in used:
            out_ref[place] = jnp.zeros(out_ref.shape[1:], out_ref.dtype)
    for copy in copies:
        copy.wait()


def pack(x_down, x_up, tile_rows, tile_cols, counts, per_half, places):
    rows, units = x_down.shape[2], 2 * per_half
    smem = pl.BlockSpec(memory_space=pltpu.SMEM)
    vmem = pl.BlockSpec(memory_space=pltpu.VMEM)
    hbm = pl.BlockSpec(memory_space=pl.ANY)
    return pl.pallas_call(
        functools.partial(pack_kernel, per_half),
        out_shape=[
            jax.ShapeDtypeStruct((places, 2, 2, rows, TILE), x_down.dtype),
            jax.ShapeDtypeStruct((2, 2 * units + 2), jnp.int32),
            jax.ShapeDtypeStruct((2, 2 * units + 2), jnp.int32),
        ],
        in_specs=[smem, smem, smem, hbm, hbm],
        out_specs=[vmem, smem, smem],
        scratch_shapes=[
            pltpu.SMEM((COLUMNS + 1,), jnp.int32),
            pltpu.SMEM((COLUMNS + 1,), jnp.int32),
            pltpu.SemaphoreType.DMA((2, 2 * units)),
        ],
        cost_estimate=pl.CostEstimate(
            flops=0, bytes_accessed=16 * units * rows * TILE, transcendentals=0
        ),
    )(tile_rows, tile_cols, counts, x_down, x_up)


def swapped(array, apart):
    size = lax.axis_size("fsdp")
    return lax.ppermute(array, "fsdp", [(i, i ^ apart) for i in range(size)])


def near_at(slot, per_owner):
    owner = slot // per_owner
    other = jnp.where(owner % CORES == lax.axis_index("fsdp") % CORES, 0, per_owner)
    return other + slot - owner * per_owner


def far_kernel(per_half, order_ref, near_ref, own_ref, partner_ref):
    per_owner, owners = near_ref.shape[1] // CORES, 2 * CORES
    unit = unit_here(per_half, owners)
    asker = jnp.where(unit < per_half, unit + per_half, unit - per_half)
    at = [
        near_at(jnp.maximum(order_ref[which, 2 * asker + 1], 0), per_owner) for which in range(2)
    ]
    for half in range(own_ref.shape[0]):
        own_ref[half] = near_ref[0, at[0]]
    partner_ref[0] = near_ref[1, at[1]]


def far_weights(near, order, per_half, halves):
    vmem = pl.BlockSpec(memory_space=pltpu.VMEM)
    return pl.pallas_call(
        functools.partial(far_kernel, per_half),
        out_shape=[
            jax.ShapeDtypeStruct((halves,) + near.shape[2:], near.dtype),
            jax.ShapeDtypeStruct((1,) + near.shape[2:], near.dtype),
        ],
        in_specs=[pl.BlockSpec(memory_space=pltpu.SMEM), vmem],
        out_specs=[vmem, vmem],
        compiler_params=IN_VMEM,
        cost_estimate=pl.CostEstimate(flops=0, bytes_accessed=300_000, transcendentals=0),
    )(order, near)


def dot(a, b, over_a, over_b):
    return lax.dot_general(
        a, b, (((over_a,), (over_b,)), ((), ())), preferred_element_type=jnp.float32
    )


def grads_kernel(
    which, per_half, owners, loss_scale, order_ref, flags_ref, x_ref, near_ref, far_ref, out_ref,
    w_unit, first_sum, second_sum,
):
    sources, _, _, rows, _ = x_ref.shape
    per_owner = near_ref.shape[1] // CORES
    unit = unit_here(per_half, owners)
    half = lax.axis_index("fsdp") // CORES
    for i in range(2):
        slot = jnp.maximum(order_ref[which, 2 * unit + i], 0)
        near = slot // per_owner // CORES == half

        @pl.when(near)
        def _():
            w_unit[i] = near_ref[which, near_at(slot, per_owner)]

        @pl.when(jnp.logical_not(near))
        def _():
            w_unit[i] = far_ref[0 if far_ref.shape[0] == 1 else 1 - half]

    together = min(SOURCES_AT_ONCE, sources)
    steps = sources // together
    if steps > 1:
        first_sum[...] = jnp.zeros_like(first_sum)
        second_sum[...] = jnp.zeros_like(second_sum)

    def sum_up(total_ref, where, term):
        total_ref[where] = total_ref[where] + term if steps > 1 else term

    coupled = flags_ref[which, 2 * unit] == 1

    def read(step):
        at = step * together
        return [
            x_ref[pl.ds(at, together), which, i].reshape(together * rows, TILE) for i in range(2)
        ]

    @pl.when(coupled)
    def _():
        def go(step, carry):
            xs = jnp.concatenate(read(step), axis=1)
            firsts = jnp.concatenate([w_unit[0, 0], w_unit[1, 0]], axis=0)
            seconds = jnp.concatenate([w_unit[0, 1], w_unit[1, 1]], axis=1)
            value, slope = gelu_pair(dot(xs, firsts, 1, 0))
            active = value.astype(jnp.bfloat16)
            delta = dot(active, seconds, 1, 0)
            cotangent = (loss_scale * (xs.astype(jnp.float32) + delta)).astype(jnp.bfloat16)
            grad_act = dot(cotangent, seconds, 1, 1)
            grad_pre = (grad_act * slope).astype(jnp.bfloat16)
            sum_up(first_sum, ..., dot(xs, grad_pre, 0, 0))
            sum_up(second_sum, ..., dot(active, cotangent, 0, 0))
            return carry

        lax.fori_loop(0, steps, go, 0, unroll=min(steps, 4))

    @pl.when(jnp.logical_not(coupled))
    def _():
        def go(step, carry):
            for i, x in enumerate(read(step)):
                across = slice(i * TILE, (i + 1) * TILE)
                value, slope = gelu_pair(dot(x, w_unit[i, 0], 1, 0))
                active = value.astype(jnp.bfloat16)
                delta = dot(active, w_unit[i, 1], 1, 0)
                cotangent = (loss_scale * (x.astype(jnp.float32) + delta)).astype(jnp.bfloat16)
                grad_act = dot(cotangent, w_unit[i, 1], 1, 1)
                grad_pre = (grad_act * slope).astype(jnp.bfloat16)
                sum_up(first_sum, (across, slice(None)), dot(x, grad_pre, 0, 0))
                sum_up(second_sum, (slice(None), across), dot(active, cotangent, 0, 0))
            return carry

        lax.fori_loop(0, steps, go, 0, unroll=min(steps, 4))

    for i in range(2):
        across = slice(i * TILE, (i + 1) * TILE)
        out_ref[i, 0] = first_sum[across, :].astype(out_ref.dtype)
        out_ref[i, 1] = second_sum[:, across].astype(out_ref.dtype)


def unit_grads(which, blocks, near, far, order, flags, per_half, owners, loss_scale, dtype):
    sources, _, _, rows, _ = blocks.shape
    smem = pl.BlockSpec(memory_space=pltpu.SMEM)
    vmem = pl.BlockSpec(memory_space=pltpu.VMEM)
    return pl.pallas_call(
        functools.partial(grads_kernel, which, per_half, owners, loss_scale),
        out_shape=jax.ShapeDtypeStruct((2, 2, TILE, TILE), dtype),
        in_specs=[smem, smem, vmem, vmem, vmem],
        out_specs=vmem,
        scratch_shapes=[
            pltpu.VMEM((2, 2, TILE, TILE), jnp.bfloat16),
            pltpu.VMEM((2 * TILE, TILE), jnp.float32),
            pltpu.VMEM((TILE, 2 * TILE), jnp.float32),
        ],
        compiler_params=IN_VMEM,
        cost_estimate=pl.CostEstimate(
            flops=20 * sources * rows * TILE * TILE,
            bytes_accessed=4 * sources * rows * TILE,
            transcendentals=2 * sources * rows * TILE,
        ),
    )(order, flags, blocks, near, far)


def add_kernel(own_ref, arrived_ref, out_ref):
    total = (own_ref[...] + arrived_ref[...].astype(jnp.float32)).astype(out_ref.dtype)
    for copy in range(out_ref.shape[0]):
        out_ref[copy] = total


def add(own, arrived, copies):
    vmem = pl.BlockSpec(memory_space=pltpu.VMEM)
    return pl.pallas_call(
        add_kernel,
        out_shape=jax.ShapeDtypeStruct((copies,) + own.shape, jnp.bfloat16),
        in_specs=[vmem, vmem],
        out_specs=vmem,
        compiler_params=IN_VMEM,
        cost_estimate=pl.CostEstimate(flops=own.size, bytes_accessed=900_000, transcendentals=0),
    )(own, arrived)


def place_kernel(per_half, order_ref, counts_ref, same_ref, other_ref, out_ref, zeros, sems, zero_sems):
    owner, owners = lax.axis_index("fsdp"), counts_ref.shape[2]
    per_owner = out_ref.shape[0]
    zeros[...] = jnp.zeros_like(zeros)

    def each(act):
        for i in range(4 * per_half):
            at = order_ref[0, i] - owner * per_owner
            mine = (at >= 0) & (at < per_owner)
            place = unit_place(i // 2, per_half, owners)
            near = owner % CORES == place % CORES
            for grads_ref, where in ((same_ref, near), (other_ref, jnp.logical_not(near))):

                @pl.when(mine & where)
                def _():
                    act(
                        pltpu.make_async_copy(
                            grads_ref.at[place // CORES, i % 2], out_ref.at[at], sems.at[i]
                        )
                    )

        for slot in range(per_owner):

            @pl.when(counts_ref[0, 0, owner] <= slot)
            def _():
                act(pltpu.make_async_copy(zeros, out_ref.at[slot], zero_sems.at[slot]))

    each(lambda copy: copy.start())
    each(lambda copy: copy.wait())


def place(same, other, order, counts, per_half, per_owner):
    smem = pl.BlockSpec(memory_space=pltpu.SMEM)
    hbm = pl.BlockSpec(memory_space=pl.ANY)
    return pl.pallas_call(
        functools.partial(place_kernel, per_half),
        out_shape=jax.ShapeDtypeStruct((per_owner,) + same.shape[2:], same.dtype),
        in_specs=[smem, smem, hbm, hbm],
        out_specs=hbm,
        scratch_shapes=[
            pltpu.VMEM(same.shape[2:], same.dtype),
            pltpu.SemaphoreType.DMA((4 * per_half,)),
            pltpu.SemaphoreType.DMA((per_owner,)),
        ],
        compiler_params=IN_VMEM,
        cost_estimate=pl.CostEstimate(flops=0, bytes_accessed=1_000_000, transcendentals=0),
    )(order, counts, same, other)


def body(x_down, x_up, w_tiles, tile_rows, tile_cols, counts):
    rows_here = x_down.shape[2]
    slots, owners = tile_cols.shape[2], counts.shape[2]
    per_half = (live_total(slots, owners) // 2 + 1) // 2
    places = lax.axis_size("dp") * lax.axis_size("fsdp")
    sections = lax.axis_size("section")
    across = [(i, (i + sections // 2) % sections) for i in range(sections)]
    loss_scale = float(2 * rows_here * places) ** (-0.5)

    packed, order, flags = pack(x_down, x_up, tile_rows, tile_cols, counts, per_half, places)
    blocks = lax.all_to_all(packed, PLANE, split_axis=0, concat_axis=0, tiled=True)
    near = jnp.concatenate([w_tiles[0], swapped(w_tiles[0], 1)], axis=1)
    halves = owners // CORES
    far_own, far_partner = far_weights(near, order, per_half, halves)
    pairs = [[half * CORES + core for half in range(halves)] for core in range(CORES)]
    far_own = lax.all_to_all(
        far_own, "fsdp", split_axis=0, concat_axis=0, axis_index_groups=pairs, tiled=True
    )
    far_partner = swapped(far_partner, CORES)
    grads = functools.partial(
        unit_grads, blocks=blocks, near=near, order=order, flags=flags,
        per_half=per_half, owners=owners, loss_scale=loss_scale,
    )
    partner = grads(1, far=far_partner, dtype=jnp.bfloat16)
    arrived = lax.ppermute(partner, "section", across)
    mine = add(grads(0, far=far_own, dtype=jnp.float32), arrived, places // CORES)
    same_core = [
        [place for place in range(places) if place % CORES == core] for core in range(CORES)
    ]
    same = lax.all_to_all(
        mine, PLANE, split_axis=0, concat_axis=0, axis_index_groups=same_core, tiled=True
    )
    other = swapped(same, 1)
    return place(same, other, order, counts, per_half, slots // owners)[None]


def solution(mesh):
    in_specs = (
        P("section", "dp", "fsdp", None),
        P("section", "dp", "fsdp", None),
        P("section", None, "fsdp", None, None, None),
        P("section", None, None),
        P("section", None, None),
        P("section", None, None),
    )
    out_specs = P("section", "fsdp", None, None, None)
    return jax.shard_map(body, mesh=mesh, in_specs=in_specs, out_specs=out_specs, check_vma=False)
```

```python
import functools
import math

import jax
import jax.numpy as jnp
from jax import lax
from jax.experimental import pallas as pl
from jax.experimental.pallas import tpu as pltpu
from jax.sharding import PartitionSpec as P

TILE = 128
PLANE = ("dp", "fsdp")
SOURCES_AT_ONCE = 8
COLUMNS = 192
CORES = 2
BF16_ROWS = 16
IN_VMEM = pltpu.CompilerParams(vmem_limit_bytes=16 * 1024 * 1024)

tanh_scale = math.sqrt(2.0 / math.pi)
cubic_coef = 0.044715


def gelu_pair(hidden):
    square = hidden * hidden
    tangent = jnp.tanh(tanh_scale * (hidden + cubic_coef * hidden * square))
    half = 0.5 * (1.0 + tangent)
    value = hidden * half
    slope = half + 0.5 * hidden * (1.0 - tangent * tangent) * tanh_scale * (
        1.0 + 3.0 * cubic_coef * square
    )
    return (value, slope)


def live_total(slots, owners):
    cap = slots // owners
    return sum(cap - i * cap // owners for i in range(owners))


def unit_place(unit, per_half, owners):
    half, at = unit // per_half, unit % per_half
    return at // CORES * owners + half * CORES + at % CORES


def unit_here(per_half, owners):
    owner = lax.axis_index("fsdp")
    at = lax.axis_index("dp") * CORES + owner % CORES
    return owner // CORES * per_half + jnp.minimum(at, per_half - 1)


def order_units(
    cols_ref, counts_ref, which, slots, per_half, order_ref, flags_ref, first_ref, last_ref
):
    per_owner, middle, unused = slots // counts_ref.shape[2], slots // 2, 4 * per_half
    for i in range(order_ref.shape[1]):
        order_ref[which, i] = -1
        flags_ref[which, i] = 0
    cols = []
    for s in range(slots):
        living = counts_ref[0, which, s // per_owner] > s % per_owner
        cols.append(jnp.where(living, cols_ref[0, which, s], COLUMNS))
    for s in range(slots):
        last_ref[cols[s]] = s
        first_ref[cols[slots - 1 - s]] = slots - 1 - s
    filled = [jnp.int32(0), jnp.int32(0)]

    def put(unit, slot_a, slot_b, coupled, really):
        at = jnp.where(really, 2 * unit, unused)
        order_ref[which, at] = slot_a
        order_ref[which, at + 1] = slot_b
        flags_ref[which, at] = coupled

    count = lambda condition: jnp.where(condition, 1, 0)
    alone, mixed = [], []
    for s in range(slots):
        living = cols[s] < COLUMNS
        first, last = first_ref[cols[s]], last_ref[cols[s]]
        leads = living & (first == s) & (last > s)
        alone.append(living & (first == last))
        half = s // middle
        pure = leads & (last < (half + 1) * middle)
        put(half * per_half + filled[half], s, last, 1, pure)
        filled[half] = filled[half] + count(pure)
        if half == 0:
            mixed.append((s, last, 1, leads & (last >= middle)))
    waiting, odd = [jnp.int32(0), jnp.int32(0)], [jnp.int32(0), jnp.int32(0)]
    for s in range(slots):
        half = s // middle
        second = alone[s] & (odd[half] == 1)
        put(half * per_half + filled[half], waiting[half], s, 0, second)
        filled[half] = filled[half] + count(second)
        odd[half] = jnp.where(alone[s], 1 - odd[half], odd[half])
        waiting[half] = jnp.where(alone[s], s, waiting[half])
    mixed.append((waiting[0], waiting[1], 0, odd[0] == 1))
    for low, high, coupled, really in mixed:
        room = filled[0] < per_half
        unit = jnp.where(room, filled[0], per_half + filled[1])
        put(unit, jnp.where(room, low, high), jnp.where(room, high, low), coupled, really)
        filled[0] = filled[0] + count(really & room)
        filled[1] = filled[1] + count(really & jnp.logical_not(room))


def pick(which, per_half, owners, rows_ref, order_ref, x_ref, out_ref, sems):
    copies, used = [], [unit_place(unit, per_half, owners) for unit in range(2 * per_half)]
    for i in range(4 * per_half):
        row = rows_ref[0, which, jnp.maximum(order_ref[which, i], 0)]
        at = pl.multiple_of(row * TILE, TILE)
        copy = pltpu.make_async_copy(
            x_ref.at[0, 0, :, pl.ds(at, TILE)], out_ref.at[used[i // 2], i % 2], sems.at[i]
        )
        copy.start()
        copies.append(copy)
    for place in range(out_ref.shape[0]):
        if place not in used:
            out_ref[place] = jnp.zeros(out_ref.shape[1:], out_ref.dtype)
    return copies


def pack_up_kernel(
    per_half, rows_ref, cols_ref, counts_ref, x_ref,
    out_ref, order_ref, flags_ref, first_ref, last_ref, sems,
):
    slots, owners = cols_ref.shape[2], counts_ref.shape[2]
    tables = (order_ref, flags_ref, first_ref, last_ref)
    order_units(cols_ref, counts_ref, 1, slots, per_half, *tables)
    copies = pick(1, per_half, owners, rows_ref, order_ref, x_ref, out_ref, sems)
    order_units(cols_ref, counts_ref, 0, slots, per_half, *tables)
    for copy in copies:
        copy.wait()


def pack_up(x_up, tile_rows, tile_cols, counts, per_half, places):
    rows, units = x_up.shape[2], 2 * per_half
    smem = pl.BlockSpec(memory_space=pltpu.SMEM)
    vmem = pl.BlockSpec(memory_space=pltpu.VMEM)
    hbm = pl.BlockSpec(memory_space=pl.ANY)
    return pl.pallas_call(
        functools.partial(pack_up_kernel, per_half),
        out_shape=[
            jax.ShapeDtypeStruct((places, 2, rows, TILE), x_up.dtype),
            jax.ShapeDtypeStruct((2, 2 * units + 2), jnp.int32),
            jax.ShapeDtypeStruct((2, 2 * units + 2), jnp.int32),
        ],
        in_specs=[smem, smem, smem, hbm],
        out_specs=[vmem, smem, smem],
        scratch_shapes=[
            pltpu.SMEM((COLUMNS + 1,), jnp.int32),
            pltpu.SMEM((COLUMNS + 1,), jnp.int32),
            pltpu.SemaphoreType.DMA((2 * units,)),
        ],
        cost_estimate=pl.CostEstimate(
            flops=0, bytes_accessed=8 * units * rows * TILE, transcendentals=0
        ),
    )(tile_rows, tile_cols, counts, x_up)


def pack_down_kernel(per_half, owners, rows_ref, order_ref, x_ref, out_ref, sems):
    for copy in pick(0, per_half, owners, rows_ref, order_ref, x_ref, out_ref, sems):
        copy.wait()


def pack_down(x_down, tile_rows, order, per_half, owners, places):
    rows, units = x_down.shape[2], 2 * per_half
    smem = pl.BlockSpec(memory_space=pltpu.SMEM)
    return pl.pallas_call(
        functools.partial(pack_down_kernel, per_half, owners),
        out_shape=jax.ShapeDtypeStruct((places, 2, rows, TILE), x_down.dtype),
        in_specs=[smem, smem, pl.BlockSpec(memory_space=pl.ANY)],
        out_specs=pl.BlockSpec(memory_space=pltpu.VMEM),
        scratch_shapes=[pltpu.SemaphoreType.DMA((2 * units,))],
        cost_estimate=pl.CostEstimate(
            flops=0, bytes_accessed=8 * units * rows * TILE, transcendentals=0
        ),
    )(tile_rows, order, x_down)


def after(array, event):
    hbm = pl.BlockSpec(memory_space=pltpu.HBM)
    return pl.pallas_call(
        lambda array_ref, event_ref, out_ref: None,
        out_shape=jax.ShapeDtypeStruct(array.shape, array.dtype),
        in_specs=[hbm, pl.BlockSpec(memory_space=pl.ANY)],
        out_specs=hbm,
        input_output_aliases={0: 0},
        cost_estimate=pl.CostEstimate(flops=0, bytes_accessed=0, transcendentals=0),
    )(array, event)


def swapped(array, apart):
    size = lax.axis_size("fsdp")
    return lax.ppermute(array, "fsdp", [(i, i ^ apart) for i in range(size)])


def near_at(slot, per_owner):
    owner = slot // per_owner
    other = jnp.where(owner % CORES == lax.axis_index("fsdp") % CORES, 0, per_owner)
    return other + slot - owner * per_owner


def far_kernel(per_half, order_ref, near_ref, out_ref):
    per_owner, owners = near_ref.shape[1] // CORES, 2 * CORES
    unit = unit_here(per_half, owners)
    asker = jnp.where(unit < per_half, unit + per_half, unit - per_half)
    for which in range(2):
        slot = jnp.maximum(order_ref[which, 2 * asker + 1], 0)
        out_ref[which] = near_ref[which, near_at(slot, per_owner)]


def far_weights(near, order, per_half):
    vmem = pl.BlockSpec(memory_space=pltpu.VMEM)
    return pl.pallas_call(
        functools.partial(far_kernel, per_half),
        out_shape=jax.ShapeDtypeStruct(near.shape[:1] + near.shape[2:], near.dtype),
        in_specs=[pl.BlockSpec(memory_space=pltpu.SMEM), vmem],
        out_specs=vmem,
        compiler_params=IN_VMEM,
        cost_estimate=pl.CostEstimate(flops=0, bytes_accessed=300_000, transcendentals=0),
    )(order, near)


def dot(a, b, over_a, over_b):
    return lax.dot_general(
        a, b, (((over_a,), (over_b,)), ((), ())), preferred_element_type=jnp.float32
    )


def grads_kernel(
    which, per_half, owners, loss_scale, order_ref, flags_ref, x_ref, near_ref, far_ref, out_ref,
    w_unit, first_sum, second_sum,
):
    sources, _, rows, _ = x_ref.shape
    per_owner = near_ref.shape[1] // CORES
    unit = unit_here(per_half, owners)
    half = lax.axis_index("fsdp") // CORES
    for i in range(2):
        slot = jnp.maximum(order_ref[which, 2 * unit + i], 0)
        near = slot // per_owner // CORES == half

        @pl.when(near)
        def _():
            w_unit[i] = near_ref[which, near_at(slot, per_owner)]

        @pl.when(jnp.logical_not(near))
        def _():
            w_unit[i] = far_ref[which]

    together = min(SOURCES_AT_ONCE, sources)
    steps = sources // together
    if steps > 1:
        first_sum[...] = jnp.zeros_like(first_sum)
        second_sum[...] = jnp.zeros_like(second_sum)

    def sum_up(total_ref, where, term):
        total_ref[where] = total_ref[where] + term if steps > 1 else term

    coupled = flags_ref[which, 2 * unit] == 1

    def read(step):
        at = step * together
        return [
            x_ref[pl.ds(at, together), i].reshape(together * rows, TILE) for i in range(2)
        ]

    @pl.when(coupled)
    def _():
        def go(step, carry):
            xs = jnp.concatenate(read(step), axis=1)
            firsts = jnp.concatenate([w_unit[0, 0], w_unit[1, 0]], axis=0)
            seconds = jnp.concatenate([w_unit[0, 1], w_unit[1, 1]], axis=1)
            value, slope = gelu_pair(dot(xs, firsts, 1, 0))
            active = value.astype(jnp.bfloat16)
            delta = dot(active, seconds, 1, 0)
            cotangent = (loss_scale * (xs.astype(jnp.float32) + delta)).astype(jnp.bfloat16)
            grad_act = dot(cotangent, seconds, 1, 1)
            grad_pre = (grad_act * slope).astype(jnp.bfloat16)
            sum_up(first_sum, ..., dot(xs, grad_pre, 0, 0))
            sum_up(second_sum, ..., dot(active, cotangent, 0, 0))
            return carry

        lax.fori_loop(0, steps, go, 0, unroll=min(steps, 4))

    @pl.when(jnp.logical_not(coupled))
    def _():
        def go(step, carry):
            for i, x in enumerate(read(step)):
                across = slice(i * TILE, (i + 1) * TILE)
                value, slope = gelu_pair(dot(x, w_unit[i, 0], 1, 0))
                active = value.astype(jnp.bfloat16)
                delta = dot(active, w_unit[i, 1], 1, 0)
                cotangent = (loss_scale * (x.astype(jnp.float32) + delta)).astype(jnp.bfloat16)
                grad_act = dot(cotangent, w_unit[i, 1], 1, 1)
                grad_pre = (grad_act * slope).astype(jnp.bfloat16)
                sum_up(first_sum, (across, slice(None)), dot(x, grad_pre, 0, 0))
                sum_up(second_sum, (slice(None), across), dot(active, cotangent, 0, 0))
            return carry

        lax.fori_loop(0, steps, go, 0, unroll=min(steps, 4))

    for i in range(2):
        across = slice(i * TILE, (i + 1) * TILE)
        out_ref[i, 0] = first_sum[across, :].astype(out_ref.dtype)
        out_ref[i, 1] = second_sum[:, across].astype(out_ref.dtype)


def unit_grads(which, blocks, near, far, order, flags, per_half, owners, loss_scale, dtype):
    sources, _, rows, _ = blocks.shape
    smem = pl.BlockSpec(memory_space=pltpu.SMEM)
    vmem = pl.BlockSpec(memory_space=pltpu.VMEM)
    return pl.pallas_call(
        functools.partial(grads_kernel, which, per_half, owners, loss_scale),
        out_shape=jax.ShapeDtypeStruct((2, 2, TILE, TILE), dtype),
        in_specs=[smem, smem, vmem, vmem, vmem],
        out_specs=vmem,
        scratch_shapes=[
            pltpu.VMEM((2, 2, TILE, TILE), jnp.bfloat16),
            pltpu.VMEM((2 * TILE, TILE), jnp.float32),
            pltpu.VMEM((TILE, 2 * TILE), jnp.float32),
        ],
        compiler_params=IN_VMEM,
        cost_estimate=pl.CostEstimate(
            flops=20 * sources * rows * TILE * TILE,
            bytes_accessed=4 * sources * rows * TILE,
            transcendentals=2 * sources * rows * TILE,
        ),
    )(order, flags, blocks, near, far)


def add_kernel(own_ref, arrived_ref, out_ref):
    total = (own_ref[...] + arrived_ref[...].astype(jnp.float32)).astype(out_ref.dtype)
    for copy in range(out_ref.shape[0]):
        out_ref[copy] = total


def add(own, arrived, copies):
    vmem = pl.BlockSpec(memory_space=pltpu.VMEM)
    return pl.pallas_call(
        add_kernel,
        out_shape=jax.ShapeDtypeStruct((copies,) + own.shape, jnp.bfloat16),
        in_specs=[vmem, vmem],
        out_specs=vmem,
        compiler_params=IN_VMEM,
        cost_estimate=pl.CostEstimate(flops=own.size, bytes_accessed=900_000, transcendentals=0),
    )(own, arrived)


def place_kernel(per_half, order_ref, counts_ref, same_ref, other_ref, out_ref, zeros, sems, zero_sems):
    owner, owners = lax.axis_index("fsdp"), counts_ref.shape[2]
    per_owner = out_ref.shape[0]
    zeros[...] = jnp.zeros_like(zeros)

    def each(act):
        for i in range(4 * per_half):
            at = order_ref[0, i] - owner * per_owner
            mine = (at >= 0) & (at < per_owner)
            place = unit_place(i // 2, per_half, owners)
            near = owner % CORES == place % CORES
            for grads_ref, where in ((same_ref, near), (other_ref, jnp.logical_not(near))):

                @pl.when(mine & where)
                def _():
                    act(
                        pltpu.make_async_copy(
                            grads_ref.at[place // CORES, i % 2], out_ref.at[at], sems.at[i]
                        )
                    )

        for slot in range(per_owner):

            @pl.when(counts_ref[0, 0, owner] <= slot)
            def _():
                act(pltpu.make_async_copy(zeros, out_ref.at[slot], zero_sems.at[slot]))

    each(lambda copy: copy.start())
    each(lambda copy: copy.wait())


def place(same, other, order, counts, per_half, per_owner):
    smem = pl.BlockSpec(memory_space=pltpu.SMEM)
    hbm = pl.BlockSpec(memory_space=pl.ANY)
    return pl.pallas_call(
        functools.partial(place_kernel, per_half),
        out_shape=jax.ShapeDtypeStruct((per_owner,) + same.shape[2:], same.dtype),
        in_specs=[smem, smem, hbm, hbm],
        out_specs=hbm,
        scratch_shapes=[
            pltpu.VMEM(same.shape[2:], same.dtype),
            pltpu.SemaphoreType.DMA((4 * per_half,)),
            pltpu.SemaphoreType.DMA((per_owner,)),
        ],
        compiler_params=IN_VMEM,
        cost_estimate=pl.CostEstimate(flops=0, bytes_accessed=1_000_000, transcendentals=0),
    )(order, counts, same, other)


def body(x_down, x_up, w_tiles, tile_rows, tile_cols, counts):
    rows_here = x_down.shape[2]
    slots, owners = tile_cols.shape[2], counts.shape[2]
    per_half = (live_total(slots, owners) // 2 + 1) // 2
    places = lax.axis_size("dp") * lax.axis_size("fsdp")
    sections = lax.axis_size("section")
    across = [(i, (i + sections // 2) % sections) for i in range(sections)]
    loss_scale = float(2 * rows_here * places) ** (-0.5)

    trade = lambda packed: lax.all_to_all(packed, PLANE, split_axis=0, concat_axis=0, tiled=True)
    up, order, flags = pack_up(x_up, tile_rows, tile_cols, counts, per_half, places)
    up = trade(up)
    near = jnp.concatenate([w_tiles[0], swapped(w_tiles[0], 1)], axis=1)
    far = swapped(far_weights(near, order, per_half), CORES)
    down = pack_down(x_down, tile_rows, order, per_half, owners, places)
    down = trade(after(down, far[0, 0, :BF16_ROWS]))
    grads = functools.partial(
        unit_grads, near=near, far=far, order=order, flags=flags,
        per_half=per_half, owners=owners, loss_scale=loss_scale,
    )
    arrived = lax.ppermute(grads(1, up, dtype=jnp.bfloat16), "section", across)
    mine = add(grads(0, down, dtype=jnp.float32), arrived, places // CORES)
    same_core = [
        [place for place in range(places) if place % CORES == core] for core in range(CORES)
    ]
    same = lax.all_to_all(
        mine, PLANE, split_axis=0, concat_axis=0, axis_index_groups=same_core, tiled=True
    )
    other = swapped(same, 1)
    return place(same, other, order, counts, per_half, slots // owners)[None]


def solution(mesh):
    in_specs = (
        P("section", "dp", "fsdp", None),
        P("section", "dp", "fsdp", None),
        P("section", None, "fsdp", None, None, None),
        P("section", None, None),
        P("section", None, None),
        P("section", None, None),
    )
    out_specs = P("section", "fsdp", None, None, None)
    return jax.shard_map(body, mesh=mesh, in_specs=in_specs, out_specs=out_specs, check_vma=False)
```

```python
import functools
import math

import jax
import jax.numpy as jnp
from jax import lax
from jax.experimental import pallas as pl
from jax.experimental.pallas import tpu as pltpu
from jax.sharding import PartitionSpec as P

TILE = 128
PLANE = ("dp", "fsdp")
SOURCES_AT_ONCE = 8
COLUMNS = 192
CORES = 2
COUPLED = 64
IN_VMEM = pltpu.CompilerParams(vmem_limit_bytes=16 * 1024 * 1024)

tanh_scale = math.sqrt(2.0 / math.pi)
cubic_coef = 0.044715


def gelu_pair(hidden):
    square = hidden * hidden
    tangent = jnp.tanh(tanh_scale * (hidden + cubic_coef * hidden * square))
    half = 0.5 * (1.0 + tangent)
    value = hidden * half
    slope = half + 0.5 * hidden * (1.0 - tangent * tangent) * tanh_scale * (
        1.0 + 3.0 * cubic_coef * square
    )
    return (value, slope)


def live_total(slots, owners):
    cap = slots // owners
    return sum(cap - i * cap // owners for i in range(owners))


def unit_place(unit, per_half, owners):
    half, at = unit // per_half, unit % per_half
    return at // CORES * owners + half * CORES + at % CORES


def unit_here(per_half, owners):
    owner = lax.axis_index("fsdp")
    at = lax.axis_index("dp") * CORES + owner % CORES
    return owner // CORES * per_half + jnp.minimum(at, per_half - 1)


def order_units(
    cols_ref, counts_ref, which, slots, per_half, order_ref, first_ref, last_ref
):
    per_owner, middle, unused = slots // counts_ref.shape[2], slots // 2, 4 * per_half
    for i in range(unused):
        order_ref[which, i] = -1
    for owner in range(counts_ref.shape[2]):
        order_ref[which, unused + 2 + owner] = counts_ref[0, which, owner]
    cols = []
    for s in range(slots):
        living = counts_ref[0, which, s // per_owner] > s % per_owner
        cols.append(jnp.where(living, cols_ref[0, which, s], COLUMNS))
    for s in range(slots):
        last_ref[cols[s]] = s
        first_ref[cols[slots - 1 - s]] = slots - 1 - s
    filled = [jnp.int32(0), jnp.int32(0)]

    def put(unit, slot_a, slot_b, coupled, really):
        at = jnp.where(really, 2 * unit, unused)
        order_ref[which, at] = slot_a + coupled * COUPLED
        order_ref[which, at + 1] = slot_b

    count = lambda condition: jnp.where(condition, 1, 0)
    alone, mixed = [], []
    for s in range(slots):
        living = cols[s] < COLUMNS
        first, last = first_ref[cols[s]], last_ref[cols[s]]
        leads = living & (first == s) & (last > s)
        alone.append(living & (first == last))
        half = s // middle
        pure = leads & (last < (half + 1) * middle)
        put(half * per_half + filled[half], s, last, 1, pure)
        filled[half] = filled[half] + count(pure)
        if half == 0:
            mixed.append((s, last, 1, leads & (last >= middle)))
    waiting, odd = [jnp.int32(0), jnp.int32(0)], [jnp.int32(0), jnp.int32(0)]
    for s in range(slots):
        half = s // middle
        second = alone[s] & (odd[half] == 1)
        put(half * per_half + filled[half], waiting[half], s, 0, second)
        filled[half] = filled[half] + count(second)
        odd[half] = jnp.where(alone[s], 1 - odd[half], odd[half])
        waiting[half] = jnp.where(alone[s], s, waiting[half])
    mixed.append((waiting[0], waiting[1], 0, odd[0] == 1))
    for low, high, coupled, really in mixed:
        room = filled[0] < per_half
        unit = jnp.where(room, filled[0], per_half + filled[1])
        put(unit, jnp.where(room, low, high), jnp.where(room, high, low), coupled, really)
        filled[0] = filled[0] + count(really & room)
        filled[1] = filled[1] + count(really & jnp.logical_not(room))


def slot_in(order_ref, which, i):
    return jnp.maximum(order_ref[which, i], 0) % COUPLED


def pack_kernel(
    per_half, rows_ref, cols_ref, counts_ref, down_ref, up_ref,
    out_ref, order_ref, held, zeros, first_ref, last_ref, in_sems, out_sems, zero_sem,
):
    slots, owners = cols_ref.shape[2], counts_ref.shape[2]
    places, units = out_ref.shape[0], 2 * per_half
    used = [unit_place(unit, per_half, owners) for unit in range(units)]
    arriving, leaving = [], []
    for which, x_ref in ((1, up_ref), (0, down_ref)):
        order_units(cols_ref, counts_ref, which, slots, per_half, order_ref, first_ref, last_ref)
        for i in range(2 * units):
            row = rows_ref[0, which, slot_in(order_ref, which, i)]
            at = pl.multiple_of(row * TILE, TILE)
            copy = pltpu.make_async_copy(
                x_ref.at[0, 0, :, pl.ds(at, TILE)], held.at[which, i], in_sems.at[which, i]
            )
            copy.start()
            arriving.append((which, i, copy))
    for which, i, copy in arriving:
        copy.wait()
        onward = pltpu.make_async_copy(
            held.at[which, i], out_ref.at[used[i // 2], which, i % 2], out_sems.at[which, i]
        )
        onward.start()
        leaving.append(onward)
    if places > units:
        zeros[...] = jnp.zeros_like(zeros)
    for place in range(places):
        if place not in used:
            empty = pltpu.make_async_copy(zeros, out_ref.at[place], zero_sem)
            empty.start()
            empty.wait()
    for onward in leaving:
        onward.wait()


def pack(x_down, x_up, tile_rows, tile_cols, counts, per_half, places):
    rows, units = x_down.shape[2], 2 * per_half
    smem = pl.BlockSpec(memory_space=pltpu.SMEM)
    hbm = pl.BlockSpec(memory_space=pl.ANY)
    return pl.pallas_call(
        functools.partial(pack_kernel, per_half),
        out_shape=[
            jax.ShapeDtypeStruct((places, 2, 2, rows, TILE), x_down.dtype),
            jax.ShapeDtypeStruct((2, 2 * units + 2 + counts.shape[2]), jnp.int32),
        ],
        in_specs=[smem, smem, smem, hbm, hbm],
        out_specs=[hbm, smem],
        scratch_shapes=[
            pltpu.VMEM((2, 2 * units, rows, TILE), x_down.dtype),
            pltpu.VMEM((2, 2, rows, TILE), x_down.dtype),
            pltpu.SMEM((COLUMNS + 1,), jnp.int32),
            pltpu.SMEM((COLUMNS + 1,), jnp.int32),
            pltpu.SemaphoreType.DMA((2, 2 * units)),
            pltpu.SemaphoreType.DMA((2, 2 * units)),
            pltpu.SemaphoreType.DMA,
        ],
        cost_estimate=pl.CostEstimate(
            flops=0, bytes_accessed=16 * units * rows * TILE, transcendentals=0
        ),
    )(tile_rows, tile_cols, counts, x_down, x_up)


def swapped(array, apart):
    size = lax.axis_size("fsdp")
    return lax.ppermute(array, "fsdp", [(i, i ^ apart) for i in range(size)])


def near_at(slot, per_owner):
    owner = slot // per_owner
    other = jnp.where(owner % CORES == lax.axis_index("fsdp") % CORES, 0, per_owner)
    return other + slot - owner * per_owner


def far_kernel(per_half, order_ref, near_ref, out_ref):
    per_owner, owners = near_ref.shape[1] // CORES, 2 * CORES
    unit = unit_here(per_half, owners)
    asker = jnp.where(unit < per_half, unit + per_half, unit - per_half)
    for which in range(2):
        slot = slot_in(order_ref, which, 2 * asker + 1)
        out_ref[which] = near_ref[which, near_at(slot, per_owner)]


def far_weights(near, order, per_half):
    vmem = pl.BlockSpec(memory_space=pltpu.VMEM)
    return pl.pallas_call(
        functools.partial(far_kernel, per_half),
        out_shape=jax.ShapeDtypeStruct(near.shape[:1] + near.shape[2:], near.dtype),
        in_specs=[pl.BlockSpec(memory_space=pltpu.SMEM), vmem],
        out_specs=vmem,
        compiler_params=IN_VMEM,
        cost_estimate=pl.CostEstimate(flops=0, bytes_accessed=300_000, transcendentals=0),
    )(order, near)


def dot(a, b, over_a, over_b):
    return lax.dot_general(
        a, b, (((over_a,), (over_b,)), ((), ())), preferred_element_type=jnp.float32
    )


def grads_kernel(
    which, per_half, owners, loss_scale, order_ref, x_ref, near_ref, far_ref, out_ref,
    w_unit, first_sum, second_sum,
):
    sources, _, _, rows, _ = x_ref.shape
    per_owner = near_ref.shape[1] // CORES
    unit = unit_here(per_half, owners)
    half = lax.axis_index("fsdp") // CORES
    for i in range(2):
        slot = slot_in(order_ref, which, 2 * unit + i)
        near = slot // per_owner // CORES == half

        @pl.when(near)
        def _():
            w_unit[i] = near_ref[which, near_at(slot, per_owner)]

        @pl.when(jnp.logical_not(near))
        def _():
            w_unit[i] = far_ref[which]

    together = min(SOURCES_AT_ONCE, sources)
    steps = sources // together
    if steps > 1:
        first_sum[...] = jnp.zeros_like(first_sum)
        second_sum[...] = jnp.zeros_like(second_sum)

    def sum_up(total_ref, where, term):
        total_ref[where] = total_ref[where] + term if steps > 1 else term

    coupled = order_ref[which, 2 * unit] >= COUPLED

    def read(step):
        at = step * together
        return [
            x_ref[pl.ds(at, together), which, i].reshape(together * rows, TILE) for i in range(2)
        ]

    @pl.when(coupled)
    def _():
        def go(step, carry):
            xs = jnp.concatenate(read(step), axis=1)
            firsts = jnp.concatenate([w_unit[0, 0], w_unit[1, 0]], axis=0)
            seconds = jnp.concatenate([w_unit[0, 1], w_unit[1, 1]], axis=1)
            value, slope = gelu_pair(dot(xs, firsts, 1, 0))
            active = value.astype(jnp.bfloat16)
            delta = dot(active, seconds, 1, 0)
            cotangent = (loss_scale * (xs.astype(jnp.float32) + delta)).astype(jnp.bfloat16)
            grad_act = dot(cotangent, seconds, 1, 1)
            grad_pre = (grad_act * slope).astype(jnp.bfloat16)
            sum_up(first_sum, ..., dot(xs, grad_pre, 0, 0))
            sum_up(second_sum, ..., dot(active, cotangent, 0, 0))
            return carry

        lax.fori_loop(0, steps, go, 0, unroll=min(steps, 4))

    @pl.when(jnp.logical_not(coupled))
    def _():
        def go(step, carry):
            for i, x in enumerate(read(step)):
                across = slice(i * TILE, (i + 1) * TILE)
                value, slope = gelu_pair(dot(x, w_unit[i, 0], 1, 0))
                active = value.astype(jnp.bfloat16)
                delta = dot(active, w_unit[i, 1], 1, 0)
                cotangent = (loss_scale * (x.astype(jnp.float32) + delta)).astype(jnp.bfloat16)
                grad_act = dot(cotangent, w_unit[i, 1], 1, 1)
                grad_pre = (grad_act * slope).astype(jnp.bfloat16)
                sum_up(first_sum, (across, slice(None)), dot(x, grad_pre, 0, 0))
                sum_up(second_sum, (slice(None), across), dot(active, cotangent, 0, 0))
            return carry

        lax.fori_loop(0, steps, go, 0, unroll=min(steps, 4))

    for i in range(2):
        across = slice(i * TILE, (i + 1) * TILE)
        out_ref[i, 0] = first_sum[across, :].astype(out_ref.dtype)
        out_ref[i, 1] = second_sum[:, across].astype(out_ref.dtype)


def unit_grads(which, blocks, near, far, order, per_half, owners, loss_scale, dtype):
    sources, _, _, rows, _ = blocks.shape
    smem = pl.BlockSpec(memory_space=pltpu.SMEM)
    vmem = pl.BlockSpec(memory_space=pltpu.VMEM)
    return pl.pallas_call(
        functools.partial(grads_kernel, which, per_half, owners, loss_scale),
        out_shape=jax.ShapeDtypeStruct((2, 2, TILE, TILE), dtype),
        in_specs=[smem, vmem, vmem, vmem],
        out_specs=vmem,
        scratch_shapes=[
            pltpu.VMEM((2, 2, TILE, TILE), jnp.bfloat16),
            pltpu.VMEM((2 * TILE, TILE), jnp.float32),
            pltpu.VMEM((TILE, 2 * TILE), jnp.float32),
        ],
        compiler_params=IN_VMEM,
        cost_estimate=pl.CostEstimate(
            flops=20 * sources * rows * TILE * TILE,
            bytes_accessed=4 * sources * rows * TILE,
            transcendentals=2 * sources * rows * TILE,
        ),
    )(order, blocks, near, far)


def add_kernel(own_ref, arrived_ref, out_ref):
    total = (own_ref[...] + arrived_ref[...].astype(jnp.float32)).astype(out_ref.dtype)
    for copy in range(out_ref.shape[0]):
        out_ref[copy] = total


def add(own, arrived, copies):
    vmem = pl.BlockSpec(memory_space=pltpu.VMEM)
    return pl.pallas_call(
        add_kernel,
        out_shape=jax.ShapeDtypeStruct((copies,) + own.shape, jnp.bfloat16),
        in_specs=[vmem, vmem],
        out_specs=vmem,
        compiler_params=IN_VMEM,
        cost_estimate=pl.CostEstimate(flops=own.size, bytes_accessed=900_000, transcendentals=0),
    )(own, arrived)


def place_kernel(per_half, owners, order_ref, same_ref, other_ref, out_ref, zeros, sems, zero_sems):
    owner = lax.axis_index("fsdp")
    per_owner = out_ref.shape[0]
    zeros[...] = jnp.zeros_like(zeros)

    def each(act):
        for i in range(4 * per_half):
            at = slot_in(order_ref, 0, i) - owner * per_owner
            mine = (order_ref[0, i] >= 0) & (at >= 0) & (at < per_owner)
            place = unit_place(i // 2, per_half, owners)
            near = owner % CORES == place % CORES
            for grads_ref, where in ((same_ref, near), (other_ref, jnp.logical_not(near))):

                @pl.when(mine & where)
                def _():
                    act(
                        pltpu.make_async_copy(
                            grads_ref.at[place // CORES, i % 2], out_ref.at[at], sems.at[i]
                        )
                    )

        for slot in range(per_owner):

            @pl.when(order_ref[0, 4 * per_half + 2 + owner] <= slot)
            def _():
                act(pltpu.make_async_copy(zeros, out_ref.at[slot], zero_sems.at[slot]))

    each(lambda copy: copy.start())
    each(lambda copy: copy.wait())


def place(same, other, order, per_half, owners, per_owner):
    smem = pl.BlockSpec(memory_space=pltpu.SMEM)
    hbm = pl.BlockSpec(memory_space=pl.ANY)
    return pl.pallas_call(
        functools.partial(place_kernel, per_half, owners),
        out_shape=jax.ShapeDtypeStruct((per_owner,) + same.shape[2:], same.dtype),
        in_specs=[smem, hbm, hbm],
        out_specs=hbm,
        scratch_shapes=[
            pltpu.VMEM(same.shape[2:], same.dtype),
            pltpu.SemaphoreType.DMA((4 * per_half,)),
            pltpu.SemaphoreType.DMA((per_owner,)),
        ],
        compiler_params=IN_VMEM,
        cost_estimate=pl.CostEstimate(flops=0, bytes_accessed=1_000_000, transcendentals=0),
    )(order, same, other)


def body(x_down, x_up, w_tiles, tile_rows, tile_cols, counts):
    rows_here = x_down.shape[2]
    slots, owners = tile_cols.shape[2], counts.shape[2]
    per_half = (live_total(slots, owners) // 2 + 1) // 2
    places = lax.axis_size("dp") * lax.axis_size("fsdp")
    sections = lax.axis_size("section")
    across = [(i, (i + sections // 2) % sections) for i in range(sections)]
    loss_scale = float(2 * rows_here * places) ** (-0.5)

    packed, order = pack(x_down, x_up, tile_rows, tile_cols, counts, per_half, places)
    blocks = lax.all_to_all(packed, PLANE, split_axis=0, concat_axis=0, tiled=True)
    near = jnp.concatenate([w_tiles[0], swapped(w_tiles[0], 1)], axis=1)
    far = swapped(far_weights(near, order, per_half), CORES)
    grads = functools.partial(
        unit_grads, blocks=blocks, near=near, far=far, order=order,
        per_half=per_half, owners=owners, loss_scale=loss_scale,
    )
    arrived = lax.ppermute(grads(1, dtype=jnp.bfloat16), "section", across)
    mine = add(grads(0, dtype=jnp.float32), arrived, places // CORES)
    same_core = [
        [place for place in range(places) if place % CORES == core] for core in range(CORES)
    ]
    same = lax.all_to_all(
        mine, PLANE, split_axis=0, concat_axis=0, axis_index_groups=same_core, tiled=True
    )
    other = swapped(same, 1)
    return place(same, other, order, per_half, owners, slots // owners)[None]


def solution(mesh):
    in_specs = (
        P("section", "dp", "fsdp", None),
        P("section", "dp", "fsdp", None),
        P("section", None, "fsdp", None, None, None),
        P("section", None, None),
        P("section", None, None),
        P("section", None, None),
    )
    out_specs = P("section", "fsdp", None, None, None)
    return jax.shard_map(body, mesh=mesh, in_specs=in_specs, out_specs=out_specs, check_vma=False)
```

```python
import functools
import math

import jax
import jax.numpy as jnp
from jax import lax
from jax.experimental import pallas as pl
from jax.experimental.pallas import tpu as pltpu
from jax.sharding import PartitionSpec as P

TILE = 128
PLANE = ("dp", "fsdp")
SOURCES_AT_ONCE = 8
COLUMNS = 192
CORES = 2
COPIES = 4
IN_VMEM = pltpu.CompilerParams(vmem_limit_bytes=16 * 1024 * 1024)

tanh_scale = math.sqrt(2.0 / math.pi)
cubic_coef = 0.044715


def gelu_pair(hidden):
    square = hidden * hidden
    tangent = jnp.tanh(tanh_scale * (hidden + cubic_coef * hidden * square))
    half = 0.5 * (1.0 + tangent)
    value = hidden * half
    slope = half + 0.5 * hidden * (1.0 - tangent * tangent) * tanh_scale * (
        1.0 + 3.0 * cubic_coef * square
    )
    return (value, slope)


def live_total(slots, owners):
    cap = slots // owners
    return sum(cap - i * cap // owners for i in range(owners))


def unit_place(unit, per_half, owners):
    half, at = unit // per_half, unit % per_half
    return at // CORES * owners + half * CORES + at % CORES


def unit_here(per_half, owners):
    owner = lax.axis_index("fsdp")
    at = lax.axis_index("dp") * CORES + owner % CORES
    return owner // CORES * per_half + jnp.minimum(at, per_half - 1)


def order_units(
    cols_ref, counts_ref, which, slots, per_half, order_ref, flags_ref, first_ref, last_ref
):
    per_owner, middle, unused = slots // counts_ref.shape[2], slots // 2, 4 * per_half
    for i in range(order_ref.shape[1]):
        order_ref[which, i] = -1
        flags_ref[which, i] = 0
    cols = []
    for s in range(slots):
        living = counts_ref[0, which, s // per_owner] > s % per_owner
        cols.append(jnp.where(living, cols_ref[0, which, s], COLUMNS))
    for s in range(slots):
        last_ref[cols[s]] = s
        first_ref[cols[slots - 1 - s]] = slots - 1 - s
    filled = [jnp.int32(0), jnp.int32(0)]

    def put(unit, slot_a, slot_b, coupled, really):
        at = jnp.where(really, 2 * unit, unused)
        order_ref[which, at] = slot_a
        order_ref[which, at + 1] = slot_b
        flags_ref[which, at] = coupled

    count = lambda condition: jnp.where(condition, 1, 0)
    alone, mixed = [], []
    for s in range(slots):
        living = cols[s] < COLUMNS
        first, last = first_ref[cols[s]], last_ref[cols[s]]
        leads = living & (first == s) & (last > s)
        alone.append(living & (first == last))
        half = s // middle
        pure = leads & (last < (half + 1) * middle)
        put(half * per_half + filled[half], s, last, 1, pure)
        filled[half] = filled[half] + count(pure)
        if half == 0:
            mixed.append((s, last, 1, leads & (last >= middle)))
    waiting, odd = [jnp.int32(0), jnp.int32(0)], [jnp.int32(0), jnp.int32(0)]
    for s in range(slots):
        half = s // middle
        second = alone[s] & (odd[half] == 1)
        put(half * per_half + filled[half], waiting[half], s, 0, second)
        filled[half] = filled[half] + count(second)
        odd[half] = jnp.where(alone[s], 1 - odd[half], odd[half])
        waiting[half] = jnp.where(alone[s], s, waiting[half])
    mixed.append((waiting[0], waiting[1], 0, odd[0] == 1))
    for low, high, coupled, really in mixed:
        room = filled[0] < per_half
        unit = jnp.where(room, filled[0], per_half + filled[1])
        put(unit, jnp.where(room, low, high), jnp.where(room, high, low), coupled, really)
        filled[0] = filled[0] + count(really & room)
        filled[1] = filled[1] + count(really & jnp.logical_not(room))


def pack_kernel(
    per_half, rows_ref, cols_ref, counts_ref, down_ref, up_ref,
    out_ref, order_ref, flags_ref, whole, first_ref, last_ref, sems,
):
    slots, owners = cols_ref.shape[2], counts_ref.shape[2]
    places, units, rows = out_ref.shape[0], 2 * per_half, whole.shape[1]
    pieces = sems.shape[1]
    copies = []
    for which, x_ref in ((0, down_ref), (1, up_ref)):
        for piece in range(pieces):
            part = pl.ds(piece * (rows // pieces), rows // pieces)
            copy = pltpu.make_async_copy(
                x_ref.at[0, 0, part], whole.at[which, part], sems.at[which, piece]
            )
            copy.start()
            copies.append(copy)
    for which in range(2):
        order_units(
            cols_ref, counts_ref, which, slots, per_half, order_ref, flags_ref, first_ref, last_ref
        )
    used = [unit_place(unit, per_half, owners) for unit in range(units)]
    for place in range(places):
        if place not in used:
            out_ref[place] = jnp.zeros(out_ref.shape[1:], out_ref.dtype)
    for which in range(2):
        for copy in copies[which * pieces : (which + 1) * pieces]:
            copy.wait()
        for i in range(2 * units):
            row = rows_ref[0, which, jnp.maximum(order_ref[which, i], 0)]
            at = pl.multiple_of(row * TILE, TILE)
            out_ref[used[i // 2], which, i % 2] = whole[which, :, pl.ds(at, TILE)]


def pack(x_down, x_up, tile_rows, tile_cols, counts, per_half, places):
    rows, units = x_down.shape[2], 2 * per_half
    smem = pl.BlockSpec(memory_space=pltpu.SMEM)
    vmem = pl.BlockSpec(memory_space=pltpu.VMEM)
    hbm = pl.BlockSpec(memory_space=pl.ANY)
    return pl.pallas_call(
        functools.partial(pack_kernel, per_half),
        out_shape=[
            jax.ShapeDtypeStruct((places, 2, 2, rows, TILE), x_down.dtype),
            jax.ShapeDtypeStruct((2, 2 * units + 2), jnp.int32),
            jax.ShapeDtypeStruct((2, 2 * units + 2), jnp.int32),
        ],
        in_specs=[smem, smem, smem, hbm, hbm],
        out_specs=[vmem, smem, smem],
        scratch_shapes=[
            pltpu.VMEM((2,) + x_down.shape[2:], x_down.dtype),
            pltpu.SMEM((COLUMNS + 1,), jnp.int32),
            pltpu.SMEM((COLUMNS + 1,), jnp.int32),
            pltpu.SemaphoreType.DMA((2, COPIES)),
        ],
        cost_estimate=pl.CostEstimate(
            flops=0, bytes_accessed=4 * x_down.size + 16 * units * rows * TILE, transcendentals=0
        ),
    )(tile_rows, tile_cols, counts, x_down, x_up)


def swapped(array, apart):
    size = lax.axis_size("fsdp")
    return lax.ppermute(array, "fsdp", [(i, i ^ apart) for i in range(size)])


def near_at(slot, per_owner):
    owner = slot // per_owner
    other = jnp.where(owner % CORES == lax.axis_index("fsdp") % CORES, 0, per_owner)
    return other + slot - owner * per_owner


def far_kernel(per_half, order_ref, near_ref, out_ref):
    per_owner, owners = near_ref.shape[1] // CORES, 2 * CORES
    unit = unit_here(per_half, owners)
    asker = jnp.where(unit < per_half, unit + per_half, unit - per_half)
    for which in range(2):
        slot = jnp.maximum(order_ref[which, 2 * asker + 1], 0)
        out_ref[which] = near_ref[which, near_at(slot, per_owner)]


def far_weights(near, order, per_half):
    vmem = pl.BlockSpec(memory_space=pltpu.VMEM)
    return pl.pallas_call(
        functools.partial(far_kernel, per_half),
        out_shape=jax.ShapeDtypeStruct(near.shape[:1] + near.shape[2:], near.dtype),
        in_specs=[pl.BlockSpec(memory_space=pltpu.SMEM), vmem],
        out_specs=vmem,
        compiler_params=IN_VMEM,
        cost_estimate=pl.CostEstimate(flops=0, bytes_accessed=300_000, transcendentals=0),
    )(order, near)


def dot(a, b, over_a, over_b):
    return lax.dot_general(
        a, b, (((over_a,), (over_b,)), ((), ())), preferred_element_type=jnp.float32
    )


def grads_kernel(
    which, per_half, owners, loss_scale, order_ref, flags_ref, x_ref, near_ref, far_ref, out_ref,
    w_unit, first_sum, second_sum,
):
    sources, _, _, rows, _ = x_ref.shape
    per_owner = near_ref.shape[1] // CORES
    unit = unit_here(per_half, owners)
    half = lax.axis_index("fsdp") // CORES
    for i in range(2):
        slot = jnp.maximum(order_ref[which, 2 * unit + i], 0)
        near = slot // per_owner // CORES == half

        @pl.when(near)
        def _():
            w_unit[i] = near_ref[which, near_at(slot, per_owner)]

        @pl.when(jnp.logical_not(near))
        def _():
            w_unit[i] = far_ref[which]

    together = min(SOURCES_AT_ONCE, sources)
    steps = sources // together
    if steps > 1:
        first_sum[...] = jnp.zeros_like(first_sum)
        second_sum[...] = jnp.zeros_like(second_sum)

    def sum_up(total_ref, where, term):
        total_ref[where] = total_ref[where] + term if steps > 1 else term

    coupled = flags_ref[which, 2 * unit] == 1

    def read(step):
        at = step * together
        return [
            x_ref[pl.ds(at, together), which, i].reshape(together * rows, TILE) for i in range(2)
        ]

    @pl.when(coupled)
    def _():
        def go(step, carry):
            xs = jnp.concatenate(read(step), axis=1)
            firsts = jnp.concatenate([w_unit[0, 0], w_unit[1, 0]], axis=0)
            seconds = jnp.concatenate([w_unit[0, 1], w_unit[1, 1]], axis=1)
            value, slope = gelu_pair(dot(xs, firsts, 1, 0))
            active = value.astype(jnp.bfloat16)
            delta = dot(active, seconds, 1, 0)
            cotangent = (loss_scale * (xs.astype(jnp.float32) + delta)).astype(jnp.bfloat16)
            grad_act = dot(cotangent, seconds, 1, 1)
            grad_pre = (grad_act * slope).astype(jnp.bfloat16)
            sum_up(first_sum, ..., dot(xs, grad_pre, 0, 0))
            sum_up(second_sum, ..., dot(active, cotangent, 0, 0))
            return carry

        lax.fori_loop(0, steps, go, 0, unroll=min(steps, 4))

    @pl.when(jnp.logical_not(coupled))
    def _():
        def go(step, carry):
            for i, x in enumerate(read(step)):
                across = slice(i * TILE, (i + 1) * TILE)
                value, slope = gelu_pair(dot(x, w_unit[i, 0], 1, 0))
                active = value.astype(jnp.bfloat16)
                delta = dot(active, w_unit[i, 1], 1, 0)
                cotangent = (loss_scale * (x.astype(jnp.float32) + delta)).astype(jnp.bfloat16)
                grad_act = dot(cotangent, w_unit[i, 1], 1, 1)
                grad_pre = (grad_act * slope).astype(jnp.bfloat16)
                sum_up(first_sum, (across, slice(None)), dot(x, grad_pre, 0, 0))
                sum_up(second_sum, (slice(None), across), dot(active, cotangent, 0, 0))
            return carry

        lax.fori_loop(0, steps, go, 0, unroll=min(steps, 4))

    for i in range(2):
        across = slice(i * TILE, (i + 1) * TILE)
        out_ref[i, 0] = first_sum[across, :].astype(out_ref.dtype)
        out_ref[i, 1] = second_sum[:, across].astype(out_ref.dtype)


def unit_grads(which, blocks, near, far, order, flags, per_half, owners, loss_scale, dtype):
    sources, _, _, rows, _ = blocks.shape
    smem = pl.BlockSpec(memory_space=pltpu.SMEM)
    vmem = pl.BlockSpec(memory_space=pltpu.VMEM)
    return pl.pallas_call(
        functools.partial(grads_kernel, which, per_half, owners, loss_scale),
        out_shape=jax.ShapeDtypeStruct((2, 2, TILE, TILE), dtype),
        in_specs=[smem, smem, vmem, vmem, vmem],
        out_specs=vmem,
        scratch_shapes=[
            pltpu.VMEM((2, 2, TILE, TILE), jnp.bfloat16),
            pltpu.VMEM((2 * TILE, TILE), jnp.float32),
            pltpu.VMEM((TILE, 2 * TILE), jnp.float32),
        ],
        compiler_params=IN_VMEM,
        cost_estimate=pl.CostEstimate(
            flops=20 * sources * rows * TILE * TILE,
            bytes_accessed=4 * sources * rows * TILE,
            transcendentals=2 * sources * rows * TILE,
        ),
    )(order, flags, blocks, near, far)


def add_kernel(own_ref, arrived_ref, out_ref):
    total = (own_ref[...] + arrived_ref[...].astype(jnp.float32)).astype(out_ref.dtype)
    for copy in range(out_ref.shape[0]):
        out_ref[copy] = total


def add(own, arrived, copies):
    vmem = pl.BlockSpec(memory_space=pltpu.VMEM)
    return pl.pallas_call(
        add_kernel,
        out_shape=jax.ShapeDtypeStruct((copies,) + own.shape, jnp.bfloat16),
        in_specs=[vmem, vmem],
        out_specs=vmem,
        compiler_params=IN_VMEM,
        cost_estimate=pl.CostEstimate(flops=own.size, bytes_accessed=900_000, transcendentals=0),
    )(own, arrived)


def place_kernel(per_half, order_ref, counts_ref, same_ref, other_ref, out_ref, zeros, sems, zero_sems):
    owner, owners = lax.axis_index("fsdp"), counts_ref.shape[2]
    per_owner = out_ref.shape[0]
    zeros[...] = jnp.zeros_like(zeros)

    def each(act):
        for i in range(4 * per_half):
            at = order_ref[0, i] - owner * per_owner
            mine = (at >= 0) & (at < per_owner)
            place = unit_place(i // 2, per_half, owners)
            near = owner % CORES == place % CORES
            for grads_ref, where in ((same_ref, near), (other_ref, jnp.logical_not(near))):

                @pl.when(mine & where)
                def _():
                    act(
                        pltpu.make_async_copy(
                            grads_ref.at[place // CORES, i % 2], out_ref.at[at], sems.at[i]
                        )
                    )

        for slot in range(per_owner):

            @pl.when(counts_ref[0, 0, owner] <= slot)
            def _():
                act(pltpu.make_async_copy(zeros, out_ref.at[slot], zero_sems.at[slot]))

    each(lambda copy: copy.start())
    each(lambda copy: copy.wait())


def place(same, other, order, counts, per_half, per_owner):
    smem = pl.BlockSpec(memory_space=pltpu.SMEM)
    hbm = pl.BlockSpec(memory_space=pl.ANY)
    return pl.pallas_call(
        functools.partial(place_kernel, per_half),
        out_shape=jax.ShapeDtypeStruct((per_owner,) + same.shape[2:], same.dtype),
        in_specs=[smem, smem, hbm, hbm],
        out_specs=hbm,
        scratch_shapes=[
            pltpu.VMEM(same.shape[2:], same.dtype),
            pltpu.SemaphoreType.DMA((4 * per_half,)),
            pltpu.SemaphoreType.DMA((per_owner,)),
        ],
        compiler_params=IN_VMEM,
        cost_estimate=pl.CostEstimate(flops=0, bytes_accessed=1_000_000, transcendentals=0),
    )(order, counts, same, other)


def body(x_down, x_up, w_tiles, tile_rows, tile_cols, counts):
    rows_here = x_down.shape[2]
    slots, owners = tile_cols.shape[2], counts.shape[2]
    per_half = (live_total(slots, owners) // 2 + 1) // 2
    places = lax.axis_size("dp") * lax.axis_size("fsdp")
    sections = lax.axis_size("section")
    across = [(i, (i + sections // 2) % sections) for i in range(sections)]
    loss_scale = float(2 * rows_here * places) ** (-0.5)

    packed, order, flags = pack(x_down, x_up, tile_rows, tile_cols, counts, per_half, places)
    blocks = lax.all_to_all(packed, PLANE, split_axis=0, concat_axis=0, tiled=True)
    near = jnp.concatenate([w_tiles[0], swapped(w_tiles[0], 1)], axis=1)
    far = swapped(far_weights(near, order, per_half), CORES)
    grads = functools.partial(
        unit_grads, blocks=blocks, near=near, far=far, order=order, flags=flags,
        per_half=per_half, owners=owners, loss_scale=loss_scale,
    )
    arrived = lax.ppermute(grads(1, dtype=jnp.bfloat16), "section", across)
    mine = add(grads(0, dtype=jnp.float32), arrived, places // CORES)
    same_core = [
        [place for place in range(places) if place % CORES == core] for core in range(CORES)
    ]
    same = lax.all_to_all(
        mine, PLANE, split_axis=0, concat_axis=0, axis_index_groups=same_core, tiled=True
    )
    other = swapped(same, 1)
    return place(same, other, order, counts, per_half, slots // owners)[None]


def solution(mesh):
    in_specs = (
        P("section", "dp", "fsdp", None),
        P("section", "dp", "fsdp", None),
        P("section", None, "fsdp", None, None, None),
        P("section", None, None),
        P("section", None, None),
        P("section", None, None),
    )
    out_specs = P("section", "fsdp", None, None, None)
    return jax.shard_map(body, mesh=mesh, in_specs=in_specs, out_specs=out_specs, check_vma=False)
```

```python
import functools
import itertools
import math

import jax
import jax.numpy as jnp
from jax import lax
from jax.experimental import pallas as pl
from jax.experimental.pallas import tpu as pltpu
from jax.sharding import PartitionSpec as P

TILE = 128
PLANE = ("dp", "fsdp")
SOURCES_AT_ONCE = 8
COLUMNS = 192
CORES = 2
COPIES = 4
IN_VMEM = pltpu.CompilerParams(vmem_limit_bytes=16 * 1024 * 1024)

tanh_scale = math.sqrt(2.0 / math.pi)
cubic_coef = 0.044715


def gelu_pair(hidden):
    square = hidden * hidden
    tangent = jnp.tanh(tanh_scale * (hidden + cubic_coef * hidden * square))
    half = 0.5 * (1.0 + tangent)
    value = hidden * half
    slope = half + 0.5 * hidden * (1.0 - tangent * tangent) * tanh_scale * (
        1.0 + 3.0 * cubic_coef * square
    )
    return (value, slope)


def live_total(slots, owners):
    cap = slots // owners
    return sum(cap - i * cap // owners for i in range(owners))


def unit_place(unit, per_half, owners):
    half, at = unit // per_half, unit % per_half
    return at // CORES * owners + half * CORES + at % CORES


def unit_here(per_half, owners):
    owner = lax.axis_index("fsdp")
    at = lax.axis_index("dp") * CORES + owner % CORES
    return owner // CORES * per_half + jnp.minimum(at, per_half - 1)


def order_units(
    cols_ref, counts_ref, which, slots, per_half, order_ref, flags_ref, first_ref, last_ref
):
    per_owner, middle, unused = slots // counts_ref.shape[2], slots // 2, 4 * per_half
    for i in range(order_ref.shape[1]):
        order_ref[which, i] = -1
        flags_ref[which, i] = 0
    cols = []
    for s in range(slots):
        living = counts_ref[0, which, s // per_owner] > s % per_owner
        cols.append(jnp.where(living, cols_ref[0, which, s], COLUMNS))
    yield
    for s in range(slots):
        last_ref[cols[s]] = s
        first_ref[cols[slots - 1 - s]] = slots - 1 - s
    yield
    filled = [jnp.int32(0), jnp.int32(0)]

    def put(unit, slot_a, slot_b, coupled, really):
        at = jnp.where(really, 2 * unit, unused)
        order_ref[which, at] = slot_a
        order_ref[which, at + 1] = slot_b
        flags_ref[which, at] = coupled

    count = lambda condition: jnp.where(condition, 1, 0)
    alone, mixed = [], []
    for s in range(slots):
        living = cols[s] < COLUMNS
        first, last = first_ref[cols[s]], last_ref[cols[s]]
        leads = living & (first == s) & (last > s)
        alone.append(living & (first == last))
        half = s // middle
        pure = leads & (last < (half + 1) * middle)
        put(half * per_half + filled[half], s, last, 1, pure)
        filled[half] = filled[half] + count(pure)
        if half == 0:
            mixed.append((s, last, 1, leads & (last >= middle)))
        yield
    waiting, odd = [jnp.int32(0), jnp.int32(0)], [jnp.int32(0), jnp.int32(0)]
    for s in range(slots):
        half = s // middle
        second = alone[s] & (odd[half] == 1)
        put(half * per_half + filled[half], waiting[half], s, 0, second)
        filled[half] = filled[half] + count(second)
        odd[half] = jnp.where(alone[s], 1 - odd[half], odd[half])
        waiting[half] = jnp.where(alone[s], s, waiting[half])
        yield
    mixed.append((waiting[0], waiting[1], 0, odd[0] == 1))
    for low, high, coupled, really in mixed:
        room = filled[0] < per_half
        unit = jnp.where(room, filled[0], per_half + filled[1])
        put(unit, jnp.where(room, low, high), jnp.where(room, high, low), coupled, really)
        filled[0] = filled[0] + count(really & room)
        filled[1] = filled[1] + count(really & jnp.logical_not(room))
        yield


def pack_kernel(
    per_half, rows_ref, cols_ref, counts_ref, down_ref, up_ref,
    out_ref, order_ref, flags_ref, whole, first_a, last_a, first_b, last_b, sems,
):
    slots, owners = cols_ref.shape[2], counts_ref.shape[2]
    places, units, rows = out_ref.shape[0], 2 * per_half, whole.shape[1]
    pieces = sems.shape[1]
    copies = []
    for which, x_ref in ((0, down_ref), (1, up_ref)):
        for piece in range(pieces):
            part = pl.ds(piece * (rows // pieces), rows // pieces)
            copy = pltpu.make_async_copy(
                x_ref.at[0, 0, part], whole.at[which, part], sems.at[which, piece]
            )
            copy.start()
            copies.append(copy)
    steps = [
        order_units(cols_ref, counts_ref, which, slots, per_half, order_ref, flags_ref, *tables)
        for which, tables in enumerate(((first_a, last_a), (first_b, last_b)))
    ]
    for _ in itertools.zip_longest(*steps):
        pass
    used = [unit_place(unit, per_half, owners) for unit in range(units)]
    for place in range(places):
        if place not in used:
            out_ref[place] = jnp.zeros(out_ref.shape[1:], out_ref.dtype)
    for which in range(2):
        for copy in copies[which * pieces : (which + 1) * pieces]:
            copy.wait()
        for i in range(2 * units):
            row = rows_ref[0, which, jnp.maximum(order_ref[which, i], 0)]
            at = pl.multiple_of(row * TILE, TILE)
            out_ref[used[i // 2], which, i % 2] = whole[which, :, pl.ds(at, TILE)]


def pack(x_down, x_up, tile_rows, tile_cols, counts, per_half, places):
    rows, units = x_down.shape[2], 2 * per_half
    smem = pl.BlockSpec(memory_space=pltpu.SMEM)
    vmem = pl.BlockSpec(memory_space=pltpu.VMEM)
    hbm = pl.BlockSpec(memory_space=pl.ANY)
    return pl.pallas_call(
        functools.partial(pack_kernel, per_half),
        out_shape=[
            jax.ShapeDtypeStruct((places, 2, 2, rows, TILE), x_down.dtype),
            jax.ShapeDtypeStruct((2, 2 * units + 2), jnp.int32),
            jax.ShapeDtypeStruct((2, 2 * units + 2), jnp.int32),
        ],
        in_specs=[smem, smem, smem, hbm, hbm],
        out_specs=[vmem, smem, smem],
        scratch_shapes=[
            pltpu.VMEM((2,) + x_down.shape[2:], x_down.dtype),
            *[pltpu.SMEM((COLUMNS + 1,), jnp.int32)] * 4,
            pltpu.SemaphoreType.DMA((2, COPIES)),
        ],
        cost_estimate=pl.CostEstimate(
            flops=0, bytes_accessed=4 * x_down.size + 16 * units * rows * TILE, transcendentals=0
        ),
    )(tile_rows, tile_cols, counts, x_down, x_up)


def swapped(array, apart):
    size = lax.axis_size("fsdp")
    return lax.ppermute(array, "fsdp", [(i, i ^ apart) for i in range(size)])


def near_at(slot, per_owner):
    owner = slot // per_owner
    other = jnp.where(owner % CORES == lax.axis_index("fsdp") % CORES, 0, per_owner)
    return other + slot - owner * per_owner


def far_kernel(per_half, order_ref, near_ref, out_ref):
    per_owner, owners = near_ref.shape[1] // CORES, 2 * CORES
    unit = unit_here(per_half, owners)
    asker = jnp.where(unit < per_half, unit + per_half, unit - per_half)
    for which in range(2):
        slot = jnp.maximum(order_ref[which, 2 * asker + 1], 0)
        out_ref[which] = near_ref[which, near_at(slot, per_owner)]


def far_weights(near, order, per_half):
    vmem = pl.BlockSpec(memory_space=pltpu.VMEM)
    return pl.pallas_call(
        functools.partial(far_kernel, per_half),
        out_shape=jax.ShapeDtypeStruct(near.shape[:1] + near.shape[2:], near.dtype),
        in_specs=[pl.BlockSpec(memory_space=pltpu.SMEM), vmem],
        out_specs=vmem,
        compiler_params=IN_VMEM,
        cost_estimate=pl.CostEstimate(flops=0, bytes_accessed=300_000, transcendentals=0),
    )(order, near)


def dot(a, b, over_a, over_b):
    return lax.dot_general(
        a, b, (((over_a,), (over_b,)), ((), ())), preferred_element_type=jnp.float32
    )


def grads_kernel(
    which, per_half, owners, loss_scale, order_ref, flags_ref, x_ref, near_ref, far_ref, out_ref,
    w_unit, first_sum, second_sum,
):
    sources, _, _, rows, _ = x_ref.shape
    per_owner = near_ref.shape[1] // CORES
    unit = unit_here(per_half, owners)
    half = lax.axis_index("fsdp") // CORES
    for i in range(2):
        slot = jnp.maximum(order_ref[which, 2 * unit + i], 0)
        near = slot // per_owner // CORES == half

        @pl.when(near)
        def _():
            w_unit[i] = near_ref[which, near_at(slot, per_owner)]

        @pl.when(jnp.logical_not(near))
        def _():
            w_unit[i] = far_ref[which]

    together = min(SOURCES_AT_ONCE, sources)
    steps = sources // together
    if steps > 1:
        first_sum[...] = jnp.zeros_like(first_sum)
        second_sum[...] = jnp.zeros_like(second_sum)

    def sum_up(total_ref, where, term):
        total_ref[where] = total_ref[where] + term if steps > 1 else term

    coupled = flags_ref[which, 2 * unit] == 1

    def read(step):
        at = step * together
        return [
            x_ref[pl.ds(at, together), which, i].reshape(together * rows, TILE) for i in range(2)
        ]

    @pl.when(coupled)
    def _():
        def go(step, carry):
            xs = jnp.concatenate(read(step), axis=1)
            firsts = jnp.concatenate([w_unit[0, 0], w_unit[1, 0]], axis=0)
            seconds = jnp.concatenate([w_unit[0, 1], w_unit[1, 1]], axis=1)
            value, slope = gelu_pair(dot(xs, firsts, 1, 0))
            active = value.astype(jnp.bfloat16)
            delta = dot(active, seconds, 1, 0)
            cotangent = (loss_scale * (xs.astype(jnp.float32) + delta)).astype(jnp.bfloat16)
            grad_act = dot(cotangent, seconds, 1, 1)
            grad_pre = (grad_act * slope).astype(jnp.bfloat16)
            sum_up(first_sum, ..., dot(xs, grad_pre, 0, 0))
            sum_up(second_sum, ..., dot(active, cotangent, 0, 0))
            return carry

        lax.fori_loop(0, steps, go, 0, unroll=min(steps, 4))

    @pl.when(jnp.logical_not(coupled))
    def _():
        def go(step, carry):
            for i, x in enumerate(read(step)):
                across = slice(i * TILE, (i + 1) * TILE)
                value, slope = gelu_pair(dot(x, w_unit[i, 0], 1, 0))
                active = value.astype(jnp.bfloat16)
                delta = dot(active, w_unit[i, 1], 1, 0)
                cotangent = (loss_scale * (x.astype(jnp.float32) + delta)).astype(jnp.bfloat16)
                grad_act = dot(cotangent, w_unit[i, 1], 1, 1)
                grad_pre = (grad_act * slope).astype(jnp.bfloat16)
                sum_up(first_sum, (across, slice(None)), dot(x, grad_pre, 0, 0))
                sum_up(second_sum, (slice(None), across), dot(active, cotangent, 0, 0))
            return carry

        lax.fori_loop(0, steps, go, 0, unroll=min(steps, 4))

    for i in range(2):
        across = slice(i * TILE, (i + 1) * TILE)
        out_ref[i, 0] = first_sum[across, :].astype(out_ref.dtype)
        out_ref[i, 1] = second_sum[:, across].astype(out_ref.dtype)


def unit_grads(which, blocks, near, far, order, flags, per_half, owners, loss_scale, dtype):
    sources, _, _, rows, _ = blocks.shape
    smem = pl.BlockSpec(memory_space=pltpu.SMEM)
    vmem = pl.BlockSpec(memory_space=pltpu.VMEM)
    return pl.pallas_call(
        functools.partial(grads_kernel, which, per_half, owners, loss_scale),
        out_shape=jax.ShapeDtypeStruct((2, 2, TILE, TILE), dtype),
        in_specs=[smem, smem, vmem, vmem, vmem],
        out_specs=vmem,
        scratch_shapes=[
            pltpu.VMEM((2, 2, TILE, TILE), jnp.bfloat16),
            pltpu.VMEM((2 * TILE, TILE), jnp.float32),
            pltpu.VMEM((TILE, 2 * TILE), jnp.float32),
        ],
        compiler_params=IN_VMEM,
        cost_estimate=pl.CostEstimate(
            flops=20 * sources * rows * TILE * TILE,
            bytes_accessed=4 * sources * rows * TILE,
            transcendentals=2 * sources * rows * TILE,
        ),
    )(order, flags, blocks, near, far)


def add_kernel(own_ref, arrived_ref, out_ref):
    total = (own_ref[...] + arrived_ref[...].astype(jnp.float32)).astype(out_ref.dtype)
    for copy in range(out_ref.shape[0]):
        out_ref[copy] = total


def add(own, arrived, copies):
    vmem = pl.BlockSpec(memory_space=pltpu.VMEM)
    return pl.pallas_call(
        add_kernel,
        out_shape=jax.ShapeDtypeStruct((copies,) + own.shape, jnp.bfloat16),
        in_specs=[vmem, vmem],
        out_specs=vmem,
        compiler_params=IN_VMEM,
        cost_estimate=pl.CostEstimate(flops=own.size, bytes_accessed=900_000, transcendentals=0),
    )(own, arrived)


def place_kernel(per_half, order_ref, counts_ref, same_ref, other_ref, out_ref, zeros, sems, zero_sems):
    owner, owners = lax.axis_index("fsdp"), counts_ref.shape[2]
    per_owner = out_ref.shape[0]
    zeros[...] = jnp.zeros_like(zeros)

    def each(act):
        for i in range(4 * per_half):
            at = order_ref[0, i] - owner * per_owner
            mine = (at >= 0) & (at < per_owner)
            place = unit_place(i // 2, per_half, owners)
            near = owner % CORES == place % CORES
            for grads_ref, where in ((same_ref, near), (other_ref, jnp.logical_not(near))):

                @pl.when(mine & where)
                def _():
                    act(
                        pltpu.make_async_copy(
                            grads_ref.at[place // CORES, i % 2], out_ref.at[at], sems.at[i]
                        )
                    )

        for slot in range(per_owner):

            @pl.when(counts_ref[0, 0, owner] <= slot)
            def _():
                act(pltpu.make_async_copy(zeros, out_ref.at[slot], zero_sems.at[slot]))

    each(lambda copy: copy.start())
    each(lambda copy: copy.wait())


def place(same, other, order, counts, per_half, per_owner):
    smem = pl.BlockSpec(memory_space=pltpu.SMEM)
    hbm = pl.BlockSpec(memory_space=pl.ANY)
    return pl.pallas_call(
        functools.partial(place_kernel, per_half),
        out_shape=jax.ShapeDtypeStruct((per_owner,) + same.shape[2:], same.dtype),
        in_specs=[smem, smem, hbm, hbm],
        out_specs=hbm,
        scratch_shapes=[
            pltpu.VMEM(same.shape[2:], same.dtype),
            pltpu.SemaphoreType.DMA((4 * per_half,)),
            pltpu.SemaphoreType.DMA((per_owner,)),
        ],
        compiler_params=IN_VMEM,
        cost_estimate=pl.CostEstimate(flops=0, bytes_accessed=1_000_000, transcendentals=0),
    )(order, counts, same, other)


def body(x_down, x_up, w_tiles, tile_rows, tile_cols, counts):
    rows_here = x_down.shape[2]
    slots, owners = tile_cols.shape[2], counts.shape[2]
    per_half = (live_total(slots, owners) // 2 + 1) // 2
    places = lax.axis_size("dp") * lax.axis_size("fsdp")
    sections = lax.axis_size("section")
    across = [(i, (i + sections // 2) % sections) for i in range(sections)]
    loss_scale = float(2 * rows_here * places) ** (-0.5)

    packed, order, flags = pack(x_down, x_up, tile_rows, tile_cols, counts, per_half, places)
    blocks = lax.all_to_all(packed, PLANE, split_axis=0, concat_axis=0, tiled=True)
    near = jnp.concatenate([w_tiles[0], swapped(w_tiles[0], 1)], axis=1)
    far = swapped(far_weights(near, order, per_half), CORES)
    grads = functools.partial(
        unit_grads, blocks=blocks, near=near, far=far, order=order, flags=flags,
        per_half=per_half, owners=owners, loss_scale=loss_scale,
    )
    arrived = lax.ppermute(grads(1, dtype=jnp.bfloat16), "section", across)
    mine = add(grads(0, dtype=jnp.float32), arrived, places // CORES)
    same_core = [
        [place for place in range(places) if place % CORES == core] for core in range(CORES)
    ]
    same = lax.all_to_all(
        mine, PLANE, split_axis=0, concat_axis=0, axis_index_groups=same_core, tiled=True
    )
    other = swapped(same, 1)
    return place(same, other, order, counts, per_half, slots // owners)[None]


def solution(mesh):
    in_specs = (
        P("section", "dp", "fsdp", None),
        P("section", "dp", "fsdp", None),
        P("section", None, "fsdp", None, None, None),
        P("section", None, None),
        P("section", None, None),
        P("section", None, None),
    )
    out_specs = P("section", "fsdp", None, None, None)
    return jax.shard_map(body, mesh=mesh, in_specs=in_specs, out_specs=out_specs, check_vma=False)
```

```python
import functools
import itertools
import math

import jax
import jax.numpy as jnp
from jax import lax
from jax.experimental import pallas as pl
from jax.experimental.pallas import tpu as pltpu
from jax.sharding import PartitionSpec as P

TILE = 128
PLANE = ("dp", "fsdp")
SOURCES_AT_ONCE = 8
COLUMNS = 192
CORES = 2
COPIES = 4
IN_VMEM = pltpu.CompilerParams(vmem_limit_bytes=16 * 1024 * 1024)

tanh_scale = math.sqrt(2.0 / math.pi)
cubic_coef = 0.044715


def gelu_pair(hidden):
    square = hidden * hidden
    tangent = jnp.tanh(tanh_scale * (hidden + cubic_coef * hidden * square))
    half = 0.5 * (1.0 + tangent)
    value = hidden * half
    slope = half + 0.5 * hidden * (1.0 - tangent * tangent) * tanh_scale * (
        1.0 + 3.0 * cubic_coef * square
    )
    return (value, slope)


def live_total(slots, owners):
    cap = slots // owners
    return sum(cap - i * cap // owners for i in range(owners))


def unit_place(unit, per_half, owners):
    half, at = unit // per_half, unit % per_half
    return at // CORES * owners + half * CORES + at % CORES


def unit_here(per_half, owners):
    owner = lax.axis_index("fsdp")
    at = lax.axis_index("dp") * CORES + owner % CORES
    return owner // CORES * per_half + jnp.minimum(at, per_half - 1)


def order_units(
    cols_ref, counts_ref, which, slots, per_half, order_ref, flags_ref, first_ref, last_ref
):
    per_owner, middle, unused = slots // counts_ref.shape[2], slots // 2, 4 * per_half
    for i in range(order_ref.shape[1]):
        order_ref[which, i] = -1
        flags_ref[which, i] = 0
    cols = []
    for s in range(slots):
        living = counts_ref[0, which, s // per_owner] > s % per_owner
        cols.append(jnp.where(living, cols_ref[0, which, s], COLUMNS))
    yield
    for s in range(slots):
        last_ref[cols[s]] = s
        first_ref[cols[slots - 1 - s]] = slots - 1 - s
    yield
    filled = [jnp.int32(0), jnp.int32(0)]

    def put(unit, slot_a, slot_b, coupled, really):
        at = jnp.where(really, 2 * unit, unused)
        order_ref[which, at] = slot_a
        order_ref[which, at + 1] = slot_b
        flags_ref[which, at] = coupled

    count = lambda condition: jnp.where(condition, 1, 0)
    alone, mixed = [], []
    for s in range(slots):
        living = cols[s] < COLUMNS
        first, last = first_ref[cols[s]], last_ref[cols[s]]
        leads = living & (first == s) & (last > s)
        alone.append(living & (first == last))
        half = s // middle
        pure = leads & (last < (half + 1) * middle)
        put(half * per_half + filled[half], s, last, 1, pure)
        filled[half] = filled[half] + count(pure)
        if half == 0:
            mixed.append((s, last, 1, leads & (last >= middle)))
        yield
    waiting, odd = [jnp.int32(0), jnp.int32(0)], [jnp.int32(0), jnp.int32(0)]
    for s in range(slots):
        half = s // middle
        second = alone[s] & (odd[half] == 1)
        put(half * per_half + filled[half], waiting[half], s, 0, second)
        filled[half] = filled[half] + count(second)
        odd[half] = jnp.where(alone[s], 1 - odd[half], odd[half])
        waiting[half] = jnp.where(alone[s], s, waiting[half])
        yield
    mixed.append((waiting[0], waiting[1], 0, odd[0] == 1))
    for low, high, coupled, really in mixed:
        room = filled[0] < per_half
        unit = jnp.where(room, filled[0], per_half + filled[1])
        put(unit, jnp.where(room, low, high), jnp.where(room, high, low), coupled, really)
        filled[0] = filled[0] + count(really & room)
        filled[1] = filled[1] + count(really & jnp.logical_not(room))
        yield


def pack_kernel(
    per_half, rows_ref, cols_ref, counts_ref, down_ref, up_ref,
    out_ref, order_ref, flags_ref, whole, first_a, last_a, first_b, last_b, sems,
):
    slots, owners = cols_ref.shape[2], counts_ref.shape[2]
    places, units, rows = out_ref.shape[0], 2 * per_half, whole.shape[1]
    pieces = sems.shape[1]
    copies = []
    for which, x_ref in ((0, down_ref), (1, up_ref)):
        for piece in range(pieces):
            part = pl.ds(piece * (rows // pieces), rows // pieces)
            copy = pltpu.make_async_copy(
                x_ref.at[0, 0, part], whole.at[which, part], sems.at[which, piece]
            )
            copy.start()
            copies.append(copy)
    steps = [
        order_units(cols_ref, counts_ref, which, slots, per_half, order_ref, flags_ref, *tables)
        for which, tables in enumerate(((first_a, last_a), (first_b, last_b)))
    ]
    for _ in itertools.zip_longest(*steps):
        pass
    used = [unit_place(unit, per_half, owners) for unit in range(units)]
    for place in range(places):
        if place not in used:
            out_ref[place] = jnp.zeros(out_ref.shape[1:], out_ref.dtype)
    for which in range(2):
        for copy in copies[which * pieces : (which + 1) * pieces]:
            copy.wait()
        for i in range(2 * units):
            row = rows_ref[0, which, jnp.maximum(order_ref[which, i], 0)]
            at = pl.multiple_of(row * TILE, TILE)
            out_ref[used[i // 2], which, i % 2] = whole[which, :, pl.ds(at, TILE)]


def pack(x_down, x_up, tile_rows, tile_cols, counts, per_half, places):
    rows, units = x_down.shape[2], 2 * per_half
    smem = pl.BlockSpec(memory_space=pltpu.SMEM)
    vmem = pl.BlockSpec(memory_space=pltpu.VMEM)
    hbm = pl.BlockSpec(memory_space=pl.ANY)
    return pl.pallas_call(
        functools.partial(pack_kernel, per_half),
        out_shape=[
            jax.ShapeDtypeStruct((places, 2, 2, rows, TILE), x_down.dtype),
            jax.ShapeDtypeStruct((2, 2 * units + 2), jnp.int32),
            jax.ShapeDtypeStruct((2, 2 * units + 2), jnp.int32),
        ],
        in_specs=[smem, smem, smem, hbm, hbm],
        out_specs=[vmem, smem, smem],
        scratch_shapes=[
            pltpu.VMEM((2,) + x_down.shape[2:], x_down.dtype),
            *[pltpu.SMEM((COLUMNS + 1,), jnp.int32)] * 4,
            pltpu.SemaphoreType.DMA((2, COPIES)),
        ],
        cost_estimate=pl.CostEstimate(
            flops=0, bytes_accessed=4 * x_down.size + 16 * units * rows * TILE, transcendentals=0
        ),
    )(tile_rows, tile_cols, counts, x_down, x_up)


def swapped(array, apart):
    size = lax.axis_size("fsdp")
    return lax.ppermute(array, "fsdp", [(i, i ^ apart) for i in range(size)])


def near_at(slot, per_owner):
    owner = slot // per_owner
    other = jnp.where(owner % CORES == lax.axis_index("fsdp") % CORES, 0, per_owner)
    return other + slot - owner * per_owner


def far_kernel(per_half, order_ref, near_ref, out_ref):
    per_owner, owners = near_ref.shape[1] // CORES, 2 * CORES
    unit = unit_here(per_half, owners)
    asker = jnp.where(unit < per_half, unit + per_half, unit - per_half)
    for which in range(2):
        slot = jnp.maximum(order_ref[which, 2 * asker + 1], 0)
        out_ref[which] = near_ref[which, near_at(slot, per_owner)]


def far_weights(near, order, per_half):
    vmem = pl.BlockSpec(memory_space=pltpu.VMEM)
    return pl.pallas_call(
        functools.partial(far_kernel, per_half),
        out_shape=jax.ShapeDtypeStruct(near.shape[:1] + near.shape[2:], near.dtype),
        in_specs=[pl.BlockSpec(memory_space=pltpu.SMEM), vmem],
        out_specs=vmem,
        compiler_params=IN_VMEM,
        cost_estimate=pl.CostEstimate(flops=0, bytes_accessed=300_000, transcendentals=0),
    )(order, near)


def dot(a, b, over_a, over_b):
    return lax.dot_general(
        a, b, (((over_a,), (over_b,)), ((), ())), preferred_element_type=jnp.float32
    )


def grads_kernel(
    which, per_half, owners, loss_scale, order_ref, flags_ref, x_ref, near_ref, far_ref, out_ref,
    w_unit, first_sum, second_sum,
):
    sources, _, _, rows, _ = x_ref.shape
    per_owner = near_ref.shape[1] // CORES
    unit = unit_here(per_half, owners)
    half = lax.axis_index("fsdp") // CORES
    for i in range(2):
        slot = jnp.maximum(order_ref[which, 2 * unit + i], 0)
        near = slot // per_owner // CORES == half

        @pl.when(near)
        def _():
            w_unit[i] = near_ref[which, near_at(slot, per_owner)]

        @pl.when(jnp.logical_not(near))
        def _():
            w_unit[i] = far_ref[which]

    together = min(SOURCES_AT_ONCE, sources)
    steps = sources // together
    if steps > 1:
        first_sum[...] = jnp.zeros_like(first_sum)
        second_sum[...] = jnp.zeros_like(second_sum)

    def sum_up(total_ref, where, term):
        total_ref[where] = total_ref[where] + term if steps > 1 else term

    coupled = flags_ref[which, 2 * unit] == 1

    def read(step):
        at = step * together
        return [
            x_ref[pl.ds(at, together), which, i].reshape(together * rows, TILE) for i in range(2)
        ]

    @pl.when(coupled)
    def _():
        def go(step, carry):
            xs = jnp.concatenate(read(step), axis=1)
            firsts = jnp.concatenate([w_unit[0, 0], w_unit[1, 0]], axis=0)
            seconds = jnp.concatenate([w_unit[0, 1], w_unit[1, 1]], axis=1)
            value, slope = gelu_pair(dot(xs, firsts, 1, 0))
            active = value.astype(jnp.bfloat16)
            delta = dot(active, seconds, 1, 0)
            cotangent = (loss_scale * (xs.astype(jnp.float32) + delta)).astype(jnp.bfloat16)
            grad_act = dot(cotangent, seconds, 1, 1)
            grad_pre = (grad_act * slope).astype(jnp.bfloat16)
            sum_up(first_sum, ..., dot(xs, grad_pre, 0, 0))
            sum_up(second_sum, ..., dot(active, cotangent, 0, 0))
            return carry

        lax.fori_loop(0, steps, go, 0, unroll=min(steps, 4))

    @pl.when(jnp.logical_not(coupled))
    def _():
        def go(step, carry):
            for i, x in enumerate(read(step)):
                across = slice(i * TILE, (i + 1) * TILE)
                value, slope = gelu_pair(dot(x, w_unit[i, 0], 1, 0))
                active = value.astype(jnp.bfloat16)
                delta = dot(active, w_unit[i, 1], 1, 0)
                cotangent = (loss_scale * (x.astype(jnp.float32) + delta)).astype(jnp.bfloat16)
                grad_act = dot(cotangent, w_unit[i, 1], 1, 1)
                grad_pre = (grad_act * slope).astype(jnp.bfloat16)
                sum_up(first_sum, (across, slice(None)), dot(x, grad_pre, 0, 0))
                sum_up(second_sum, (slice(None), across), dot(active, cotangent, 0, 0))
            return carry

        lax.fori_loop(0, steps, go, 0, unroll=min(steps, 4))

    for i in range(2):
        across = slice(i * TILE, (i + 1) * TILE)
        out_ref[i, 0] = first_sum[across, :].astype(out_ref.dtype)
        out_ref[i, 1] = second_sum[:, across].astype(out_ref.dtype)


def unit_grads(which, blocks, near, far, order, flags, per_half, owners, loss_scale, dtype):
    sources, _, _, rows, _ = blocks.shape
    smem = pl.BlockSpec(memory_space=pltpu.SMEM)
    vmem = pl.BlockSpec(memory_space=pltpu.VMEM)
    return pl.pallas_call(
        functools.partial(grads_kernel, which, per_half, owners, loss_scale),
        out_shape=jax.ShapeDtypeStruct((2, 2, TILE, TILE), dtype),
        in_specs=[smem, smem, vmem, vmem, vmem],
        out_specs=vmem,
        scratch_shapes=[
            pltpu.VMEM((2, 2, TILE, TILE), jnp.bfloat16),
            pltpu.VMEM((2 * TILE, TILE), jnp.float32),
            pltpu.VMEM((TILE, 2 * TILE), jnp.float32),
        ],
        compiler_params=IN_VMEM,
        cost_estimate=pl.CostEstimate(
            flops=20 * sources * rows * TILE * TILE,
            bytes_accessed=4 * sources * rows * TILE,
            transcendentals=2 * sources * rows * TILE,
        ),
    )(order, flags, blocks, near, far)


def add_kernel(own_ref, arrived_ref, out_ref):
    out_ref[...] = (own_ref[...] + arrived_ref[...].astype(jnp.float32)).astype(out_ref.dtype)


def add(own, arrived):
    vmem = pl.BlockSpec(memory_space=pltpu.VMEM)
    return pl.pallas_call(
        add_kernel,
        out_shape=jax.ShapeDtypeStruct(own.shape, jnp.bfloat16),
        in_specs=[vmem, vmem],
        out_specs=vmem,
        compiler_params=IN_VMEM,
        cost_estimate=pl.CostEstimate(flops=own.size, bytes_accessed=900_000, transcendentals=0),
    )(own, arrived)


def hand_round(mine):
    replicas = lax.axis_size("dp")
    near = jnp.concatenate(
        [mine]
        + [
            lax.ppermute(mine, "dp", [(i, (i + by) % replicas) for i in range(replicas)])
            for by in range(1, replicas)
        ],
        axis=0,
    )
    return jnp.concatenate([near, swapped(near[1::2], CORES)], axis=0)


def place_kernel(per_half, order_ref, counts_ref, same_ref, other_ref, out_ref, zeros, sems, zero_sems):
    owner, replicas = lax.axis_index("fsdp"), same_ref.shape[0] // 3
    per_owner = out_ref.shape[0]
    zeros[...] = jnp.zeros_like(zeros)

    def each(act):
        for i in range(4 * per_half):
            at = order_ref[0, i] - owner * per_owner
            mine = (at >= 0) & (at < per_owner)
            half, spot = i // 2 // per_half, i // 2 % per_half
            by = (lax.axis_index("dp") - spot // CORES + replicas) % replicas
            held = jnp.where(owner // CORES == half, 2 * by + i % 2, 2 * replicas + by)
            near = owner % CORES == spot % CORES
            for grads_ref, where in ((same_ref, near), (other_ref, jnp.logical_not(near))):

                @pl.when(mine & where)
                def _():
                    act(
                        pltpu.make_async_copy(
                            grads_ref.at[held], out_ref.at[at], sems.at[i]
                        )
                    )

        for slot in range(per_owner):

            @pl.when(counts_ref[0, 0, owner] <= slot)
            def _():
                act(pltpu.make_async_copy(zeros, out_ref.at[slot], zero_sems.at[slot]))

    each(lambda copy: copy.start())
    each(lambda copy: copy.wait())


def place(same, other, order, counts, per_half, per_owner):
    smem = pl.BlockSpec(memory_space=pltpu.SMEM)
    hbm = pl.BlockSpec(memory_space=pl.ANY)
    return pl.pallas_call(
        functools.partial(place_kernel, per_half),
        out_shape=jax.ShapeDtypeStruct((per_owner,) + same.shape[1:], same.dtype),
        in_specs=[smem, smem, hbm, hbm],
        out_specs=hbm,
        scratch_shapes=[
            pltpu.VMEM(same.shape[1:], same.dtype),
            pltpu.SemaphoreType.DMA((4 * per_half,)),
            pltpu.SemaphoreType.DMA((per_owner,)),
        ],
        compiler_params=IN_VMEM,
        cost_estimate=pl.CostEstimate(flops=0, bytes_accessed=1_000_000, transcendentals=0),
    )(order, counts, same, other)


def body(x_down, x_up, w_tiles, tile_rows, tile_cols, counts):
    rows_here = x_down.shape[2]
    slots, owners = tile_cols.shape[2], counts.shape[2]
    per_half = (live_total(slots, owners) // 2 + 1) // 2
    places = lax.axis_size("dp") * lax.axis_size("fsdp")
    sections = lax.axis_size("section")
    across = [(i, (i + sections // 2) % sections) for i in range(sections)]
    loss_scale = float(2 * rows_here * places) ** (-0.5)

    packed, order, flags = pack(x_down, x_up, tile_rows, tile_cols, counts, per_half, places)
    blocks = lax.all_to_all(packed, PLANE, split_axis=0, concat_axis=0, tiled=True)
    near = jnp.concatenate([w_tiles[0], swapped(w_tiles[0], 1)], axis=1)
    far = swapped(far_weights(near, order, per_half), CORES)
    grads = functools.partial(
        unit_grads, blocks=blocks, near=near, far=far, order=order, flags=flags,
        per_half=per_half, owners=owners, loss_scale=loss_scale,
    )
    arrived = lax.ppermute(grads(1, dtype=jnp.bfloat16), "section", across)
    mine = add(grads(0, dtype=jnp.float32), arrived)
    same = hand_round(mine)
    other = swapped(same, 1)
    return place(same, other, order, counts, per_half, slots // owners)[None]


def solution(mesh):
    in_specs = (
        P("section", "dp", "fsdp", None),
        P("section", "dp", "fsdp", None),
        P("section", None, "fsdp", None, None, None),
        P("section", None, None),
        P("section", None, None),
        P("section", None, None),
    )
    out_specs = P("section", "fsdp", None, None, None)
    return jax.shard_map(body, mesh=mesh, in_specs=in_specs, out_specs=out_specs, check_vma=False)
```

```python
import functools
import itertools
import math

import jax
import jax.numpy as jnp
from jax import lax
from jax.experimental import pallas as pl
from jax.experimental.pallas import tpu as pltpu
from jax.sharding import PartitionSpec as P

TILE = 128
PLANE = ("dp", "fsdp")
SOURCES_AT_ONCE = 8
COLUMNS = 192
CORES = 2
COPIES = 4
IN_VMEM = pltpu.CompilerParams(vmem_limit_bytes=16 * 1024 * 1024)

tanh_scale = math.sqrt(2.0 / math.pi)
cubic_coef = 0.044715


def gelu_pair(hidden):
    square = hidden * hidden
    tangent = jnp.tanh(tanh_scale * (hidden + cubic_coef * hidden * square))
    half = 0.5 * (1.0 + tangent)
    value = hidden * half
    slope = half + 0.5 * hidden * (1.0 - tangent * tangent) * tanh_scale * (
        1.0 + 3.0 * cubic_coef * square
    )
    return (value, slope)


def live_total(slots, owners):
    cap = slots // owners
    return sum(cap - i * cap // owners for i in range(owners))


def unit_place(unit, per_half, owners):
    half, at = unit // per_half, unit % per_half
    return at // CORES * owners + half * CORES + at % CORES


def unit_here(per_half, owners):
    owner = lax.axis_index("fsdp")
    at = lax.axis_index("dp") * CORES + owner % CORES
    return owner // CORES * per_half + jnp.minimum(at, per_half - 1)


def order_units(
    cols_ref, counts_ref, which, slots, per_half, order_ref, flags_ref, first_ref, last_ref
):
    per_owner, middle, unused = slots // counts_ref.shape[2], slots // 2, 4 * per_half
    for i in range(order_ref.shape[1]):
        order_ref[which, i] = -1
        flags_ref[which, i] = 0
    cols = []
    for s in range(slots):
        living = counts_ref[0, which, s // per_owner] > s % per_owner
        cols.append(jnp.where(living, cols_ref[0, which, s], COLUMNS))
    yield
    for s in range(slots):
        last_ref[cols[s]] = s
        first_ref[cols[slots - 1 - s]] = slots - 1 - s
    yield
    filled = [jnp.int32(0), jnp.int32(0)]

    def put(unit, slot_a, slot_b, coupled, really):
        at = jnp.where(really, 2 * unit, unused)
        order_ref[which, at] = slot_a
        order_ref[which, at + 1] = slot_b
        flags_ref[which, at] = coupled

    count = lambda condition: jnp.where(condition, 1, 0)
    alone, mixed = [], []
    for s in range(slots):
        living = cols[s] < COLUMNS
        first, last = first_ref[cols[s]], last_ref[cols[s]]
        leads = living & (first == s) & (last > s)
        alone.append(living & (first == last))
        half = s // middle
        pure = leads & (last < (half + 1) * middle)
        put(half * per_half + filled[half], s, last, 1, pure)
        filled[half] = filled[half] + count(pure)
        if half == 0:
            mixed.append((s, last, 1, leads & (last >= middle)))
        yield
    waiting, odd = [jnp.int32(0), jnp.int32(0)], [jnp.int32(0), jnp.int32(0)]
    for s in range(slots):
        half = s // middle
        second = alone[s] & (odd[half] == 1)
        put(half * per_half + filled[half], waiting[half], s, 0, second)
        filled[half] = filled[half] + count(second)
        odd[half] = jnp.where(alone[s], 1 - odd[half], odd[half])
        waiting[half] = jnp.where(alone[s], s, waiting[half])
        yield
    mixed.append((waiting[0], waiting[1], 0, odd[0] == 1))
    for low, high, coupled, really in mixed:
        room = filled[0] < per_half
        unit = jnp.where(room, filled[0], per_half + filled[1])
        put(unit, jnp.where(room, low, high), jnp.where(room, high, low), coupled, really)
        filled[0] = filled[0] + count(really & room)
        filled[1] = filled[1] + count(really & jnp.logical_not(room))
        yield


def pack_kernel(
    per_half, rows_ref, cols_ref, counts_ref, down_ref, up_ref,
    out_ref, order_ref, flags_ref, whole, first_a, last_a, first_b, last_b, sems,
):
    slots, owners = cols_ref.shape[2], counts_ref.shape[2]
    places, units, rows = out_ref.shape[0], 2 * per_half, whole.shape[1]
    pieces = sems.shape[1]
    copies = []
    for which, x_ref in ((0, down_ref), (1, up_ref)):
        for piece in range(pieces):
            part = pl.ds(piece * (rows // pieces), rows // pieces)
            copy = pltpu.make_async_copy(
                x_ref.at[0, 0, part], whole.at[which, part], sems.at[which, piece]
            )
            copy.start()
            copies.append(copy)
    steps = [
        order_units(cols_ref, counts_ref, which, slots, per_half, order_ref, flags_ref, *tables)
        for which, tables in enumerate(((first_a, last_a), (first_b, last_b)))
    ]
    for _ in itertools.zip_longest(*steps):
        pass
    used = [unit_place(unit, per_half, owners) for unit in range(units)]
    for place in range(places):
        if place not in used:
            out_ref[place] = jnp.zeros(out_ref.shape[1:], out_ref.dtype)
    for which in range(2):
        for copy in copies[which * pieces : (which + 1) * pieces]:
            copy.wait()
        for i in range(2 * units):
            row = rows_ref[0, which, jnp.maximum(order_ref[which, i], 0)]
            at = pl.multiple_of(row * TILE, TILE)
            out_ref[used[i // 2], which, i % 2] = whole[which, :, pl.ds(at, TILE)]


def pack(x_down, x_up, tile_rows, tile_cols, counts, per_half, places):
    rows, units = x_down.shape[2], 2 * per_half
    smem = pl.BlockSpec(memory_space=pltpu.SMEM)
    vmem = pl.BlockSpec(memory_space=pltpu.VMEM)
    hbm = pl.BlockSpec(memory_space=pl.ANY)
    return pl.pallas_call(
        functools.partial(pack_kernel, per_half),
        out_shape=[
            jax.ShapeDtypeStruct((places, 2, 2, rows, TILE), x_down.dtype),
            jax.ShapeDtypeStruct((2, 2 * units + 2), jnp.int32),
            jax.ShapeDtypeStruct((2, 2 * units + 2), jnp.int32),
        ],
        in_specs=[smem, smem, smem, hbm, hbm],
        out_specs=[vmem, smem, smem],
        scratch_shapes=[
            pltpu.VMEM((2,) + x_down.shape[2:], x_down.dtype),
            *[pltpu.SMEM((COLUMNS + 1,), jnp.int32)] * 4,
            pltpu.SemaphoreType.DMA((2, COPIES)),
        ],
        cost_estimate=pl.CostEstimate(
            flops=0, bytes_accessed=4 * x_down.size + 16 * units * rows * TILE, transcendentals=0
        ),
    )(tile_rows, tile_cols, counts, x_down, x_up)


def swapped(array, apart):
    size = lax.axis_size("fsdp")
    return lax.ppermute(array, "fsdp", [(i, i ^ apart) for i in range(size)])


def near_at(slot, per_owner):
    owner = slot // per_owner
    other = jnp.where(owner % CORES == lax.axis_index("fsdp") % CORES, 0, per_owner)
    return other + slot - owner * per_owner


def far_kernel(per_half, order_ref, near_ref, out_ref):
    per_owner, owners = near_ref.shape[1] // CORES, 2 * CORES
    unit = unit_here(per_half, owners)
    asker = jnp.where(unit < per_half, unit + per_half, unit - per_half)
    for which in range(2):
        slot = jnp.maximum(order_ref[which, 2 * asker + 1], 0)
        out_ref[which] = near_ref[which, near_at(slot, per_owner)]


def far_weights(near, order, per_half):
    vmem = pl.BlockSpec(memory_space=pltpu.VMEM)
    return pl.pallas_call(
        functools.partial(far_kernel, per_half),
        out_shape=jax.ShapeDtypeStruct(near.shape[:1] + near.shape[2:], near.dtype),
        in_specs=[pl.BlockSpec(memory_space=pltpu.SMEM), vmem],
        out_specs=vmem,
        compiler_params=IN_VMEM,
        cost_estimate=pl.CostEstimate(flops=0, bytes_accessed=300_000, transcendentals=0),
    )(order, near)


def dot(a, b, over_a, over_b):
    return lax.dot_general(
        a, b, (((over_a,), (over_b,)), ((), ())), preferred_element_type=jnp.float32
    )


def grads_kernel(
    which, per_half, owners, loss_scale, order_ref, flags_ref, x_ref, near_ref, far_ref, out_ref,
    w_unit, first_sum, second_sum,
):
    sources, _, _, rows, _ = x_ref.shape
    per_owner = near_ref.shape[1] // CORES
    unit = unit_here(per_half, owners)
    half = lax.axis_index("fsdp") // CORES
    for i in range(2):
        slot = jnp.maximum(order_ref[which, 2 * unit + i], 0)
        near = slot // per_owner // CORES == half

        @pl.when(near)
        def _():
            w_unit[i] = near_ref[which, near_at(slot, per_owner)]

        @pl.when(jnp.logical_not(near))
        def _():
            w_unit[i] = far_ref[which]

    together = min(SOURCES_AT_ONCE, sources)
    steps = sources // together
    if steps > 1:
        first_sum[...] = jnp.zeros_like(first_sum)
        second_sum[...] = jnp.zeros_like(second_sum)

    def sum_up(total_ref, where, term):
        total_ref[where] = total_ref[where] + term if steps > 1 else term

    coupled = flags_ref[which, 2 * unit] == 1

    def read(step):
        at = step * together
        return [
            x_ref[pl.ds(at, together), which, i].reshape(together * rows, TILE) for i in range(2)
        ]

    @pl.when(coupled)
    def _():
        def go(step, carry):
            xs = jnp.concatenate(read(step), axis=1)
            firsts = jnp.concatenate([w_unit[0, 0], w_unit[1, 0]], axis=0)
            seconds = jnp.concatenate([w_unit[0, 1], w_unit[1, 1]], axis=1)
            value, slope = gelu_pair(dot(xs, firsts, 1, 0))
            active = value.astype(jnp.bfloat16)
            delta = dot(active, seconds, 1, 0)
            cotangent = (loss_scale * (xs.astype(jnp.float32) + delta)).astype(jnp.bfloat16)
            grad_act = dot(cotangent, seconds, 1, 1)
            grad_pre = (grad_act * slope).astype(jnp.bfloat16)
            sum_up(first_sum, ..., dot(xs, grad_pre, 0, 0))
            sum_up(second_sum, ..., dot(active, cotangent, 0, 0))
            return carry

        lax.fori_loop(0, steps, go, 0, unroll=min(steps, 4))

    @pl.when(jnp.logical_not(coupled))
    def _():
        def go(step, carry):
            for i, x in enumerate(read(step)):
                across = slice(i * TILE, (i + 1) * TILE)
                value, slope = gelu_pair(dot(x, w_unit[i, 0], 1, 0))
                active = value.astype(jnp.bfloat16)
                delta = dot(active, w_unit[i, 1], 1, 0)
                cotangent = (loss_scale * (x.astype(jnp.float32) + delta)).astype(jnp.bfloat16)
                grad_act = dot(cotangent, w_unit[i, 1], 1, 1)
                grad_pre = (grad_act * slope).astype(jnp.bfloat16)
                sum_up(first_sum, (across, slice(None)), dot(x, grad_pre, 0, 0))
                sum_up(second_sum, (slice(None), across), dot(active, cotangent, 0, 0))
            return carry

        lax.fori_loop(0, steps, go, 0, unroll=min(steps, 4))

    for i in range(2):
        across = slice(i * TILE, (i + 1) * TILE)
        out_ref[i, 0] = first_sum[across, :].astype(out_ref.dtype)
        out_ref[i, 1] = second_sum[:, across].astype(out_ref.dtype)


def unit_grads(which, blocks, near, far, order, flags, per_half, owners, loss_scale, dtype):
    sources, _, _, rows, _ = blocks.shape
    smem = pl.BlockSpec(memory_space=pltpu.SMEM)
    vmem = pl.BlockSpec(memory_space=pltpu.VMEM)
    return pl.pallas_call(
        functools.partial(grads_kernel, which, per_half, owners, loss_scale),
        out_shape=jax.ShapeDtypeStruct((2, 2, TILE, TILE), dtype),
        in_specs=[smem, smem, vmem, vmem, vmem],
        out_specs=vmem,
        scratch_shapes=[
            pltpu.VMEM((2, 2, TILE, TILE), jnp.bfloat16),
            pltpu.VMEM((2 * TILE, TILE), jnp.float32),
            pltpu.VMEM((TILE, 2 * TILE), jnp.float32),
        ],
        compiler_params=IN_VMEM,
        cost_estimate=pl.CostEstimate(
            flops=20 * sources * rows * TILE * TILE,
            bytes_accessed=4 * sources * rows * TILE,
            transcendentals=2 * sources * rows * TILE,
        ),
    )(order, flags, blocks, near, far)


def add_kernel(own_ref, arrived_ref, out_ref):
    out_ref[...] = (own_ref[...] + arrived_ref[...].astype(jnp.float32)).astype(out_ref.dtype)


def add(own, arrived):
    vmem = pl.BlockSpec(memory_space=pltpu.VMEM)
    return pl.pallas_call(
        add_kernel,
        out_shape=jax.ShapeDtypeStruct(own.shape, jnp.bfloat16),
        in_specs=[vmem, vmem],
        out_specs=vmem,
        compiler_params=IN_VMEM,
        cost_estimate=pl.CostEstimate(flops=own.size, bytes_accessed=900_000, transcendentals=0),
    )(own, arrived)


def hand_round(mine):
    replicas = lax.axis_size("dp")
    near = jnp.concatenate(
        [mine]
        + [
            lax.ppermute(mine, "dp", [(i, (i + by) % replicas) for i in range(replicas)])
            for by in range(1, replicas)
        ],
        axis=0,
    )
    return jnp.concatenate([near, swapped(near[1::2], CORES)], axis=0)


def place_kernel(
    per_half, order_ref, counts_ref, same_ref, other_ref, out_ref, zeros, source_ref, sems
):
    owner, replicas = lax.axis_index("fsdp"), same_ref.shape[0] // 3
    per_owner = out_ref.shape[0]
    zeros[...] = jnp.zeros_like(zeros)
    for slot in range(per_owner):
        source_ref[slot] = 0
    for i in range(4 * per_half):
        at = order_ref[0, i] - owner * per_owner
        mine = (at >= 0) & (at < per_owner)
        half, spot = i // 2 // per_half, i // 2 % per_half
        by = (lax.axis_index("dp") - spot // CORES + replicas) % replicas
        held = jnp.where(owner // CORES == half, 2 * by + i % 2, 2 * replicas + by)
        other = jnp.where(owner % CORES == spot % CORES, 0, 1)
        source_ref[jnp.where(mine, at, per_owner)] = 2 * held + other
    for slot in range(per_owner):
        living, source = counts_ref[0, 0, owner] > slot, source_ref[slot]
        for kind, grads_ref in enumerate((same_ref, other_ref)):

            @pl.when(living & (source % 2 == kind))
            def _():
                pltpu.make_async_copy(
                    grads_ref.at[source // 2], out_ref.at[slot], sems.at[slot]
                ).start()

        @pl.when(jnp.logical_not(living))
        def _():
            pltpu.make_async_copy(zeros, out_ref.at[slot], sems.at[slot]).start()

    for slot in range(per_owner):
        pltpu.make_async_copy(zeros, out_ref.at[slot], sems.at[slot]).wait()


def place(same, other, order, counts, per_half, per_owner):
    smem = pl.BlockSpec(memory_space=pltpu.SMEM)
    hbm = pl.BlockSpec(memory_space=pl.ANY)
    return pl.pallas_call(
        functools.partial(place_kernel, per_half),
        out_shape=jax.ShapeDtypeStruct((per_owner,) + same.shape[1:], same.dtype),
        in_specs=[smem, smem, hbm, hbm],
        out_specs=hbm,
        scratch_shapes=[
            pltpu.VMEM(same.shape[1:], same.dtype),
            pltpu.SMEM((per_owner + 1,), jnp.int32),
            pltpu.SemaphoreType.DMA((per_owner,)),
        ],
        compiler_params=IN_VMEM,
        cost_estimate=pl.CostEstimate(flops=0, bytes_accessed=1_000_000, transcendentals=0),
    )(order, counts, same, other)


def body(x_down, x_up, w_tiles, tile_rows, tile_cols, counts):
    rows_here = x_down.shape[2]
    slots, owners = tile_cols.shape[2], counts.shape[2]
    per_half = (live_total(slots, owners) // 2 + 1) // 2
    places = lax.axis_size("dp") * lax.axis_size("fsdp")
    sections = lax.axis_size("section")
    across = [(i, (i + sections // 2) % sections) for i in range(sections)]
    loss_scale = float(2 * rows_here * places) ** (-0.5)

    packed, order, flags = pack(x_down, x_up, tile_rows, tile_cols, counts, per_half, places)
    blocks = lax.all_to_all(packed, PLANE, split_axis=0, concat_axis=0, tiled=True)
    near = jnp.concatenate([w_tiles[0], swapped(w_tiles[0], 1)], axis=1)
    far = swapped(far_weights(near, order, per_half), CORES)
    grads = functools.partial(
        unit_grads, blocks=blocks, near=near, far=far, order=order, flags=flags,
        per_half=per_half, owners=owners, loss_scale=loss_scale,
    )
    arrived = lax.ppermute(grads(1, dtype=jnp.bfloat16), "section", across)
    mine = add(grads(0, dtype=jnp.float32), arrived)
    same = hand_round(mine)
    other = swapped(same, 1)
    return place(same, other, order, counts, per_half, slots // owners)[None]


def solution(mesh):
    in_specs = (
        P("section", "dp", "fsdp", None),
        P("section", "dp", "fsdp", None),
        P("section", None, "fsdp", None, None, None),
        P("section", None, None),
        P("section", None, None),
        P("section", None, None),
    )
    out_specs = P("section", "fsdp", None, None, None)
    return jax.shard_map(body, mesh=mesh, in_specs=in_specs, out_specs=out_specs, check_vma=False)
```

```python
import functools
import itertools
import math

import jax
import jax.numpy as jnp
from jax import lax
from jax.experimental import pallas as pl
from jax.experimental.pallas import tpu as pltpu
from jax.sharding import PartitionSpec as P

TILE = 128
PLANE = ("dp", "fsdp")
SOURCES_AT_ONCE = 8
COLUMNS = 192
CORES = 2
COPIES = 1
IN_VMEM = pltpu.CompilerParams(vmem_limit_bytes=16 * 1024 * 1024)

tanh_scale = math.sqrt(2.0 / math.pi)
cubic_coef = 0.044715


def gelu_pair(hidden):
    square = hidden * hidden
    tangent = jnp.tanh(tanh_scale * (hidden + cubic_coef * hidden * square))
    half = 0.5 * (1.0 + tangent)
    value = hidden * half
    slope = half + 0.5 * hidden * (1.0 - tangent * tangent) * tanh_scale * (
        1.0 + 3.0 * cubic_coef * square
    )
    return (value, slope)


def live_total(slots, owners):
    cap = slots // owners
    return sum(cap - i * cap // owners for i in range(owners))


def unit_place(unit, per_half, owners):
    half, at = unit // per_half, unit % per_half
    return at // CORES * owners + half * CORES + at % CORES


def unit_here(per_half, owners):
    owner = lax.axis_index("fsdp")
    at = lax.axis_index("dp") * CORES + owner % CORES
    return owner // CORES * per_half + jnp.minimum(at, per_half - 1)


def order_units(
    cols_ref, counts_ref, which, slots, per_half, order_ref, flags_ref, first_ref, last_ref
):
    per_owner, middle, unused = slots // counts_ref.shape[2], slots // 2, 4 * per_half
    for i in range(order_ref.shape[1]):
        order_ref[which, i] = -1
        flags_ref[which, i] = 0
    cols = []
    for s in range(slots):
        living = counts_ref[0, which, s // per_owner] > s % per_owner
        cols.append(jnp.where(living, cols_ref[0, which, s], COLUMNS))
    yield
    for s in range(slots):
        last_ref[cols[s]] = s
        first_ref[cols[slots - 1 - s]] = slots - 1 - s
    yield
    filled = [jnp.int32(0), jnp.int32(0)]

    def put(unit, slot_a, slot_b, coupled, really):
        at = jnp.where(really, 2 * unit, unused)
        order_ref[which, at] = slot_a
        order_ref[which, at + 1] = slot_b
        flags_ref[which, at] = coupled

    count = lambda condition: jnp.where(condition, 1, 0)
    alone, mixed = [], []
    for s in range(slots):
        living = cols[s] < COLUMNS
        first, last = first_ref[cols[s]], last_ref[cols[s]]
        leads = living & (first == s) & (last > s)
        alone.append(living & (first == last))
        half = s // middle
        pure = leads & (last < (half + 1) * middle)
        put(half * per_half + filled[half], s, last, 1, pure)
        filled[half] = filled[half] + count(pure)
        if half == 0:
            mixed.append((s, last, 1, leads & (last >= middle)))
        yield
    waiting, odd = [jnp.int32(0), jnp.int32(0)], [jnp.int32(0), jnp.int32(0)]
    for s in range(slots):
        half = s // middle
        second = alone[s] & (odd[half] == 1)
        put(half * per_half + filled[half], waiting[half], s, 0, second)
        filled[half] = filled[half] + count(second)
        odd[half] = jnp.where(alone[s], 1 - odd[half], odd[half])
        waiting[half] = jnp.where(alone[s], s, waiting[half])
        yield
    mixed.append((waiting[0], waiting[1], 0, odd[0] == 1))
    for low, high, coupled, really in mixed:
        room = filled[0] < per_half
        unit = jnp.where(room, filled[0], per_half + filled[1])
        put(unit, jnp.where(room, low, high), jnp.where(room, high, low), coupled, really)
        filled[0] = filled[0] + count(really & room)
        filled[1] = filled[1] + count(really & jnp.logical_not(room))
        yield


def pack_kernel(
    per_half, rows_ref, cols_ref, counts_ref, down_ref, up_ref,
    out_ref, order_ref, flags_ref, whole, first_a, last_a, first_b, last_b, sems,
):
    slots, owners = cols_ref.shape[2], counts_ref.shape[2]
    places, units, rows = out_ref.shape[0], 2 * per_half, whole.shape[1]
    pieces = sems.shape[1]
    copies = []
    for which, x_ref in ((0, down_ref), (1, up_ref)):
        for piece in range(pieces):
            part = pl.ds(piece * (rows // pieces), rows // pieces)
            copy = pltpu.make_async_copy(
                x_ref.at[0, 0, part], whole.at[which, part], sems.at[which, piece]
            )
            copy.start()
            copies.append(copy)
    steps = [
        order_units(cols_ref, counts_ref, which, slots, per_half, order_ref, flags_ref, *tables)
        for which, tables in enumerate(((first_a, last_a), (first_b, last_b)))
    ]
    for _ in itertools.zip_longest(*steps):
        pass
    used = [unit_place(unit, per_half, owners) for unit in range(units)]
    for place in range(places):
        if place not in used:
            out_ref[place] = jnp.zeros(out_ref.shape[1:], out_ref.dtype)
    for which in range(2):
        for copy in copies[which * pieces : (which + 1) * pieces]:
            copy.wait()
        for i in range(2 * units):
            row = rows_ref[0, which, jnp.maximum(order_ref[which, i], 0)]
            at = pl.multiple_of(row * TILE, TILE)
            out_ref[used[i // 2], which, i % 2] = whole[which, :, pl.ds(at, TILE)]


def pack(x_down, x_up, tile_rows, tile_cols, counts, per_half, places):
    rows, units = x_down.shape[2], 2 * per_half
    smem = pl.BlockSpec(memory_space=pltpu.SMEM)
    vmem = pl.BlockSpec(memory_space=pltpu.VMEM)
    hbm = pl.BlockSpec(memory_space=pl.ANY)
    return pl.pallas_call(
        functools.partial(pack_kernel, per_half),
        out_shape=[
            jax.ShapeDtypeStruct((places, 2, 2, rows, TILE), x_down.dtype),
            jax.ShapeDtypeStruct((2, 2 * units + 2), jnp.int32),
            jax.ShapeDtypeStruct((2, 2 * units + 2), jnp.int32),
        ],
        in_specs=[smem, smem, smem, hbm, hbm],
        out_specs=[vmem, smem, smem],
        scratch_shapes=[
            pltpu.VMEM((2,) + x_down.shape[2:], x_down.dtype),
            *[pltpu.SMEM((COLUMNS + 1,), jnp.int32)] * 4,
            pltpu.SemaphoreType.DMA((2, COPIES)),
        ],
        cost_estimate=pl.CostEstimate(
            flops=0, bytes_accessed=4 * x_down.size + 16 * units * rows * TILE, transcendentals=0
        ),
    )(tile_rows, tile_cols, counts, x_down, x_up)


def swapped(array, apart):
    size = lax.axis_size("fsdp")
    return lax.ppermute(array, "fsdp", [(i, i ^ apart) for i in range(size)])


def near_at(slot, per_owner):
    owner = slot // per_owner
    other = jnp.where(owner % CORES == lax.axis_index("fsdp") % CORES, 0, per_owner)
    return other + slot - owner * per_owner


def far_kernel(per_half, order_ref, near_ref, out_ref):
    per_owner, owners = near_ref.shape[1] // CORES, 2 * CORES
    unit = unit_here(per_half, owners)
    asker = jnp.where(unit < per_half, unit + per_half, unit - per_half)
    for which in range(2):
        slot = jnp.maximum(order_ref[which, 2 * asker + 1], 0)
        out_ref[which] = near_ref[which, near_at(slot, per_owner)]


def far_weights(near, order, per_half):
    vmem = pl.BlockSpec(memory_space=pltpu.VMEM)
    return pl.pallas_call(
        functools.partial(far_kernel, per_half),
        out_shape=jax.ShapeDtypeStruct(near.shape[:1] + near.shape[2:], near.dtype),
        in_specs=[pl.BlockSpec(memory_space=pltpu.SMEM), vmem],
        out_specs=vmem,
        compiler_params=IN_VMEM,
        cost_estimate=pl.CostEstimate(flops=0, bytes_accessed=300_000, transcendentals=0),
    )(order, near)


def dot(a, b, over_a, over_b):
    return lax.dot_general(
        a, b, (((over_a,), (over_b,)), ((), ())), preferred_element_type=jnp.float32
    )


def grads_kernel(
    which, per_half, owners, loss_scale, order_ref, flags_ref, x_ref, near_ref, far_ref, out_ref,
    w_unit, first_sum, second_sum,
):
    sources, _, _, rows, _ = x_ref.shape
    per_owner = near_ref.shape[1] // CORES
    unit = unit_here(per_half, owners)
    half = lax.axis_index("fsdp") // CORES
    for i in range(2):
        slot = jnp.maximum(order_ref[which, 2 * unit + i], 0)
        near = slot // per_owner // CORES == half

        @pl.when(near)
        def _():
            w_unit[i] = near_ref[which, near_at(slot, per_owner)]

        @pl.when(jnp.logical_not(near))
        def _():
            w_unit[i] = far_ref[which]

    together = min(SOURCES_AT_ONCE, sources)
    steps = sources // together
    if steps > 1:
        first_sum[...] = jnp.zeros_like(first_sum)
        second_sum[...] = jnp.zeros_like(second_sum)

    def sum_up(total_ref, where, term):
        total_ref[where] = total_ref[where] + term if steps > 1 else term

    coupled = flags_ref[which, 2 * unit] == 1

    def read(step):
        at = step * together
        return [
            x_ref[pl.ds(at, together), which, i].reshape(together * rows, TILE) for i in range(2)
        ]

    @pl.when(coupled)
    def _():
        def go(step, carry):
            xs = jnp.concatenate(read(step), axis=1)
            firsts = jnp.concatenate([w_unit[0, 0], w_unit[1, 0]], axis=0)
            seconds = jnp.concatenate([w_unit[0, 1], w_unit[1, 1]], axis=1)
            value, slope = gelu_pair(dot(xs, firsts, 1, 0))
            active = value.astype(jnp.bfloat16)
            delta = dot(active, seconds, 1, 0)
            cotangent = (loss_scale * (xs.astype(jnp.float32) + delta)).astype(jnp.bfloat16)
            grad_act = dot(cotangent, seconds, 1, 1)
            grad_pre = (grad_act * slope).astype(jnp.bfloat16)
            sum_up(first_sum, ..., dot(xs, grad_pre, 0, 0))
            sum_up(second_sum, ..., dot(active, cotangent, 0, 0))
            return carry

        lax.fori_loop(0, steps, go, 0, unroll=min(steps, 4))

    @pl.when(jnp.logical_not(coupled))
    def _():
        def go(step, carry):
            for i, x in enumerate(read(step)):
                across = slice(i * TILE, (i + 1) * TILE)
                value, slope = gelu_pair(dot(x, w_unit[i, 0], 1, 0))
                active = value.astype(jnp.bfloat16)
                delta = dot(active, w_unit[i, 1], 1, 0)
                cotangent = (loss_scale * (x.astype(jnp.float32) + delta)).astype(jnp.bfloat16)
                grad_act = dot(cotangent, w_unit[i, 1], 1, 1)
                grad_pre = (grad_act * slope).astype(jnp.bfloat16)
                sum_up(first_sum, (across, slice(None)), dot(x, grad_pre, 0, 0))
                sum_up(second_sum, (slice(None), across), dot(active, cotangent, 0, 0))
            return carry

        lax.fori_loop(0, steps, go, 0, unroll=min(steps, 4))

    for i in range(2):
        across = slice(i * TILE, (i + 1) * TILE)
        out_ref[i, 0] = first_sum[across, :].astype(out_ref.dtype)
        out_ref[i, 1] = second_sum[:, across].astype(out_ref.dtype)


def unit_grads(which, blocks, near, far, order, flags, per_half, owners, loss_scale, dtype):
    sources, _, _, rows, _ = blocks.shape
    smem = pl.BlockSpec(memory_space=pltpu.SMEM)
    vmem = pl.BlockSpec(memory_space=pltpu.VMEM)
    return pl.pallas_call(
        functools.partial(grads_kernel, which, per_half, owners, loss_scale),
        out_shape=jax.ShapeDtypeStruct((2, 2, TILE, TILE), dtype),
        in_specs=[smem, smem, vmem, vmem, vmem],
        out_specs=vmem,
        scratch_shapes=[
            pltpu.VMEM((2, 2, TILE, TILE), jnp.bfloat16),
            pltpu.VMEM((2 * TILE, TILE), jnp.float32),
            pltpu.VMEM((TILE, 2 * TILE), jnp.float32),
        ],
        compiler_params=IN_VMEM,
        cost_estimate=pl.CostEstimate(
            flops=20 * sources * rows * TILE * TILE,
            bytes_accessed=4 * sources * rows * TILE,
            transcendentals=2 * sources * rows * TILE,
        ),
    )(order, flags, blocks, near, far)


def add_kernel(own_ref, arrived_ref, out_ref):
    out_ref[...] = (own_ref[...] + arrived_ref[...].astype(jnp.float32)).astype(out_ref.dtype)


def add(own, arrived):
    vmem = pl.BlockSpec(memory_space=pltpu.VMEM)
    return pl.pallas_call(
        add_kernel,
        out_shape=jax.ShapeDtypeStruct(own.shape, jnp.bfloat16),
        in_specs=[vmem, vmem],
        out_specs=vmem,
        compiler_params=IN_VMEM,
        cost_estimate=pl.CostEstimate(flops=own.size, bytes_accessed=900_000, transcendentals=0),
    )(own, arrived)


def hand_round(mine):
    replicas = lax.axis_size("dp")
    near = jnp.concatenate(
        [mine]
        + [
            lax.ppermute(mine, "dp", [(i, (i + by) % replicas) for i in range(replicas)])
            for by in range(1, replicas)
        ],
        axis=0,
    )
    return jnp.concatenate([near, swapped(near[1::2], CORES)], axis=0)


def place_kernel(
    per_half, order_ref, counts_ref, same_ref, other_ref, out_ref, zeros, source_ref, sems
):
    owner, replicas = lax.axis_index("fsdp"), same_ref.shape[0] // 3
    per_owner = out_ref.shape[0]
    zeros[...] = jnp.zeros_like(zeros)
    for slot in range(per_owner):
        source_ref[slot] = 0
    for i in range(4 * per_half):
        at = order_ref[0, i] - owner * per_owner
        mine = (at >= 0) & (at < per_owner)
        half, spot = i // 2 // per_half, i // 2 % per_half
        by = (lax.axis_index("dp") - spot // CORES + replicas) % replicas
        held = jnp.where(owner // CORES == half, 2 * by + i % 2, 2 * replicas + by)
        other = jnp.where(owner % CORES == spot % CORES, 0, 1)
        source_ref[jnp.where(mine, at, per_owner)] = 2 * held + other
    for slot in range(per_owner):
        living, source = counts_ref[0, 0, owner] > slot, source_ref[slot]
        for kind, grads_ref in enumerate((same_ref, other_ref)):

            @pl.when(living & (source % 2 == kind))
            def _():
                pltpu.make_async_copy(
                    grads_ref.at[source // 2], out_ref.at[slot], sems.at[slot]
                ).start()

        @pl.when(jnp.logical_not(living))
        def _():
            pltpu.make_async_copy(zeros, out_ref.at[slot], sems.at[slot]).start()

    for slot in range(per_owner):
        pltpu.make_async_copy(zeros, out_ref.at[slot], sems.at[slot]).wait()


def place(same, other, order, counts, per_half, per_owner):
    smem = pl.BlockSpec(memory_space=pltpu.SMEM)
    hbm = pl.BlockSpec(memory_space=pl.ANY)
    return pl.pallas_call(
        functools.partial(place_kernel, per_half),
        out_shape=jax.ShapeDtypeStruct((per_owner,) + same.shape[1:], same.dtype),
        in_specs=[smem, smem, hbm, hbm],
        out_specs=hbm,
        scratch_shapes=[
            pltpu.VMEM(same.shape[1:], same.dtype),
            pltpu.SMEM((per_owner + 1,), jnp.int32),
            pltpu.SemaphoreType.DMA((per_owner,)),
        ],
        compiler_params=IN_VMEM,
        cost_estimate=pl.CostEstimate(flops=0, bytes_accessed=1_000_000, transcendentals=0),
    )(order, counts, same, other)


def body(x_down, x_up, w_tiles, tile_rows, tile_cols, counts):
    rows_here = x_down.shape[2]
    slots, owners = tile_cols.shape[2], counts.shape[2]
    per_half = (live_total(slots, owners) // 2 + 1) // 2
    places = lax.axis_size("dp") * lax.axis_size("fsdp")
    sections = lax.axis_size("section")
    across = [(i, (i + sections // 2) % sections) for i in range(sections)]
    loss_scale = float(2 * rows_here * places) ** (-0.5)

    packed, order, flags = pack(x_down, x_up, tile_rows, tile_cols, counts, per_half, places)
    blocks = lax.all_to_all(packed, PLANE, split_axis=0, concat_axis=0, tiled=True)
    near = jnp.concatenate([w_tiles[0], swapped(w_tiles[0], 1)], axis=1)
    far = swapped(far_weights(near, order, per_half), CORES)
    grads = functools.partial(
        unit_grads, blocks=blocks, near=near, far=far, order=order, flags=flags,
        per_half=per_half, owners=owners, loss_scale=loss_scale,
    )
    arrived = lax.ppermute(grads(1, dtype=jnp.bfloat16), "section", across)
    mine = add(grads(0, dtype=jnp.float32), arrived)
    same = hand_round(mine)
    other = swapped(same, 1)
    return place(same, other, order, counts, per_half, slots // owners)[None]


def solution(mesh):
    in_specs = (
        P("section", "dp", "fsdp", None),
        P("section", "dp", "fsdp", None),
        P("section", None, "fsdp", None, None, None),
        P("section", None, None),
        P("section", None, None),
        P("section", None, None),
    )
    out_specs = P("section", "fsdp", None, None, None)
    return jax.shard_map(body, mesh=mesh, in_specs=in_specs, out_specs=out_specs, check_vma=False)
```

```python
import functools
import itertools
import math

import jax
import jax.numpy as jnp
from jax import lax
from jax.experimental import pallas as pl
from jax.experimental.pallas import tpu as pltpu
from jax.sharding import PartitionSpec as P

TILE = 128
PLANE = ("dp", "fsdp")
SOURCES_AT_ONCE = 8
COLUMNS = 192
CORES = 2
COPIES = 1
IN_VMEM = pltpu.CompilerParams(vmem_limit_bytes=16 * 1024 * 1024)

tanh_scale = math.sqrt(2.0 / math.pi)
cubic_coef = 0.044715


def gelu_pair(hidden):
    square = hidden * hidden
    tangent = jnp.tanh(tanh_scale * (hidden + cubic_coef * hidden * square))
    half = 0.5 * (1.0 + tangent)
    value = hidden * half
    slope = half + value * (1.0 - half) * (
        2.0 * tanh_scale + 6.0 * tanh_scale * cubic_coef * square
    )
    return (value, slope)


def live_total(slots, owners):
    cap = slots // owners
    return sum(cap - i * cap // owners for i in range(owners))


def unit_place(unit, per_half, owners):
    half, at = unit // per_half, unit % per_half
    return at // CORES * owners + half * CORES + at % CORES


def unit_here(per_half, owners):
    owner = lax.axis_index("fsdp")
    at = lax.axis_index("dp") * CORES + owner % CORES
    return owner // CORES * per_half + jnp.minimum(at, per_half - 1)


def order_units(
    cols_ref, counts_ref, which, slots, per_half, order_ref, flags_ref, first_ref, last_ref
):
    per_owner, middle, unused = slots // counts_ref.shape[2], slots // 2, 4 * per_half
    for i in range(order_ref.shape[1]):
        order_ref[which, i] = -1
        flags_ref[which, i] = 0
    cols = []
    for s in range(slots):
        living = counts_ref[0, which, s // per_owner] > s % per_owner
        cols.append(jnp.where(living, cols_ref[0, which, s], COLUMNS))
    yield
    for s in range(slots):
        last_ref[cols[s]] = s
        first_ref[cols[slots - 1 - s]] = slots - 1 - s
    yield
    filled = [jnp.int32(0), jnp.int32(0)]

    def put(unit, slot_a, slot_b, coupled, really):
        at = jnp.where(really, 2 * unit, unused)
        order_ref[which, at] = slot_a
        order_ref[which, at + 1] = slot_b
        flags_ref[which, at] = coupled

    count = lambda condition: jnp.where(condition, 1, 0)
    alone, mixed = [], []
    for s in range(slots):
        living = cols[s] < COLUMNS
        first, last = first_ref[cols[s]], last_ref[cols[s]]
        leads = living & (first == s) & (last > s)
        alone.append(living & (first == last))
        half = s // middle
        pure = leads & (last < (half + 1) * middle)
        put(half * per_half + filled[half], s, last, 1, pure)
        filled[half] = filled[half] + count(pure)
        if half == 0:
            mixed.append((s, last, 1, leads & (last >= middle)))
        yield
    waiting, odd = [jnp.int32(0), jnp.int32(0)], [jnp.int32(0), jnp.int32(0)]
    for s in range(slots):
        half = s // middle
        second = alone[s] & (odd[half] == 1)
        put(half * per_half + filled[half], waiting[half], s, 0, second)
        filled[half] = filled[half] + count(second)
        odd[half] = jnp.where(alone[s], 1 - odd[half], odd[half])
        waiting[half] = jnp.where(alone[s], s, waiting[half])
        yield
    mixed.append((waiting[0], waiting[1], 0, odd[0] == 1))
    for low, high, coupled, really in mixed:
        room = filled[0] < per_half
        unit = jnp.where(room, filled[0], per_half + filled[1])
        put(unit, jnp.where(room, low, high), jnp.where(room, high, low), coupled, really)
        filled[0] = filled[0] + count(really & room)
        filled[1] = filled[1] + count(really & jnp.logical_not(room))
        yield


def pack_kernel(
    per_half, rows_ref, cols_ref, counts_ref, down_ref, up_ref,
    out_ref, order_ref, flags_ref, whole, first_a, last_a, first_b, last_b, sems,
):
    slots, owners = cols_ref.shape[2], counts_ref.shape[2]
    places, units, rows = out_ref.shape[0], 2 * per_half, whole.shape[1]
    pieces = sems.shape[1]
    copies = []
    for which, x_ref in ((0, down_ref), (1, up_ref)):
        for piece in range(pieces):
            part = pl.ds(piece * (rows // pieces), rows // pieces)
            copy = pltpu.make_async_copy(
                x_ref.at[0, 0, part], whole.at[which, part], sems.at[which, piece]
            )
            copy.start()
            copies.append(copy)
    steps = [
        order_units(cols_ref, counts_ref, which, slots, per_half, order_ref, flags_ref, *tables)
        for which, tables in enumerate(((first_a, last_a), (first_b, last_b)))
    ]
    for _ in itertools.zip_longest(*steps):
        pass
    used = [unit_place(unit, per_half, owners) for unit in range(units)]
    for place in range(places):
        if place not in used:
            out_ref[place] = jnp.zeros(out_ref.shape[1:], out_ref.dtype)
    for which in range(2):
        for copy in copies[which * pieces : (which + 1) * pieces]:
            copy.wait()
        for i in range(2 * units):
            row = rows_ref[0, which, jnp.maximum(order_ref[which, i], 0)]
            at = pl.multiple_of(row * TILE, TILE)
            out_ref[used[i // 2], which, i % 2] = whole[which, :, pl.ds(at, TILE)]


def pack(x_down, x_up, tile_rows, tile_cols, counts, per_half, places):
    rows, units = x_down.shape[2], 2 * per_half
    smem = pl.BlockSpec(memory_space=pltpu.SMEM)
    vmem = pl.BlockSpec(memory_space=pltpu.VMEM)
    hbm = pl.BlockSpec(memory_space=pl.ANY)
    return pl.pallas_call(
        functools.partial(pack_kernel, per_half),
        out_shape=[
            jax.ShapeDtypeStruct((places, 2, 2, rows, TILE), x_down.dtype),
            jax.ShapeDtypeStruct((2, 2 * units + 2), jnp.int32),
            jax.ShapeDtypeStruct((2, 2 * units + 2), jnp.int32),
        ],
        in_specs=[smem, smem, smem, hbm, hbm],
        out_specs=[vmem, smem, smem],
        scratch_shapes=[
            pltpu.VMEM((2,) + x_down.shape[2:], x_down.dtype),
            *[pltpu.SMEM((COLUMNS + 1,), jnp.int32)] * 4,
            pltpu.SemaphoreType.DMA((2, COPIES)),
        ],
        cost_estimate=pl.CostEstimate(
            flops=0, bytes_accessed=4 * x_down.size + 16 * units * rows * TILE, transcendentals=0
        ),
    )(tile_rows, tile_cols, counts, x_down, x_up)


def swapped(array, apart):
    size = lax.axis_size("fsdp")
    return lax.ppermute(array, "fsdp", [(i, i ^ apart) for i in range(size)])


def near_at(slot, per_owner):
    owner = slot // per_owner
    other = jnp.where(owner % CORES == lax.axis_index("fsdp") % CORES, 0, per_owner)
    return other + slot - owner * per_owner


def far_kernel(per_half, order_ref, near_ref, out_ref):
    per_owner, owners = near_ref.shape[1] // CORES, 2 * CORES
    unit = unit_here(per_half, owners)
    asker = jnp.where(unit < per_half, unit + per_half, unit - per_half)
    for which in range(2):
        slot = jnp.maximum(order_ref[which, 2 * asker + 1], 0)
        out_ref[which] = near_ref[which, near_at(slot, per_owner)]


def far_weights(near, order, per_half):
    vmem = pl.BlockSpec(memory_space=pltpu.VMEM)
    return pl.pallas_call(
        functools.partial(far_kernel, per_half),
        out_shape=jax.ShapeDtypeStruct(near.shape[:1] + near.shape[2:], near.dtype),
        in_specs=[pl.BlockSpec(memory_space=pltpu.SMEM), vmem],
        out_specs=vmem,
        compiler_params=IN_VMEM,
        cost_estimate=pl.CostEstimate(flops=0, bytes_accessed=300_000, transcendentals=0),
    )(order, near)


def dot(a, b, over_a, over_b):
    return lax.dot_general(
        a, b, (((over_a,), (over_b,)), ((), ())), preferred_element_type=jnp.float32
    )


def grads_kernel(
    which, per_half, owners, loss_scale, order_ref, flags_ref, x_ref, near_ref, far_ref, out_ref,
    w_unit, first_sum, second_sum,
):
    sources, _, _, rows, _ = x_ref.shape
    per_owner = near_ref.shape[1] // CORES
    unit = unit_here(per_half, owners)
    half = lax.axis_index("fsdp") // CORES
    for i in range(2):
        slot = jnp.maximum(order_ref[which, 2 * unit + i], 0)
        near = slot // per_owner // CORES == half

        @pl.when(near)
        def _():
            w_unit[i] = near_ref[which, near_at(slot, per_owner)]

        @pl.when(jnp.logical_not(near))
        def _():
            w_unit[i] = far_ref[which]

    together = min(SOURCES_AT_ONCE, sources)
    steps = sources // together
    if steps > 1:
        first_sum[...] = jnp.zeros_like(first_sum)
        second_sum[...] = jnp.zeros_like(second_sum)

    def sum_up(total_ref, where, term):
        total_ref[where] = total_ref[where] + term if steps > 1 else term

    coupled = flags_ref[which, 2 * unit] == 1

    def read(step):
        at = step * together
        return [
            x_ref[pl.ds(at, together), which, i].reshape(together * rows, TILE) for i in range(2)
        ]

    @pl.when(coupled)
    def _():
        def go(step, carry):
            xs = jnp.concatenate(read(step), axis=1)
            firsts = jnp.concatenate([w_unit[0, 0], w_unit[1, 0]], axis=0)
            seconds = jnp.concatenate([w_unit[0, 1], w_unit[1, 1]], axis=1)
            value, slope = gelu_pair(dot(xs, firsts, 1, 0))
            active = value.astype(jnp.bfloat16)
            delta = dot(active, seconds, 1, 0)
            cotangent = (loss_scale * (xs.astype(jnp.float32) + delta)).astype(jnp.bfloat16)
            grad_act = dot(cotangent, seconds, 1, 1)
            grad_pre = (grad_act * slope).astype(jnp.bfloat16)
            sum_up(first_sum, ..., dot(xs, grad_pre, 0, 0))
            sum_up(second_sum, ..., dot(active, cotangent, 0, 0))
            return carry

        lax.fori_loop(0, steps, go, 0, unroll=min(steps, 4))

    @pl.when(jnp.logical_not(coupled))
    def _():
        def go(step, carry):
            for i, x in enumerate(read(step)):
                across = slice(i * TILE, (i + 1) * TILE)
                value, slope = gelu_pair(dot(x, w_unit[i, 0], 1, 0))
                active = value.astype(jnp.bfloat16)
                delta = dot(active, w_unit[i, 1], 1, 0)
                cotangent = (loss_scale * (x.astype(jnp.float32) + delta)).astype(jnp.bfloat16)
                grad_act = dot(cotangent, w_unit[i, 1], 1, 1)
                grad_pre = (grad_act * slope).astype(jnp.bfloat16)
                sum_up(first_sum, (across, slice(None)), dot(x, grad_pre, 0, 0))
                sum_up(second_sum, (slice(None), across), dot(active, cotangent, 0, 0))
            return carry

        lax.fori_loop(0, steps, go, 0, unroll=min(steps, 4))

    for i in range(2):
        across = slice(i * TILE, (i + 1) * TILE)
        out_ref[i, 0] = first_sum[across, :].astype(out_ref.dtype)
        out_ref[i, 1] = second_sum[:, across].astype(out_ref.dtype)


def unit_grads(which, blocks, near, far, order, flags, per_half, owners, loss_scale, dtype):
    sources, _, _, rows, _ = blocks.shape
    smem = pl.BlockSpec(memory_space=pltpu.SMEM)
    vmem = pl.BlockSpec(memory_space=pltpu.VMEM)
    return pl.pallas_call(
        functools.partial(grads_kernel, which, per_half, owners, loss_scale),
        out_shape=jax.ShapeDtypeStruct((2, 2, TILE, TILE), dtype),
        in_specs=[smem, smem, vmem, vmem, vmem],
        out_specs=vmem,
        scratch_shapes=[
            pltpu.VMEM((2, 2, TILE, TILE), jnp.bfloat16),
            pltpu.VMEM((2 * TILE, TILE), jnp.float32),
            pltpu.VMEM((TILE, 2 * TILE), jnp.float32),
        ],
        compiler_params=IN_VMEM,
        cost_estimate=pl.CostEstimate(
            flops=20 * sources * rows * TILE * TILE,
            bytes_accessed=4 * sources * rows * TILE,
            transcendentals=2 * sources * rows * TILE,
        ),
    )(order, flags, blocks, near, far)


def add_kernel(own_ref, arrived_ref, out_ref):
    out_ref[...] = (own_ref[...] + arrived_ref[...].astype(jnp.float32)).astype(out_ref.dtype)


def add(own, arrived):
    vmem = pl.BlockSpec(memory_space=pltpu.VMEM)
    return pl.pallas_call(
        add_kernel,
        out_shape=jax.ShapeDtypeStruct(own.shape, jnp.bfloat16),
        in_specs=[vmem, vmem],
        out_specs=vmem,
        compiler_params=IN_VMEM,
        cost_estimate=pl.CostEstimate(flops=own.size, bytes_accessed=900_000, transcendentals=0),
    )(own, arrived)


def hand_round(mine):
    replicas = lax.axis_size("dp")
    near = jnp.concatenate(
        [mine]
        + [
            lax.ppermute(mine, "dp", [(i, (i + by) % replicas) for i in range(replicas)])
            for by in range(1, replicas)
        ],
        axis=0,
    )
    return jnp.concatenate([near, swapped(near[1::2], CORES)], axis=0)


def place_kernel(
    per_half, order_ref, counts_ref, same_ref, other_ref, out_ref, zeros, source_ref, sems
):
    owner, replicas = lax.axis_index("fsdp"), same_ref.shape[0] // 3
    per_owner = out_ref.shape[0]
    zeros[...] = jnp.zeros_like(zeros)
    for slot in range(per_owner):
        source_ref[slot] = 0
    for i in range(4 * per_half):
        at = order_ref[0, i] - owner * per_owner
        mine = (at >= 0) & (at < per_owner)
        half, spot = i // 2 // per_half, i // 2 % per_half
        by = (lax.axis_index("dp") - spot // CORES + replicas) % replicas
        held = jnp.where(owner // CORES == half, 2 * by + i % 2, 2 * replicas + by)
        other = jnp.where(owner % CORES == spot % CORES, 0, 1)
        source_ref[jnp.where(mine, at, per_owner)] = 2 * held + other
    for slot in range(per_owner):
        living, source = counts_ref[0, 0, owner] > slot, source_ref[slot]
        for kind, grads_ref in enumerate((same_ref, other_ref)):

            @pl.when(living & (source % 2 == kind))
            def _():
                pltpu.make_async_copy(
                    grads_ref.at[source // 2], out_ref.at[slot], sems.at[slot]
                ).start()

        @pl.when(jnp.logical_not(living))
        def _():
            pltpu.make_async_copy(zeros, out_ref.at[slot], sems.at[slot]).start()

    for slot in range(per_owner):
        pltpu.make_async_copy(zeros, out_ref.at[slot], sems.at[slot]).wait()


def place(same, other, order, counts, per_half, per_owner):
    smem = pl.BlockSpec(memory_space=pltpu.SMEM)
    hbm = pl.BlockSpec(memory_space=pl.ANY)
    return pl.pallas_call(
        functools.partial(place_kernel, per_half),
        out_shape=jax.ShapeDtypeStruct((per_owner,) + same.shape[1:], same.dtype),
        in_specs=[smem, smem, hbm, hbm],
        out_specs=hbm,
        scratch_shapes=[
            pltpu.VMEM(same.shape[1:], same.dtype),
            pltpu.SMEM((per_owner + 1,), jnp.int32),
            pltpu.SemaphoreType.DMA((per_owner,)),
        ],
        compiler_params=IN_VMEM,
        cost_estimate=pl.CostEstimate(flops=0, bytes_accessed=1_000_000, transcendentals=0),
    )(order, counts, same, other)


def body(x_down, x_up, w_tiles, tile_rows, tile_cols, counts):
    rows_here = x_down.shape[2]
    slots, owners = tile_cols.shape[2], counts.shape[2]
    per_half = (live_total(slots, owners) // 2 + 1) // 2
    places = lax.axis_size("dp") * lax.axis_size("fsdp")
    sections = lax.axis_size("section")
    across = [(i, (i + sections // 2) % sections) for i in range(sections)]
    loss_scale = float(2 * rows_here * places) ** (-0.5)

    packed, order, flags = pack(x_down, x_up, tile_rows, tile_cols, counts, per_half, places)
    blocks = lax.all_to_all(packed, PLANE, split_axis=0, concat_axis=0, tiled=True)
    near = jnp.concatenate([w_tiles[0], swapped(w_tiles[0], 1)], axis=1)
    far = swapped(far_weights(near, order, per_half), CORES)
    grads = functools.partial(
        unit_grads, blocks=blocks, near=near, far=far, order=order, flags=flags,
        per_half=per_half, owners=owners, loss_scale=loss_scale,
    )
    arrived = lax.ppermute(grads(1, dtype=jnp.bfloat16), "section", across)
    mine = add(grads(0, dtype=jnp.float32), arrived)
    same = hand_round(mine)
    other = swapped(same, 1)
    return place(same, other, order, counts, per_half, slots // owners)[None]


def solution(mesh):
    in_specs = (
        P("section", "dp", "fsdp", None),
        P("section", "dp", "fsdp", None),
        P("section", None, "fsdp", None, None, None),
        P("section", None, None),
        P("section", None, None),
        P("section", None, None),
    )
    out_specs = P("section", "fsdp", None, None, None)
    return jax.shard_map(body, mesh=mesh, in_specs=in_specs, out_specs=out_specs, check_vma=False)
```
